32 devices in a mesh: dp: 8 (over z, x), mp: 4 (over y, core).
Axes of the slice: x: 2, y: 2, z: 4, core: 2. Of those that a mesh axis runs over, the one named last changes fastest.
Arguments:
- hidden_in: bfloat16 [16384, 768], P(('dp', 'mp')), may hold values from -6 to 6
- image_feats: bfloat16 [256, 257, 1408], P('dp'), may hold values from -6 to 6
- caption_lengths: int32 [256], P('dp'), may hold values from 5 to 32, as said below
- out_grad: bfloat16 [16384, 768], P(('dp', 'mp')), may hold values from -6 to 6
- proj_in: float32 [4, 768, 768], P(None, 'dp', 'mp')
- proj_in_moments: float32 [2, 4, 768, 768], P(None, None, 'dp', 'mp')
- proj_in_average: float32 [4, 768, 768], P(None, 'dp', 'mp')
- proj_out: float32 [2, 768, 768], P(None, ('mp', 'dp'))
- proj_out_moments: float32 [2, 2, 768, 768], P(None, None, ('mp', 'dp'))
- proj_out_average: float32 [2, 768, 768], P(None, ('mp', 'dp'))
- image_kv: float32 [2, 1408, 768], P(None, 'dp', 'mp')
- image_kv_moments: float32 [2, 2, 1408, 768], P(None, None, 'dp', 'mp')
- image_kv_average: float32 [2, 1408, 768], P(None, 'dp', 'mp')
- feed_up: float32 [768, 3072], P('dp', 'mp')
- feed_up_moments: float32 [2, 768, 3072], P(None, 'dp', 'mp')
- feed_up_average: float32 [768, 3072], P('dp', 'mp')
- feed_down: float32 [3072, 768], P(('mp', 'dp'))
- feed_down_moments: float32 [2, 3072, 768], P(None, ('mp', 'dp'))
- feed_down_average: float32 [3072, 768], P(('mp', 'dp'))
- norm_params: float32 [6, 768], P(None, ('mp', 'dp'))
- norm_params_moments: float32 [2, 6, 768], P(None, None, ('mp', 'dp'))
- norm_params_average: float32 [6, 768], P(None, ('mp', 'dp'))
Outputs:
- block_out: bfloat16 [16384, 768], P(('dp', 'mp'))
- input_grad: bfloat16 [16384, 768], P(('dp', 'mp'))
- new_proj_in: float32 [4, 768, 768], P(None, 'dp', 'mp')
- new_proj_in_moments: float32 [2, 4, 768, 768], P(None, None, 'dp', 'mp')
- new_proj_in_average: float32 [4, 768, 768], P(None, 'dp', 'mp')
- new_proj_out: float32 [2, 768, 768], P(None, ('mp', 'dp'))
- new_proj_out_moments: float32 [2, 2, 768, 768], P(None, None, ('mp', 'dp'))
- new_proj_out_average: float32 [2, 768, 768], P(None, ('mp', 'dp'))
- new_image_kv: float32 [2, 1408, 768], P(None, 'dp', 'mp')
- new_image_kv_moments: float32 [2, 2, 1408, 768], P(None, None, 'dp', 'mp')
- new_image_kv_average: float32 [2, 1408, 768], P(None, 'dp', 'mp')
- new_feed_up: float32 [768, 3072], P('dp', 'mp')
- new_feed_up_moments: float32 [2, 768, 3072], P(None, 'dp', 'mp')
- new_feed_up_average: float32 [768, 3072], P('dp', 'mp')
- new_feed_down: float32 [3072, 768], P(('mp', 'dp'))
- new_feed_down_moments: float32 [2, 3072, 768], P(None, ('mp', 'dp'))
- new_feed_down_average: float32 [3072, 768], P(('mp', 'dp'))
- new_norm_params: float32 [6, 768], P(None, ('mp', 'dp'))
- new_norm_params_moments: float32 [2, 6, 768], P(None, None, ('mp', 'dp'))
- new_norm_params_average: float32 [6, 768], P(None, ('mp', 'dp'))
- trust_ratios: float32 [16], replicated
- norm_values: float32 [2, 16], replicated
The draws below stay inside these ranges and needn't reach their ends.
Inputs may be any that keep to these rules, and one draw needn't show every extreme that they name: `caption_lengths`: in every draw some caption has 32 tokens and some has 5.
All inputs are finite; a program needn't handle non-finite values.
Results may differ from the reference program's by a relative error of at most 0.025.
The reference program's roundings to bfloat16 on the way count: a program that leaves them out, or rounds other values in their place, can miss the bound.
Values may be sent and summed in bfloat16 or wider, within the bound.
No kernel may reach another device: no remote copies, remote signals or barrier semaphores. Data moves between devices by JAX's collectives and lax.ppermute only.
A program may use at most 192 MiB of HBM per device.

```python
import math
import jax
import jax.numpy as jnp
from jax import lax

D = 768
HEADS = 12
HEAD = 64
FF = 3072
ENC = 1408
PATCHES = 257
QUERIES = 32
TEXT = 32
MIN_TEXT = 5
STEP = 10
ITEMS_DEV = 32
ITEMS = 256
TOKENS = 16384
HEADS_DEV = 3
N_DP = 8


def axis_ramp(position, ways):
    if ways < 2:
        return jnp.ones(position.shape, jnp.float32)
    return 0.5 + position.astype(jnp.float32) / (ways - 1)


def ramp_scale(length, outer_ways, inner_ways):
    position = jnp.arange(length)
    stride = length // (outer_ways * inner_ways)
    inner_pos = position // stride % inner_ways
    outer_pos = position // (stride * inner_ways)
    return jnp.sqrt(axis_ramp(inner_pos, inner_ways) * axis_ramp(outer_pos, outer_ways))


def axis_ways():
    return (ITEMS // ITEMS_DEV, HEADS // HEADS_DEV)


def entries(key, array_shape):
    normal_key = jax.random.fold_in(key, 0)
    gauss_values = jax.random.normal(normal_key, array_shape, jnp.float32)
    return gauss_values


def proj_in_layout():
    data_ways, model_ways = axis_ways()
    ramp_part = ramp_scale(D, 1, data_ways)[None, :, None] * ramp_scale(D, model_ways, 1)[None, None, :]
    token_root = math.sqrt(TOKENS)
    query_root = math.sqrt(ITEMS * QUERIES)
    grad_size = jnp.array([0.5 * token_root, 0.5 * token_root, 0.5 * token_root, 0.7 * query_root], jnp.float32)[:, None, None]
    return ((4, D, D), ramp_part * D ** (-0.5), ramp_part, grad_size)


def proj_out_layout():
    data_ways, model_ways = axis_ways()
    ramp_part = ramp_scale(D, model_ways, data_ways)[None, :, None]
    fan_scale = jnp.array([(D // 16) ** (-0.5), (D // 96) ** (-0.5)], jnp.float32)[:, None, None]
    token_root = math.sqrt(TOKENS)
    query_root = math.sqrt(ITEMS * QUERIES)
    grad_size = jnp.array([0.17 * token_root, 0.07 * query_root], jnp.float32)[:, None, None]
    return ((2, D, D), ramp_part * fan_scale, ramp_part, grad_size)


def image_kv_layout():
    data_ways, model_ways = axis_ways()
    ramp_part = ramp_scale(ENC, 1, data_ways)[None, :, None] * ramp_scale(D, model_ways, 1)[None, None, :]
    grad_size = 0.4 * math.sqrt(ITEMS * PATCHES)
    return ((2, ENC, D), ramp_part * ENC ** (-0.5), ramp_part, grad_size)


def feed_up_layout():
    data_ways, model_ways = axis_ways()
    ramp_part = ramp_scale(D, 1, data_ways)[:, None] * ramp_scale(FF, model_ways, 1)[None, :]
    grad_size = 0.2 * math.sqrt(TOKENS)
    return ((D, FF), ramp_part * D ** (-0.5), ramp_part, grad_size)


def feed_down_layout():
    data_ways, model_ways = axis_ways()
    ramp_part = ramp_scale(FF, model_ways, data_ways)[:, None]
    grad_size = 0.45 * math.sqrt(TOKENS)
    return ((FF, D), ramp_part * FF ** (-0.5), ramp_part, grad_size)


def norm_layout():
    data_ways, model_ways = axis_ways()
    ramp_part = ramp_scale(D, model_ways, data_ways)[None, :]
    token_root = math.sqrt(TOKENS)
    query_root = math.sqrt(ITEMS * QUERIES)
    grad_size = jnp.array([0.5 * token_root, token_root, 0.5 * query_root, query_root, 0.7 * token_root, token_root], jnp.float32)[:, None]
    return ((6, D), ramp_part, ramp_part, grad_size)


def weight_draw(key, layout_parts):
    array_shape, weight_scale, ramp_part, grad_size = layout_parts
    return entries(key, array_shape) * weight_scale


def norm_draw(key):
    array_shape, weight_scale, ramp_part, grad_size = norm_layout()
    centre_value = jnp.array([1.0, 0.0, 1.0, 0.0, 1.0, 0.0], jnp.float32)[:, None]
    spread = jnp.array([0.15, 0.3, 0.15, 0.3, 0.15, 0.3], jnp.float32)[:, None]
    return (centre_value + spread * entries(key, array_shape)) * ramp_part


def moment_draw(key, layout_parts):
    array_shape, weight_scale, ramp_part, grad_size = layout_parts
    first_key, second_key = jax.random.split(key)
    moment_one = 0.1 / 0.9 * grad_size * ramp_part * entries(first_key, array_shape)
    factor = jnp.exp(jax.random.uniform(second_key, array_shape, jnp.float32, 0.0, math.log(4.0)))
    moment_two = 0.001 / 0.999 * grad_size * grad_size * factor
    return jnp.stack([moment_one, moment_two])


def draw_caption_lengths(key, part):
    key = jax.random.fold_in(key, 5)
    base_key, long_key, short_key = jax.random.split(key, 3)
    lengths = jax.random.randint(base_key, (ITEMS,), MIN_TEXT, TEXT + 1)
    longest = jax.random.randint(long_key, (), 0, ITEMS)
    shortest = (longest + jax.random.randint(short_key, (), 1, ITEMS)) % ITEMS
    return lengths.at[longest].set(TEXT).at[shortest].set(MIN_TEXT)


def draw_proj_in(key, part):
    key = jax.random.fold_in(key, 11)
    return weight_draw(key, proj_in_layout())


def draw_proj_in_moments(key, part):
    key = jax.random.fold_in(key, 21)
    return moment_draw(key, proj_in_layout())


def draw_proj_in_average(key, part):
    key = jax.random.fold_in(key, 31)
    return weight_draw(key, proj_in_layout())


def draw_proj_out(key, part):
    key = jax.random.fold_in(key, 12)
    return weight_draw(key, proj_out_layout())


def draw_proj_out_moments(key, part):
    key = jax.random.fold_in(key, 22)
    return moment_draw(key, proj_out_layout())


def draw_proj_out_average(key, part):
    key = jax.random.fold_in(key, 32)
    return weight_draw(key, proj_out_layout())


def draw_image_kv(key, part):
    key = jax.random.fold_in(key, 13)
    return weight_draw(key, image_kv_layout())


def draw_image_kv_moments(key, part):
    key = jax.random.fold_in(key, 23)
    return moment_draw(key, image_kv_layout())


def draw_image_kv_average(key, part):
    key = jax.random.fold_in(key, 33)
    return weight_draw(key, image_kv_layout())


def draw_feed_up(key, part):
    key = jax.random.fold_in(key, 14)
    return weight_draw(key, feed_up_layout())


def draw_feed_up_moments(key, part):
    key = jax.random.fold_in(key, 24)
    return moment_draw(key, feed_up_layout())


def draw_feed_up_average(key, part):
    key = jax.random.fold_in(key, 34)
    return weight_draw(key, feed_up_layout())


def draw_feed_down(key, part):
    key = jax.random.fold_in(key, 15)
    return weight_draw(key, feed_down_layout())


def draw_feed_down_moments(key, part):
    key = jax.random.fold_in(key, 25)
    return moment_draw(key, feed_down_layout())


def draw_feed_down_average(key, part):
    key = jax.random.fold_in(key, 35)
    return weight_draw(key, feed_down_layout())


def draw_norm_params(key, part):
    key = jax.random.fold_in(key, 16)
    return norm_draw(key)


def draw_norm_params_moments(key, part):
    key = jax.random.fold_in(key, 26)
    return moment_draw(key, norm_layout())


def draw_norm_params_average(key, part):
    key = jax.random.fold_in(key, 36)
    return norm_draw(key)


def level_of(own_key, shape, cuts, smallest, largest):
    def one(dim, blocks):
        heights = jax.random.uniform(jax.random.fold_in(jax.random.fold_in(own_key, 6), dim), (blocks,), jnp.float32, smallest / len(cuts), largest / len(cuts))
        return jnp.repeat(jnp.exp(heights), shape[dim] // blocks).reshape((-1,) + (1,) * (len(shape) - dim - 1))

    level = one(*cuts[0])
    for cut in cuts[1:]:
        level = level * one(*cut)
    return level


def gaussian(stream_key, dims, width, limit, cuts=(), held_as=jnp.bfloat16):
    level = level_of(stream_key, dims, cuts, -0.22, 0.18) if cuts else 1.0
    values = jax.random.normal(stream_key, dims, jnp.float32) * width * level
    return jnp.minimum(jnp.maximum(values, -limit), limit).astype(held_as)


def setup_inputs(seed: int = 0) -> dict:
    keys = jax.random.split(jax.random.key(seed), 23)
    hidden_in = gaussian(keys[0], (TOKENS, D), 1.0, 6.0, ((0, 32),))
    image_feats = gaussian(keys[1], (ITEMS, PATCHES, ENC), 1.0, 6.0, ((0, 8),))
    caption_lengths = draw_caption_lengths(jax.random.fold_in(keys[22], 71), 0)
    out_grad = gaussian(keys[3], (TOKENS, D), 1.0, 6.0, ((0, 32),))
    proj_in = draw_proj_in(jax.random.fold_in(keys[22], 71), 0)
    proj_in_moments = draw_proj_in_moments(jax.random.fold_in(keys[22], 71), 0)
    proj_in_average = draw_proj_in_average(jax.random.fold_in(keys[22], 71), 0)
    proj_out = draw_proj_out(jax.random.fold_in(keys[22], 71), 0)
    proj_out_moments = draw_proj_out_moments(jax.random.fold_in(keys[22], 71), 0)
    proj_out_average = draw_proj_out_average(jax.random.fold_in(keys[22], 71), 0)
    image_kv = draw_image_kv(jax.random.fold_in(keys[22], 71), 0)
    image_kv_moments = draw_image_kv_moments(jax.random.fold_in(keys[22], 71), 0)
    image_kv_average = draw_image_kv_average(jax.random.fold_in(keys[22], 71), 0)
    feed_up = draw_feed_up(jax.random.fold_in(keys[22], 71), 0)
    feed_up_moments = draw_feed_up_moments(jax.random.fold_in(keys[22], 71), 0)
    feed_up_average = draw_feed_up_average(jax.random.fold_in(keys[22], 71), 0)
    feed_down = draw_feed_down(jax.random.fold_in(keys[22], 71), 0)
    feed_down_moments = draw_feed_down_moments(jax.random.fold_in(keys[22], 71), 0)
    feed_down_average = draw_feed_down_average(jax.random.fold_in(keys[22], 71), 0)
    norm_params = draw_norm_params(jax.random.fold_in(keys[22], 71), 0)
    norm_params_moments = draw_norm_params_moments(jax.random.fold_in(keys[22], 71), 0)
    norm_params_average = draw_norm_params_average(jax.random.fold_in(keys[22], 71), 0)
    return {"hidden_in": hidden_in, "image_feats": image_feats, "caption_lengths": caption_lengths, "out_grad": out_grad, "proj_in": proj_in, "proj_in_moments": proj_in_moments, "proj_in_average": proj_in_average, "proj_out": proj_out, "proj_out_moments": proj_out_moments, "proj_out_average": proj_out_average, "image_kv": image_kv, "image_kv_moments": image_kv_moments, "image_kv_average": image_kv_average, "feed_up": feed_up, "feed_up_moments": feed_up_moments, "feed_up_average": feed_up_average, "feed_down": feed_down, "feed_down_moments": feed_down_moments, "feed_down_average": feed_down_average, "norm_params": norm_params, "norm_params_moments": norm_params_moments, "norm_params_average": norm_params_average}


NORM_EPSILON = 1e-06
ADAM_EPSILON = 1e-06
SQUARE_EPSILON = 1e-06
BETA_ONE = 0.9
BETA_TWO = 0.999
LEARN_RATE = 0.5
DECAY_RATE = 0.01
AVERAGE_RATE = 0.6
MASK_VALUE = -1e+30

@jax.custom_vjp
def low(v):
    return lax.optimization_barrier(v.astype(jnp.bfloat16)).astype(jnp.float32)

@jax.custom_vjp
def low_back(v):
    return v

def low_keep(v):
    return (low(v), None)

def low_pass(kept, grad):
    return (grad,)

def back_keep(v):
    return (v, None)

def back_low(kept, grad):
    return (low(grad),)
low.defvjp(low_keep, low_pass)
low_back.defvjp(back_keep, back_low)

def matmul(left_side, right_side):
    return jnp.dot(left_side, right_side, precision=lax.Precision.HIGHEST, preferred_element_type=jnp.float32)

def layer_norm(inputs, gain, shift):
    centred = inputs - lax.optimization_barrier(jnp.mean(inputs, axis=-1, keepdims=True))
    inverse = lax.rsqrt(lax.optimization_barrier(jnp.mean(centred * centred, axis=-1, keepdims=True)) + NORM_EPSILON)
    return centred * inverse * gain + shift

def attend(queries, key_rows, value_rows, key_live):
    scale = queries.shape[-1] ** (-0.5)
    scores = low_back(jnp.einsum('bqhe,bkhe->bhqk', queries, key_rows, precision=lax.Precision.HIGHEST) * scale)
    scores = jnp.where(key_live[:, None, None, :], scores, MASK_VALUE)
    attn_probs = jax.nn.softmax(scores, axis=-1)
    result = jnp.einsum('bhqk,bkhe->bqhe', low(attn_probs), value_rows, precision=lax.Precision.HIGHEST)
    return low(low_back(result))

def qformer_layer(params, row_block, image_block, length_block):
    proj_in, proj_out, image_kv, feed_up, feed_down, norm_params = [low(weight) for weight in params]
    items = length_block.shape[0]
    features = row_block.shape[1]
    head_count = features // HEAD
    seq_len = QUERIES + TEXT
    position = jnp.arange(seq_len)
    key_live = (position[None, :] < QUERIES) | (position[None, :] - QUERIES < length_block[:, None])
    patch_live = jnp.ones((items, PATCHES), dtype=bool)

    def split_heads(values, length):
        return values.reshape(items, length, head_count, HEAD)
    queries = low(low_back(matmul(row_block, proj_in[0])))
    key_rows = low(low_back(matmul(row_block, proj_in[1])))
    value_rows = low(low_back(matmul(row_block, proj_in[2])))
    self_heads = attend(split_heads(queries, seq_len), split_heads(key_rows, seq_len), split_heads(value_rows, seq_len), key_live)
    first_in = row_block + low_back(matmul(self_heads.reshape(items * seq_len, features), proj_out[0]))
    after_one = layer_norm(first_in, norm_params[0], norm_params[1])
    one_items = after_one.reshape(items, seq_len, features)
    one_query = one_items[:, :QUERIES].reshape(items * QUERIES, features)
    cross_queries = low(low_back(matmul(low(one_query), proj_in[3])))
    cross_keys = low(low_back(jnp.einsum('ipe,ec->ipc', image_block, image_kv[0], precision=lax.Precision.HIGHEST)))
    cross_values = low(low_back(jnp.einsum('ipe,ec->ipc', image_block, image_kv[1], precision=lax.Precision.HIGHEST)))
    cross_heads = attend(split_heads(cross_queries, QUERIES), split_heads(cross_keys, PATCHES), split_heads(cross_values, PATCHES), patch_live)
    second_in = one_query + low_back(matmul(cross_heads.reshape(items * QUERIES, features), proj_out[1]))
    after_two = layer_norm(second_in, norm_params[2], norm_params[3])
    two_rows = jnp.concatenate([after_two.reshape(items, QUERIES, features), one_items[:, QUERIES:]], axis=1).reshape(items * seq_len, features)
    pre_act = low_back(matmul(low(two_rows), feed_up))
    active = low(jax.nn.gelu(pre_act, approximate=False))
    third_in = two_rows + low_back(matmul(active, feed_down))
    return layer_norm(third_in, norm_params[4], norm_params[5])

def adam_step(weight, moments, gradient, decay_rate):
    moment_one = BETA_ONE * moments[0] + (1.0 - BETA_ONE) * gradient
    moment_two = BETA_TWO * moments[1] + (1.0 - BETA_TWO) * gradient * gradient
    update = moment_one / (1.0 - BETA_ONE ** STEP) / (jnp.sqrt(moment_two / (1.0 - BETA_TWO ** STEP)) + ADAM_EPSILON) + decay_rate * weight
    return (moment_one, moment_two, update)

def tensor_squares(values, per_slice):
    if per_slice:
        return lax.optimization_barrier(jnp.sum(values * values, axis=tuple(range(1, values.ndim))))
    return jnp.sum(values * values)[None]

def reference(hidden_in, image_feats, caption_lengths, out_grad, proj_in, proj_in_moments, proj_in_average, proj_out, proj_out_moments, proj_out_average, image_kv, image_kv_moments, image_kv_average, feed_up, feed_up_moments, feed_up_average, feed_down, feed_down_moments, feed_down_average, norm_params, norm_params_moments, norm_params_average):
    weights = (proj_in, proj_out, image_kv, feed_up, feed_down, norm_params)
    seq_len = QUERIES + TEXT
    all_rows = hidden_in.astype(jnp.float32).reshape(N_DP, ITEMS_DEV * seq_len, D)
    images = image_feats.astype(jnp.float32).reshape(N_DP, ITEMS_DEV, PATCHES, ENC)
    lengths = caption_lengths.reshape(N_DP, ITEMS_DEV)
    slopes = out_grad.astype(jnp.float32).reshape(N_DP, ITEMS_DEV * seq_len, D)

    def block_step(totals, pieces):
        row_block, image_block, length_block, slope_block = pieces

        def forward(params, inputs):
            return qformer_layer(params, inputs, image_block, length_block)
        result, pullback = jax.vjp(forward, weights, row_block)
        position = jnp.arange(seq_len)
        row_live = (position[None, :] < QUERIES) | (position[None, :] - QUERIES < length_block[:, None])
        weight_grads, row_grads = pullback(slope_block * row_live.reshape(-1, 1).astype(jnp.float32))
        totals = jax.tree.map(lambda left_side, right_side: left_side + right_side, totals, weight_grads)
        return (totals, (result.astype(jnp.bfloat16), row_grads.astype(jnp.bfloat16)))
    zero_grads = jax.tree.map(jnp.zeros_like, weights)
    weight_sums, (result_rows, input_rows) = lax.scan(block_step, zero_grads, (all_rows, images, lengths, slopes))
    block_out = result_rows.reshape(TOKENS, D)
    input_grad = input_rows.reshape(TOKENS, D)
    groups = [(proj_in, proj_in_moments, proj_in_average, weight_sums[0], DECAY_RATE, True), (proj_out, proj_out_moments, proj_out_average, weight_sums[1], DECAY_RATE, True), (image_kv, image_kv_moments, image_kv_average, weight_sums[2], DECAY_RATE, True), (feed_up, feed_up_moments, feed_up_average, weight_sums[3], DECAY_RATE, False), (feed_down, feed_down_moments, feed_down_average, weight_sums[4], DECAY_RATE, False), (norm_params, norm_params_moments, norm_params_average, weight_sums[5], 0.0, True)]
    updates = []
    weight_squares = []
    update_squares = []
    for weight, moments, average, gradient, decay_rate, per_slice in groups:
        moment_one, moment_two, update = adam_step(weight, moments, gradient, decay_rate)
        updates.append((moment_one, moment_two, update))
        weight_squares.append(tensor_squares(weight, per_slice))
        update_squares.append(tensor_squares(update, per_slice))
    squares = jnp.stack([jnp.concatenate(weight_squares), jnp.concatenate(update_squares)])
    trust = jnp.sqrt(squares[0]) * lax.rsqrt(squares[1] + SQUARE_EPSILON)
    outputs = []
    offset = 0
    for group, stepped in zip(groups, updates):
        weight, moments, average, gradient, decay_rate, per_slice = group
        moment_one, moment_two, update = stepped
        slices = weight.shape[0] if per_slice else 1
        trust_part = trust[offset:offset + slices]
        if per_slice:
            trust_part = trust_part.reshape((slices,) + (1,) * (weight.ndim - 1))
        else:
            trust_part = trust_part[0]
        new_weight = weight - LEARN_RATE * trust_part * update
        outputs.append(new_weight)
        outputs.append(jnp.stack([moment_one, moment_two]))
        outputs.append(AVERAGE_RATE * average + (1.0 - AVERAGE_RATE) * new_weight)
        offset += slices
    return (block_out, input_grad, outputs[0], outputs[1], outputs[2], outputs[3], outputs[4], outputs[5], outputs[6], outputs[7], outputs[8], outputs[9], outputs[10], outputs[11], outputs[12], outputs[13], outputs[14], outputs[15], outputs[16], outputs[17], trust, jnp.sqrt(squares))
```

```python
import jax
import jax.numpy as jnp
from jax import lax
from jax.experimental import pallas as pl
from jax.experimental.pallas import tpu as pltpu
from jax.sharding import PartitionSpec as P

HEAD = 64
PATCHES = 257
QUERIES = 32
TEXT = 32
SEQ = QUERIES + TEXT
STEP = 10


NORM_EPSILON = 1e-06
ADAM_EPSILON = 1e-06
SQUARE_EPSILON = 1e-06
BETA_ONE = 0.9
BETA_TWO = 0.999
LEARN_RATE = 0.5
DECAY_RATE = 0.01
AVERAGE_RATE = 0.6
MASK_VALUE = -1e30

AXES = ("dp", "mp")
GROUPS = 8
MODEL = 4
SLOTS = 16
NORM_ROWS = 8
BLOCK = 256
WIDE = 256
VMEM_LIMIT = 60 * 1024 * 1024

BF16 = jnp.bfloat16
F32 = jnp.float32


def dot_nn(left_side, right_side):
    return lax.dot_general(
        left_side, right_side, (((1,), (0,)), ((), ())), preferred_element_type=F32
    )


def dot_nt(left_side, right_side):
    return lax.dot_general(
        left_side, right_side, (((1,), (1,)), ((), ())), preferred_element_type=F32
    )


def dot_tn(left_side, right_side):
    return lax.dot_general(
        left_side, right_side, (((0,), (0,)), ((), ())), preferred_element_type=F32
    )


def normalise(inputs):
    centred = inputs - jnp.mean(inputs, axis=-1, keepdims=True)
    inverse = lax.rsqrt(jnp.mean(centred * centred, axis=-1, keepdims=True) + NORM_EPSILON)
    return centred * inverse, inverse


def norm_back(gradient, normed, inverse, gain):
    scaled = gradient * gain
    centre_term = jnp.mean(scaled, axis=-1, keepdims=True)
    normed_term = jnp.mean(scaled * normed, axis=-1, keepdims=True)
    return inverse * (scaled - centre_term - normed * normed_term)


def slot_x(place, block, y_rel):
    return place[block] * 8 + y_rel * 4 + place[GROUPS + block]


def slot_y(place, block, y_rel):
    return y_rel * 8 + place[block] * 4 + place[GROUPS + block]


def softmax(scores):
    exponents = jnp.exp(scores - jnp.max(scores, axis=-1, keepdims=True))
    return exponents / jnp.sum(exponents, axis=-1, keepdims=True)


def block_mask(lengths, first_item):
    per_block = BLOCK // SEQ
    row = lax.broadcasted_iota(jnp.int32, (BLOCK, BLOCK), 0)
    column = lax.broadcasted_iota(jnp.int32, (BLOCK, BLOCK), 1)
    row_item, column_item = lax.shift_right_logical(row, 6), lax.shift_right_logical(column, 6)
    slot = column - column_item * SEQ
    limit = jnp.zeros((BLOCK, BLOCK), jnp.int32)
    for item in range(per_block):
        limit = jnp.where(column_item == item, lengths[first_item + item] + QUERIES, limit)
    return (row_item == column_item) & (slot < limit)


def self_forward_kernel(
    place,
    lengths,
    hidden,
    in_own,
    in_other,
    out_own,
    out_other,
    first_in,
    qkv,
    heads,
    w_qkv,
    w_cross,
    w_self_out,
    w_cross_out,
    norm,
    self_rows,
    cross_rows,
):
    rows, features = hidden.shape
    width = features // MODEL
    block_rows = features // GROUPS
    out_rows = width // GROUPS
    norm_sum = jnp.zeros((NORM_ROWS, features), F32)
    for block in range(GROUPS):
        pieces = []
        for model in range(MODEL):
            side, y_rel = divmod(model, 2)
            pieces.append((in_own, in_other)[side][slot_x(place, block, y_rel)])
            out_piece = (out_own, out_other)[side][slot_y(place, block, y_rel)].astype(F32)
            begin = model * width + block * out_rows
            self_rows[begin : begin + out_rows, :] = out_piece[:out_rows]
            cross_rows[begin : begin + out_rows, :] = out_piece[out_rows : 2 * out_rows]
            norm_sum = norm_sum + out_piece[2 * out_rows :]
        begin = block * block_rows
        for kind in range(4):
            joined = jnp.concatenate(
                [piece[:, kind * width : (kind + 1) * width] for piece in pieces], axis=1
            )
            if kind < 3:
                w_qkv[begin : begin + block_rows, kind * features : (kind + 1) * features] = joined
            else:
                w_cross[begin : begin + block_rows, :] = joined
    norm[...] = norm_sum
    w_self_out[...] = self_rows[...].astype(BF16)
    w_cross_out[...] = cross_rows[...].astype(BF16)
    tokens = hidden[...]
    for kind in range(3):
        columns = slice(kind * features, (kind + 1) * features)
        qkv[:, columns] = dot_nn(tokens, w_qkv[:, columns]).astype(BF16)
    scale = HEAD ** (-0.5)
    for begin in range(0, rows, BLOCK):
        span = slice(begin, begin + BLOCK)
        mask = block_mask(lengths, begin // SEQ)
        for pair in range(features // (2 * HEAD)):
            results = []
            for head in (2 * pair, 2 * pair + 1):
                parts = [
                    qkv[span, kind * features + head * HEAD : kind * features + (head + 1) * HEAD]
                    for kind in range(3)
                ]
                scores = jnp.where(mask, dot_nt(parts[0], parts[1]) * scale, MASK_VALUE)
                results.append(dot_nn(softmax(scores).astype(BF16), parts[2]).astype(BF16))
            heads[span, pair * 2 * HEAD : (pair + 1) * 2 * HEAD] = jnp.concatenate(results, axis=1)
    first_in[...] = tokens.astype(F32) + dot_nn(heads[...], w_self_out[...])


def assemble_image(place, image_own, image_other, weight):
    block_rows = image_own.shape[1]
    width = image_own.shape[2] // 2
    features = width * MODEL
    for block in range(GROUPS):
        pieces = []
        for model in range(MODEL):
            side, y_rel = divmod(model, 2)
            pieces.append((image_own, image_other)[side][slot_y(place, block, y_rel)])
        begin = block * block_rows
        for kind in range(2):
            weight[begin : begin + block_rows, kind * features : (kind + 1) * features] = (
                jnp.concatenate(
                    [piece[:, kind * width : (kind + 1) * width] for piece in pieces], axis=1
                )
            )


def image_forward_kernel(place, feats, image_own, image_other, key_values, weight):
    @pl.when(pl.program_id(0) == 0)
    def _():
        assemble_image(place, image_own, image_other, weight)

    key_values[0] = dot_nn(feats[0], weight[...]).astype(BF16)


def head_rows(values, head_mask):
    stacked = jnp.concatenate([values] * (WIDE // HEAD), axis=0)
    return jnp.where(head_mask, stacked, jnp.zeros_like(stacked))


def fold_heads(values, head_mask):
    kept = jnp.where(head_mask, values, 0.0)
    count = WIDE // HEAD
    size = values.shape[0] // count
    total = kept[:size]
    for index in range(1, count):
        total = total + kept[index * size : (index + 1) * size]
    return total


def query_head_mask():
    shape = (QUERIES * (WIDE // HEAD), WIDE)
    row = lax.broadcasted_iota(jnp.int32, shape, 0)
    column = lax.broadcasted_iota(jnp.int32, shape, 1)
    return lax.shift_right_logical(row, 5) == lax.shift_right_logical(column, 6)


def query_rows(values):
    items = values.shape[0] // SEQ
    return jnp.concatenate(
        [values[item * SEQ : item * SEQ + QUERIES] for item in range(items)], axis=0
    )


def cross_forward_kernel(first_in, norm, w_cross, w_cross_out, key_values, second_in, queries, heads):
    features = first_in.shape[1]
    items = key_values.shape[0]
    normed, _ = normalise(query_rows(first_in[...]))
    one_query = normed * norm[0:1, :] + norm[1:2, :]
    queries[...] = dot_nn(one_query.astype(BF16), w_cross[...]).astype(BF16)
    head_mask = query_head_mask()
    scale = HEAD ** (-0.5)

    @pl.loop(0, items)
    def _(item):
        span = pl.ds(pl.multiple_of(item * QUERIES, QUERIES), QUERIES)
        for begin in range(0, features, WIDE):
            columns = slice(begin, begin + WIDE)
            value_columns = slice(features + begin, features + begin + WIDE)
            expanded = head_rows(queries[span, columns], head_mask)
            probs = softmax(dot_nt(expanded, key_values[item, :, columns]) * scale)
            mixed = dot_nn(probs.astype(BF16), key_values[item, :, value_columns])
            heads[span, columns] = fold_heads(mixed, head_mask).astype(BF16)

    second_in[...] = one_query + dot_nn(heads[...], w_cross_out[...])


def gelu_cumulative(inputs):
    return 0.5 * (1.0 + lax.erf(inputs * 0.7071067811865476))


def feed_kernel(
    place,
    lengths,
    first_in,
    second_in,
    norm,
    out_grad,
    up_own,
    up_other,
    down_own,
    down_other,
    block_out,
    two_grad,
    up_keep,
    up_send,
    down_keep,
    down_send,
    norm_grads,
    w_up,
    w_down,
    two_rows,
    pre_act,
    active,
):
    rows, features = first_in.shape
    items = rows // SEQ
    hidden_width = up_own.shape[2]
    up_rows = up_own.shape[1]
    down_rows = down_own.shape[1]
    for block in range(GROUPS):
        for model in range(MODEL):
            side, y_rel = divmod(model, 2)
            w_up[
                block * up_rows : (block + 1) * up_rows,
                model * hidden_width : (model + 1) * hidden_width,
            ] = (up_own, up_other)[side][slot_x(place, block, y_rel)]
            begin = model * hidden_width + block * down_rows
            w_down[begin : begin + down_rows, :] = (down_own, down_other)[side][
                slot_y(place, block, y_rel)
            ]
    normed_one, _ = normalise(first_in[...])
    after_one = normed_one * norm[0:1, :] + norm[1:2, :]
    normed_two, _ = normalise(second_in[...])
    after_two = normed_two * norm[2:3, :] + norm[3:4, :]
    for item in range(items):
        begin = item * SEQ
        two_rows[begin : begin + QUERIES, :] = after_two[item * QUERIES : (item + 1) * QUERIES]
        two_rows[begin + QUERIES : begin + SEQ, :] = after_one[begin + QUERIES : begin + SEQ]
    feed_in = two_rows[...].astype(BF16)
    third_in = two_rows[...]
    for model in range(MODEL):
        columns = slice(model * hidden_width, (model + 1) * hidden_width)
        pre = dot_nn(feed_in, w_up[:, columns])
        pre_act[:, columns] = pre
        act = (pre * gelu_cumulative(pre)).astype(BF16)
        active[:, columns] = act
        third_in = third_in + dot_nn(act, w_down[columns, :])
    normed, inverse = normalise(third_in)
    block_out[...] = (normed * norm[4:5, :] + norm[5:6, :]).astype(BF16)
    position = lax.broadcasted_iota(jnp.int32, (SEQ, features), 0)
    slope = jnp.concatenate(
        [
            jnp.where(
                position < lengths[item] + QUERIES,
                out_grad[item * SEQ : (item + 1) * SEQ, :].astype(F32),
                0.0,
            )
            for item in range(items)
        ],
        axis=0,
    )
    norm_grads[...] = jnp.zeros_like(norm_grads)
    norm_grads[4:5, :] = jnp.sum(slope * normed, axis=0, keepdims=True)
    norm_grads[5:6, :] = jnp.sum(slope, axis=0, keepdims=True)
    third_grad = norm_back(slope, normed, inverse, norm[4:5, :])
    grad_rows = third_grad.astype(BF16)
    two_grad[...] = third_grad
    for model in range(MODEL):
        side, y_rel = divmod(model, 2)
        columns = slice(model * hidden_width, (model + 1) * hidden_width)
        grad_down = dot_tn(active[:, columns], grad_rows).astype(BF16)
        for block in range(GROUPS):
            (down_keep, down_send)[side][slot_y(place, block, y_rel)] = grad_down[
                block * down_rows : (block + 1) * down_rows
            ]
        pre = pre_act[:, columns]
        density = jnp.exp(-0.5 * pre * pre) * 0.3989422804014327
        slope_part = gelu_cumulative(pre) + pre * density
        grad_pre = (dot_nt(grad_rows, w_down[columns, :]) * slope_part).astype(BF16)
        grad_up = dot_tn(feed_in, grad_pre).astype(BF16)
        for block in range(GROUPS):
            (up_keep, up_send)[side][slot_x(place, block, y_rel)] = grad_up[
                block * up_rows : (block + 1) * up_rows
            ]
        two_grad[...] += dot_nt(grad_pre, w_up[:, columns])


def cross_backward_kernel(
    two_grad,
    first_in,
    second_in,
    norm,
    w_cross,
    w_cross_out,
    queries,
    heads,
    key_values,
    norm_grads_in,
    grad_key_values,
    grad_cross,
    grad_cross_out,
    one_query_grad,
    norm_grads,
    head_grads,
    query_grads,
):
    features = first_in.shape[1]
    items = key_values.shape[0]
    two_query = query_rows(two_grad[...])
    normed, inverse = normalise(second_in[...])
    norm_grads[...] = norm_grads_in[...]
    norm_grads[2:3, :] = jnp.sum(two_query * normed, axis=0, keepdims=True)
    norm_grads[3:4, :] = jnp.sum(two_query, axis=0, keepdims=True)
    second_grad = norm_back(two_query, normed, inverse, norm[2:3, :])
    grad_rows = second_grad.astype(BF16)
    head_grads[...] = dot_nt(grad_rows, w_cross_out[...]).astype(BF16)
    grad_cross_out[...] = dot_tn(heads[...], grad_rows).astype(BF16)
    head_mask = query_head_mask()
    scale = HEAD ** (-0.5)

    @pl.loop(0, items)
    def _(item):
        span = pl.ds(pl.multiple_of(item * QUERIES, QUERIES), QUERIES)
        for begin in range(0, features, WIDE):
            columns = slice(begin, begin + WIDE)
            value_columns = slice(features + begin, features + begin + WIDE)
            expanded = head_rows(queries[span, columns], head_mask)
            expanded_grad = head_rows(head_grads[span, columns], head_mask)
            keys = key_values[item, :, columns]
            probs = softmax(dot_nt(expanded, keys) * scale)
            grad_probs = dot_nt(expanded_grad, key_values[item, :, value_columns])
            inner = jnp.sum(grad_probs * probs, axis=-1, keepdims=True)
            grad_scores = (probs * (grad_probs - inner)).astype(BF16)
            grad_key_values[item, :, value_columns] = dot_tn(
                probs.astype(BF16), expanded_grad
            ).astype(BF16)
            grad_key_values[item, :, columns] = (dot_tn(grad_scores, expanded) * scale).astype(BF16)
            query_grads[span, columns] = (
                fold_heads(dot_nn(grad_scores, keys), head_mask) * scale
            ).astype(BF16)

    normed_one, _ = normalise(query_rows(first_in[...]))
    query_in = (normed_one * norm[0:1, :] + norm[1:2, :]).astype(BF16)
    grad_cross[...] = dot_tn(query_in, query_grads[...]).astype(BF16)
    one_query_grad[...] = second_grad + dot_nt(query_grads[...], w_cross[...])


def image_backward_kernel(place, feats, grad_key_values, image_keep, image_send, total):
    block_rows = image_keep.shape[1]
    width = image_keep.shape[2] // 2
    features = width * MODEL

    @pl.when(pl.program_id(0) == 0)
    def _():
        total[...] = jnp.zeros_like(total)

    total[...] += dot_tn(feats[0], grad_key_values[0])

    @pl.when(pl.program_id(0) == pl.num_programs(0) - 1)
    def _():
        for block in range(GROUPS):
            span = slice(block * block_rows, (block + 1) * block_rows)
            for model in range(MODEL):
                side, y_rel = divmod(model, 2)
                piece = jnp.concatenate(
                    [
                        total[span, begin + model * width : begin + (model + 1) * width]
                        for begin in (0, features)
                    ],
                    axis=1,
                )
                (image_keep, image_send)[side][slot_y(place, block, y_rel)] = piece.astype(BF16)


def self_backward_kernel(
    place,
    lengths,
    one_query_grad,
    two_grad,
    first_in,
    norm,
    hidden,
    qkv,
    heads,
    w_qkv,
    w_self_out,
    grad_cross,
    grad_cross_out,
    norm_grads_in,
    input_grad,
    in_keep,
    in_send,
    out_keep,
    out_send,
    one_grad,
    head_grads,
    grad_qkv,
    grad_weights,
):
    rows, features = hidden.shape
    items = rows // SEQ
    width = features // MODEL
    block_rows = features // GROUPS
    out_rows = width // GROUPS
    for item in range(items):
        begin = item * SEQ
        one_grad[begin : begin + QUERIES, :] = one_query_grad[
            item * QUERIES : (item + 1) * QUERIES, :
        ]
        one_grad[begin + QUERIES : begin + SEQ, :] = two_grad[begin + QUERIES : begin + SEQ, :]
    normed, inverse = normalise(first_in[...])
    gradient = one_grad[...]
    norm_total = norm_grads_in[...] + jnp.concatenate(
        [
            jnp.sum(gradient * normed, axis=0, keepdims=True),
            jnp.sum(gradient, axis=0, keepdims=True),
            jnp.zeros((NORM_ROWS - 2, features), F32),
        ],
        axis=0,
    )
    first_grad = norm_back(gradient, normed, inverse, norm[0:1, :])
    one_grad[...] = first_grad
    grad_rows = first_grad.astype(BF16)
    head_grads[...] = dot_nt(grad_rows, w_self_out[...]).astype(BF16)
    scale = HEAD ** (-0.5)
    for begin in range(0, rows, BLOCK):
        span = slice(begin, begin + BLOCK)
        mask = block_mask(lengths, begin // SEQ)
        for pair in range(features // (2 * HEAD)):
            results = [[], [], []]
            for head in (2 * pair, 2 * pair + 1):
                queries, key_rows, value_rows = [
                    qkv[span, kind * features + head * HEAD : kind * features + (head + 1) * HEAD]
                    for kind in range(3)
                ]
                head_grad = head_grads[span, head * HEAD : (head + 1) * HEAD]
                probs = softmax(jnp.where(mask, dot_nt(queries, key_rows) * scale, MASK_VALUE))
                grad_probs = dot_nt(head_grad, value_rows)
                inner = jnp.sum(grad_probs * probs, axis=-1, keepdims=True)
                grad_scores = (probs * (grad_probs - inner)).astype(BF16)
                results[0].append((dot_nn(grad_scores, key_rows) * scale).astype(BF16))
                results[1].append((dot_tn(grad_scores, queries) * scale).astype(BF16))
                results[2].append(dot_tn(probs.astype(BF16), head_grad).astype(BF16))
            for kind in range(3):
                first = kind * features + pair * 2 * HEAD
                grad_qkv[span, first : first + 2 * HEAD] = jnp.concatenate(results[kind], axis=1)
    tokens = hidden[...]
    total = one_grad[...]
    for kind in range(3):
        columns = slice(kind * features, (kind + 1) * features)
        total = total + dot_nt(grad_qkv[:, columns], w_qkv[:, columns])
        grad_weights[:, columns] = dot_tn(tokens, grad_qkv[:, columns]).astype(BF16)
    input_grad[...] = total.astype(BF16)
    for block in range(GROUPS):
        span = slice(block * block_rows, (block + 1) * block_rows)
        for model in range(MODEL):
            side, y_rel = divmod(model, 2)
            columns = slice(model * width, (model + 1) * width)
            piece = [
                grad_weights[
                    span, kind * features + model * width : kind * features + (model + 1) * width
                ]
                for kind in range(3)
            ]
            piece.append(grad_cross[span, columns])
            (in_keep, in_send)[side][slot_x(place, block, y_rel)] = jnp.concatenate(piece, axis=1)
    grad_self_out = dot_tn(heads[...], grad_rows)
    grad_other_out = grad_cross_out[...].astype(F32)
    for block in range(GROUPS):
        for model in range(MODEL):
            side, y_rel = divmod(model, 2)
            begin = model * width + block * out_rows
            piece = jnp.concatenate(
                [
                    grad_self_out[begin : begin + out_rows],
                    grad_other_out[begin : begin + out_rows],
                    norm_total,
                ],
                axis=0,
            )
            (out_keep, out_send)[side][slot_y(place, block, y_rel)] = piece.astype(BF16)


SCALARS = pl.BlockSpec(memory_space=pltpu.SMEM)
WHOLE = pl.BlockSpec(memory_space=pltpu.VMEM)


def local_call(kernel, scalars, arrays, out_shapes, scratch, flops, name):
    size = sum(a.size * a.dtype.itemsize for a in arrays)
    size += sum(a.size * a.dtype.itemsize for a in out_shapes)
    return pl.pallas_call(
        kernel,
        out_shape=tuple(out_shapes),
        in_specs=[SCALARS] * len(scalars) + [WHOLE] * len(arrays),
        out_specs=tuple([WHOLE] * len(out_shapes)),
        scratch_shapes=scratch,
        compiler_params=pltpu.CompilerParams(vmem_limit_bytes=VMEM_LIMIT),
        cost_estimate=pl.CostEstimate(flops=flops, bytes_accessed=size, transcendentals=0),
        name=name,
    )(*scalars, *arrays)


def shape_of(*dims, dtype=BF16):
    return jax.ShapeDtypeStruct(dims, dtype)


class Direct:
    def __init__(self, dp, mp):
        self.count = dp * mp
        self.mp = mp
        self.depth = dp // 2
        index = lax.axis_index("dp")
        block = jnp.arange(GROUPS, dtype=jnp.int32)
        along_x = (block % 2) ^ (index % 2)
        along_z = (index // 2 - block // 2) % self.depth
        self.place = jnp.concatenate([along_x, along_z]).astype(jnp.int32)

    def hop(self, values, flip):
        return lax.ppermute(values, AXES, [(i, i ^ flip) for i in range(self.count)])

    def hop_core(self, values):
        return self.hop(values, 1)

    def hop_y(self, values):
        return self.hop(values, 2)

    def hop_x(self, values):
        return self.hop(values, self.mp)

    def hop_z(self, values):
        step = 2 * self.mp
        return lax.ppermute(values, AXES, [(i, (i + step) % self.count) for i in range(self.count)])

    def collect(self, piece, x_last):
        ring = [piece]
        for _ in range(self.depth - 1):
            ring.append(self.hop_z(ring[-1]))
        held = jnp.stack(ring)
        for hop in (self.hop_y, self.hop_x) if x_last else (self.hop_x, self.hop_y):
            held = jnp.concatenate([held, hop(held)])
        return held, self.hop_core(held)

    def scatter(self, keep, send, x_first):
        total = add(keep, self.hop_core(send))
        for hop in (self.hop_x, self.hop_y) if x_first else (self.hop_y, self.hop_x):
            half = total.shape[0] // 2
            total = add(total[:half], hop(total[half:]))
        carried = self.hop_z(total[1])
        for index in range(2, self.depth):
            carried = self.hop_z(add(total[index], carried))
        return total[0].astype(F32) + carried.astype(F32)


class Plain:
    def __init__(self, dp, mp):
        self.dp = dp
        self.mp = mp
        block = jnp.arange(GROUPS, dtype=jnp.int32)
        self.place = jnp.concatenate([block % 2, block // 2]).astype(jnp.int32)

    def collect(self, piece, x_last):
        rows, width = piece.shape
        blocks = lax.all_gather(piece, AXES, axis=0).reshape(self.dp, self.mp, rows, width)
        blocks = blocks.transpose(1, 0, 2, 3).reshape(2, 2, 4, 2, rows * self.dp // GROUPS, width)
        order = (0, 3, 1, 2, 4, 5) if x_last else (0, 1, 3, 2, 4, 5)
        blocks = blocks.transpose(order).reshape(2, SLOTS, rows * self.dp // GROUPS, width)
        return blocks[0], blocks[1]

    def scatter(self, keep, send, x_first):
        _, rows, width = keep.shape
        both = jnp.stack([keep, send])
        if x_first:
            both = both.reshape(2, 2, 2, 4, rows, width).transpose(0, 2, 3, 1, 4, 5)
        else:
            both = both.reshape(2, 2, 2, 4, rows, width).transpose(0, 1, 3, 2, 4, 5)
        both = both.reshape(self.mp, self.dp, rows * GROUPS // self.dp, width)
        both = both.transpose(1, 0, 2, 3).reshape(-1, width)
        return lax.psum_scatter(both.astype(F32), AXES, scatter_dimension=0, tiled=True)


def add(left_side, right_side):
    return (left_side.astype(F32) + right_side.astype(F32)).astype(BF16)


def adam_step(weight, moments, gradient, decay_rate):
    moment_one = BETA_ONE * moments[0] + (1.0 - BETA_ONE) * gradient
    moment_two = BETA_TWO * moments[1] + (1.0 - BETA_TWO) * gradient * gradient
    update = (
        moment_one
        / (1.0 - BETA_ONE**STEP)
        / (jnp.sqrt(moment_two / (1.0 - BETA_TWO**STEP)) + ADAM_EPSILON)
        + decay_rate * weight
    )
    return (moment_one, moment_two, update)


def tensor_squares(values, per_slice):
    if per_slice:
        return jnp.sum(values * values, axis=tuple(range(1, values.ndim)))
    return jnp.sum(values * values)[None]


def per_device(
    hidden_in,
    image_feats,
    caption_lengths,
    out_grad,
    proj_in,
    proj_in_moments,
    proj_in_average,
    proj_out,
    proj_out_moments,
    proj_out_average,
    image_kv,
    image_kv_moments,
    image_kv_average,
    feed_up,
    feed_up_moments,
    feed_up_average,
    feed_down,
    feed_down_moments,
    feed_down_average,
    norm_params,
    norm_params_moments,
    norm_params_average,
):
    data_ways, model_ways = lax.axis_size("dp"), lax.axis_size("mp")
    data_index, model_index = lax.axis_index("dp"), lax.axis_index("mp")
    rows, features = hidden_in.shape
    items = rows // SEQ
    patches, encoded = image_feats.shape[1:]
    hidden_width = feed_up.shape[1] * model_ways
    width = features // model_ways
    own_norm = norm_params.shape[1]
    norm_begin = (model_index * data_ways + data_index) * own_norm
    direct = data_ways == GROUPS and model_ways == MODEL
    moves = (Direct if direct else Plain)(data_ways, model_ways)
    place = moves.place
    lengths = lax.dynamic_slice_in_dim(caption_lengths, model_index * items, items, 0)
    first_item = (model_index * items).astype(jnp.int32)

    image_piece = jnp.concatenate([image_kv[0], image_kv[1]], axis=1).astype(BF16)
    in_piece = jnp.concatenate([proj_in[kind] for kind in range(4)], axis=1).astype(BF16)
    norm_rows = lax.dynamic_update_slice(
        jnp.zeros((NORM_ROWS, features), F32), norm_params, (0, norm_begin)
    ).astype(BF16)
    in_own, in_other = moves.collect(in_piece, True)
    if direct:
        out_piece = jnp.concatenate(
            [proj_out[0].astype(BF16), proj_out[1].astype(BF16), norm_rows], axis=0
        )
        out_own, out_other = moves.collect(out_piece, False)
    else:
        parts = [moves.collect(proj_out[kind].astype(BF16), False) for kind in range(2)]
        norm_all = lax.psum(norm_rows.astype(F32), AXES).astype(BF16)
        norm_first = jnp.zeros((SLOTS, NORM_ROWS, features), BF16).at[0].set(norm_all)
        out_own = jnp.concatenate([parts[0][0], parts[1][0], norm_first], axis=1)
        out_other = jnp.concatenate(
            [parts[0][1], parts[1][1], jnp.zeros_like(norm_first)], axis=1
        )
    image_own, image_other = moves.collect(image_piece, False)
    up_own, up_other = moves.collect(feed_up.astype(BF16), True)
    down_own, down_other = moves.collect(feed_down.astype(BF16), False)

    first_in, qkv, heads, w_qkv, w_cross, w_self_out, w_cross_out, norm = local_call(
        self_forward_kernel,
        (place, lengths),
        (hidden_in, in_own, in_other, out_own, out_other),
        (
            shape_of(rows, features, dtype=F32),
            shape_of(rows, 3 * features),
            shape_of(rows, features),
            shape_of(features, 3 * features),
            shape_of(features, features),
            shape_of(features, features),
            shape_of(features, features),
            shape_of(NORM_ROWS, features, dtype=F32),
        ),
        [pltpu.VMEM((features, features), F32), pltpu.VMEM((features, features), F32)],
        10 * rows * features * features,
        "self_forward",
    )
    image_place = jnp.concatenate([place, first_item[None]])
    feats_spec = pl.BlockSpec(
        (1, patches, encoded), lambda item, where: (where[2 * GROUPS] + item, 0, 0)
    )
    item_spec = pl.BlockSpec((1, patches, 2 * features), lambda item, where: (item, 0, 0))
    piece_spec = pl.BlockSpec(image_own.shape, lambda item, where: (0, 0, 0))
    image_cost = pl.CostEstimate(
        flops=4 * items * patches * encoded * features,
        bytes_accessed=2 * items * patches * (encoded + 2 * features) + 4 * encoded * features,
        transcendentals=0,
    )
    key_values = pl.pallas_call(
        image_forward_kernel,
        out_shape=shape_of(items, patches, 2 * features),
        grid_spec=pltpu.PrefetchScalarGridSpec(
            num_scalar_prefetch=1,
            grid=(items,),
            in_specs=[feats_spec, piece_spec, piece_spec],
            out_specs=item_spec,
            scratch_shapes=[pltpu.VMEM((encoded, 2 * features), BF16)],
        ),
        compiler_params=pltpu.CompilerParams(vmem_limit_bytes=VMEM_LIMIT),
        cost_estimate=image_cost,
        name="image_forward",
    )(image_place, image_feats, image_own, image_other)
    query_count = items * QUERIES
    second_in, cross_queries, cross_heads = local_call(
        cross_forward_kernel,
        (),
        (first_in, norm, w_cross, w_cross_out, key_values),
        (
            shape_of(query_count, features, dtype=F32),
            shape_of(query_count, features),
            shape_of(query_count, features),
        ),
        [],
        4 * query_count * features * features,
        "cross_forward",
    )
    piece_shape = up_own.shape
    block_out, two_grad, up_keep, up_send, down_keep, down_send, norm_grads = local_call(
        feed_kernel,
        (place, lengths),
        (
            first_in,
            second_in,
            norm,
            out_grad,
            up_own,
            up_other,
            down_own,
            down_other,
        ),
        (
            shape_of(rows, features),
            shape_of(rows, features, dtype=F32),
            shape_of(*piece_shape),
            shape_of(*piece_shape),
            shape_of(*down_own.shape),
            shape_of(*down_own.shape),
            shape_of(NORM_ROWS, features, dtype=F32),
        ),
        [
            pltpu.VMEM((features, hidden_width), BF16),
            pltpu.VMEM((hidden_width, features), BF16),
            pltpu.VMEM((rows, features), F32),
            pltpu.VMEM((rows, hidden_width), F32),
            pltpu.VMEM((rows, hidden_width), BF16),
        ],
        12 * rows * features * hidden_width,
        "feed",
    )
    up_shard = moves.scatter(up_keep, up_send, True)
    down_shard = moves.scatter(down_keep, down_send, False)

    grad_key_values, grad_cross, grad_cross_out, one_query_grad, norm_grads = local_call(
        cross_backward_kernel,
        (),
        (
            two_grad,
            first_in,
            second_in,
            norm,
            w_cross,
            w_cross_out,
            cross_queries,
            cross_heads,
            key_values,
            norm_grads,
        ),
        (
            shape_of(items, patches, 2 * features),
            shape_of(features, features),
            shape_of(features, features),
            shape_of(query_count, features, dtype=F32),
            shape_of(NORM_ROWS, features, dtype=F32),
        ),
        [pltpu.VMEM((query_count, features), BF16), pltpu.VMEM((query_count, features), BF16)],
        8 * query_count * features * features,
        "cross_backward",
    )
    image_keep, image_send = pl.pallas_call(
        image_backward_kernel,
        out_shape=(shape_of(*image_own.shape), shape_of(*image_own.shape)),
        grid_spec=pltpu.PrefetchScalarGridSpec(
            num_scalar_prefetch=1,
            grid=(items,),
            in_specs=[feats_spec, item_spec],
            out_specs=(piece_spec, piece_spec),
            scratch_shapes=[pltpu.VMEM((encoded, 2 * features), F32)],
        ),
        compiler_params=pltpu.CompilerParams(vmem_limit_bytes=VMEM_LIMIT),
        cost_estimate=image_cost,
        name="image_backward",
    )(image_place, image_feats, grad_key_values)
    image_shard = moves.scatter(image_keep, image_send, False)
    input_grad, in_keep, in_send, out_keep, out_send = local_call(
        self_backward_kernel,
        (place, lengths),
        (
            one_query_grad,
            two_grad,
            first_in,
            norm,
            hidden_in,
            qkv,
            heads,
            w_qkv,
            w_self_out,
            grad_cross,
            grad_cross_out,
            norm_grads,
        ),
        (
            shape_of(rows, features),
            shape_of(*in_own.shape),
            shape_of(*in_own.shape),
            shape_of(*out_own.shape),
            shape_of(*out_own.shape),
        ),
        [
            pltpu.VMEM((rows, features), F32),
            pltpu.VMEM((rows, features), BF16),
            pltpu.VMEM((rows, 3 * features), BF16),
            pltpu.VMEM((features, 3 * features), BF16),
        ],
        20 * rows * features * features,
        "self_backward",
    )
    in_shard = moves.scatter(in_keep, in_send, True)
    out_rows = proj_out.shape[1]
    if direct:
        out_sum = moves.scatter(out_keep, out_send, False)
        norm_sum = out_sum[2 * out_rows :]
        out_shard = jnp.stack([out_sum[:out_rows], out_sum[out_rows : 2 * out_rows]])
    else:
        piece = width // GROUPS
        norm_sum = lax.psum(out_keep[0, 2 * piece :].astype(F32), AXES)
        out_shard = jnp.stack(
            [
                moves.scatter(
                    out_keep[:, kind * piece : (kind + 1) * piece],
                    out_send[:, kind * piece : (kind + 1) * piece],
                    False,
                )
                for kind in range(2)
            ]
        )
    norm_shard = lax.dynamic_slice(norm_sum, (0, norm_begin), norm_params.shape)
    in_shard = jnp.stack([in_shard[:, kind * width : (kind + 1) * width] for kind in range(4)])
    image_shard = jnp.stack([image_shard[:, :width], image_shard[:, width:]])

    groups = [
        (proj_in, proj_in_moments, proj_in_average, in_shard, DECAY_RATE, True),
        (proj_out, proj_out_moments, proj_out_average, out_shard, DECAY_RATE, True),
        (image_kv, image_kv_moments, image_kv_average, image_shard, DECAY_RATE, True),
        (feed_up, feed_up_moments, feed_up_average, up_shard, DECAY_RATE, False),
        (feed_down, feed_down_moments, feed_down_average, down_shard, DECAY_RATE, False),
        (norm_params, norm_params_moments, norm_params_average, norm_shard, 0.0, True),
    ]
    updates = []
    weight_squares = []
    update_squares = []
    for weight, moments, average, gradient, decay_rate, per_slice in groups:
        moment_one, moment_two, update = adam_step(weight, moments, gradient, decay_rate)
        updates.append((moment_one, moment_two, update))
        weight_squares.append(tensor_squares(weight, per_slice))
        update_squares.append(tensor_squares(update, per_slice))
    own_squares = jnp.stack([jnp.concatenate(weight_squares), jnp.concatenate(update_squares)])
    ways = data_ways * model_ways
    copies = jnp.broadcast_to(own_squares[None], (ways,) + own_squares.shape)
    squares = jnp.sum(lax.all_to_all(copies, AXES, 0, 0, tiled=True), axis=0)
    trust = jnp.sqrt(squares[0]) * lax.rsqrt(squares[1] + SQUARE_EPSILON)
    outputs = []
    offset = 0
    for group, stepped in zip(groups, updates):
        weight, moments, average, gradient, decay_rate, per_slice = group
        moment_one, moment_two, update = stepped
        slices = weight.shape[0] if per_slice else 1
        trust_part = trust[offset : offset + slices]
        if per_slice:
            trust_part = trust_part.reshape((slices,) + (1,) * (weight.ndim - 1))
        else:
            trust_part = trust_part[0]
        new_weight = weight - LEARN_RATE * trust_part * update
        outputs.append(new_weight)
        outputs.append(jnp.stack([moment_one, moment_two]))
        outputs.append(AVERAGE_RATE * average + (1.0 - AVERAGE_RATE) * new_weight)
        offset += slices
    return (block_out, input_grad, *outputs, trust, jnp.sqrt(squares))


def solution(mesh):
    rows = P(AXES, None)
    by_column = P(None, "dp", "mp")
    by_row = P(None, ("mp", "dp"), None)
    weights = (
        by_column,
        P(None, None, "dp", "mp"),
        by_column,
        by_row,
        P(None, None, ("mp", "dp"), None),
        by_row,
        by_column,
        P(None, None, "dp", "mp"),
        by_column,
        P("dp", "mp"),
        P(None, "dp", "mp"),
        P("dp", "mp"),
        P(("mp", "dp"), None),
        P(None, ("mp", "dp"), None),
        P(("mp", "dp"), None),
        P(None, ("mp", "dp")),
        P(None, None, ("mp", "dp")),
        P(None, ("mp", "dp")),
    )
    return jax.shard_map(
        per_device,
        mesh=mesh,
        in_specs=(rows, P("dp", None, None), P("dp"), rows, *weights),
        out_specs=(rows, rows, *weights, P(), P()),
        check_vma=False,
    )
```

```python
import jax
import jax.numpy as jnp
from jax import lax
from jax.experimental import pallas as pl
from jax.experimental.pallas import tpu as pltpu
from jax.sharding import PartitionSpec as P

HEAD = 64
PATCHES = 257
QUERIES = 32
TEXT = 32
SEQ = QUERIES + TEXT
STEP = 10


NORM_EPSILON = 1e-06
ADAM_EPSILON = 1e-06
SQUARE_EPSILON = 1e-06
BETA_ONE = 0.9
BETA_TWO = 0.999
LEARN_RATE = 0.5
DECAY_RATE = 0.01
AVERAGE_RATE = 0.6
MASK_VALUE = -1e30

AXES = ("dp", "mp")
GROUPS = 8
MODEL = 4
SLOTS = 16
NORM_ROWS = 8
BLOCK = 256
WIDE = 256
MIB = 1024 * 1024

BF16 = jnp.bfloat16
F32 = jnp.float32


def dot_nn(left_side, right_side):
    return lax.dot_general(
        left_side, right_side, (((1,), (0,)), ((), ())), preferred_element_type=F32
    )


def dot_nt(left_side, right_side):
    return lax.dot_general(
        left_side, right_side, (((1,), (1,)), ((), ())), preferred_element_type=F32
    )


def dot_tn(left_side, right_side):
    return lax.dot_general(
        left_side, right_side, (((0,), (0,)), ((), ())), preferred_element_type=F32
    )


def normalise(inputs):
    centred = inputs - jnp.mean(inputs, axis=-1, keepdims=True)
    inverse = lax.rsqrt(jnp.mean(centred * centred, axis=-1, keepdims=True) + NORM_EPSILON)
    return centred * inverse, inverse


def norm_back(gradient, normed, inverse, gain):
    scaled = gradient * gain
    centre_term = jnp.mean(scaled, axis=-1, keepdims=True)
    normed_term = jnp.mean(scaled * normed, axis=-1, keepdims=True)
    return inverse * (scaled - centre_term - normed * normed_term)


def slot_of(place, block, y_rel):
    return place[block] * 8 + y_rel * 4 + place[GROUPS + block]


def softmax(scores):
    exponents = jnp.exp(scores - jnp.max(scores, axis=-1, keepdims=True))
    return exponents / jnp.sum(exponents, axis=-1, keepdims=True)


def block_mask(lengths, first_item):
    per_block = BLOCK // SEQ
    row = lax.broadcasted_iota(jnp.int32, (BLOCK, BLOCK), 0)
    column = lax.broadcasted_iota(jnp.int32, (BLOCK, BLOCK), 1)
    row_item, column_item = lax.shift_right_logical(row, 6), lax.shift_right_logical(column, 6)
    slot = column - column_item * SEQ
    limit = jnp.zeros((BLOCK, BLOCK), jnp.int32)
    for item in range(per_block):
        limit = jnp.where(column_item == item, lengths[first_item + item] + QUERIES, limit)
    return (row_item == column_item) & (slot < limit)


def self_forward_kernel(
    place,
    lengths,
    hidden,
    begin_own,
    begin_other,
    first_in,
    qkv,
    heads,
    w_qkv,
    w_cross,
    w_self_out,
    w_cross_out,
    norm,
    self_rows,
    cross_rows,
):
    rows, features = hidden.shape
    width = features // MODEL
    block_rows = features // GROUPS
    out_rows = width // GROUPS
    half, part = block_rows // 2, begin_own.shape[1] // 2
    norm_sum = jnp.zeros((NORM_ROWS, features), F32)
    for block in range(GROUPS):
        pieces = []
        for model in range(MODEL):
            side, y_rel = divmod(model, 2)
            source, slot = (begin_own, begin_other)[side], slot_of(place, block, y_rel)
            pieces.append(
                jnp.concatenate(
                    [source[slot, :half, :], source[slot, part : part + half, :]], axis=0
                )
            )
            cross_part = source[slot, half:part, :].astype(F32)
            self_part = source[slot, part + half :, :].astype(F32)
            begin = model * width + block * out_rows
            cross_rows[begin : begin + out_rows, :] = cross_part[:out_rows]
            self_rows[begin : begin + out_rows, :] = self_part[:out_rows]
            norm_sum = norm_sum + self_part[out_rows:]
        begin = block * block_rows
        for kind in range(4):
            joined = jnp.concatenate(
                [piece[:, kind * width : (kind + 1) * width] for piece in pieces], axis=1
            )
            if kind < 3:
                w_qkv[begin : begin + block_rows, kind * features : (kind + 1) * features] = joined
            else:
                w_cross[begin : begin + block_rows, :] = joined
    norm[...] = norm_sum
    w_self_out[...] = self_rows[...].astype(BF16)
    w_cross_out[...] = cross_rows[...].astype(BF16)
    tokens = hidden[...]
    for kind in range(3):
        columns = slice(kind * features, (kind + 1) * features)
        qkv[:, columns] = dot_nn(tokens, w_qkv[:, columns]).astype(BF16)
    scale = HEAD ** (-0.5)
    for begin in range(0, rows, BLOCK):
        span = slice(begin, begin + BLOCK)
        mask = block_mask(lengths, begin // SEQ)
        for pair in range(features // (2 * HEAD)):
            results = []
            for head in (2 * pair, 2 * pair + 1):
                parts = [
                    qkv[span, kind * features + head * HEAD : kind * features + (head + 1) * HEAD]
                    for kind in range(3)
                ]
                scores = jnp.where(mask, dot_nt(parts[0], parts[1]) * scale, MASK_VALUE)
                results.append(dot_nn(softmax(scores).astype(BF16), parts[2]).astype(BF16))
            heads[span, pair * 2 * HEAD : (pair + 1) * 2 * HEAD] = jnp.concatenate(results, axis=1)
    first_in[...] = tokens.astype(F32) + dot_nn(heads[...], w_self_out[...])


def assemble_image(place, image_own, image_other, weight):
    block_rows = image_own.shape[1]
    width = image_own.shape[2] // 2
    features = width * MODEL
    for block in range(GROUPS):
        pieces = []
        for model in range(MODEL):
            side, y_rel = divmod(model, 2)
            pieces.append((image_own, image_other)[side][slot_of(place, block, y_rel)])
        begin = block * block_rows
        for kind in range(2):
            weight[begin : begin + block_rows, kind * features : (kind + 1) * features] = (
                jnp.concatenate(
                    [piece[:, kind * width : (kind + 1) * width] for piece in pieces], axis=1
                )
            )


def image_forward_kernel(place, feats, image_own, image_other, key_values, weight):
    @pl.when(pl.program_id(0) == 0)
    def _():
        assemble_image(place, image_own, image_other, weight)

    key_values[0] = dot_nn(feats[0], weight[...]).astype(BF16)


def head_rows(values, head_mask):
    stacked = jnp.concatenate([values] * (WIDE // HEAD), axis=0)
    return jnp.where(head_mask, stacked, jnp.zeros_like(stacked))


def fold_heads(values, head_mask):
    kept = jnp.where(head_mask, values, 0.0)
    count = WIDE // HEAD
    size = values.shape[0] // count
    total = kept[:size]
    for index in range(1, count):
        total = total + kept[index * size : (index + 1) * size]
    return total


def query_head_mask():
    shape = (QUERIES * (WIDE // HEAD), WIDE)
    row = lax.broadcasted_iota(jnp.int32, shape, 0)
    column = lax.broadcasted_iota(jnp.int32, shape, 1)
    return lax.shift_right_logical(row, 5) == lax.shift_right_logical(column, 6)


def query_rows(values):
    items = values.shape[0] // SEQ
    return jnp.concatenate(
        [values[item * SEQ : item * SEQ + QUERIES] for item in range(items)], axis=0
    )


def cross_forward_kernel(first_in, norm, w_cross, w_cross_out, key_values, second_in, queries, heads):
    features = first_in.shape[1]
    items = key_values.shape[0]
    normed, _ = normalise(query_rows(first_in[...]))
    one_query = normed * norm[0:1, :] + norm[1:2, :]
    queries[...] = dot_nn(one_query.astype(BF16), w_cross[...]).astype(BF16)
    head_mask = query_head_mask()
    scale = HEAD ** (-0.5)

    @pl.loop(0, items)
    def _(item):
        span = pl.ds(pl.multiple_of(item * QUERIES, QUERIES), QUERIES)
        for begin in range(0, features, WIDE):
            columns = slice(begin, begin + WIDE)
            value_columns = slice(features + begin, features + begin + WIDE)
            expanded = head_rows(queries[span, columns], head_mask)
            probs = softmax(dot_nt(expanded, key_values[item, :, columns]) * scale)
            mixed = dot_nn(probs.astype(BF16), key_values[item, :, value_columns])
            heads[span, columns] = fold_heads(mixed, head_mask).astype(BF16)

    second_in[...] = one_query + dot_nn(heads[...], w_cross_out[...])


def gelu_cumulative(inputs):
    return 0.5 * (1.0 + lax.erf(inputs * 0.7071067811865476))


def feed_kernel(
    place,
    lengths,
    first_in,
    second_in,
    norm,
    out_grad,
    feed_own,
    feed_other,
    block_out,
    two_grad,
    feed_keep,
    feed_send,
    norm_grads,
    w_up,
    w_down,
    two_rows,
    pre_act,
    active,
):
    rows, features = first_in.shape
    items = rows // SEQ
    hidden_width = feed_own.shape[2]
    up_rows = down_rows = feed_own.shape[1] // 2
    for block in range(GROUPS):
        for model in range(MODEL):
            side, y_rel = divmod(model, 2)
            source, slot = (feed_own, feed_other)[side], slot_of(place, block, y_rel)
            w_up[
                block * up_rows : (block + 1) * up_rows,
                model * hidden_width : (model + 1) * hidden_width,
            ] = source[slot, :up_rows, :]
            begin = model * hidden_width + block * down_rows
            w_down[begin : begin + down_rows, :] = source[slot, up_rows:, :]
    normed_one, _ = normalise(first_in[...])
    after_one = normed_one * norm[0:1, :] + norm[1:2, :]
    normed_two, _ = normalise(second_in[...])
    after_two = normed_two * norm[2:3, :] + norm[3:4, :]
    for item in range(items):
        begin = item * SEQ
        two_rows[begin : begin + QUERIES, :] = after_two[item * QUERIES : (item + 1) * QUERIES]
        two_rows[begin + QUERIES : begin + SEQ, :] = after_one[begin + QUERIES : begin + SEQ]
    feed_in = two_rows[...].astype(BF16)
    third_in = two_rows[...]
    for model in range(MODEL):
        columns = slice(model * hidden_width, (model + 1) * hidden_width)
        pre = dot_nn(feed_in, w_up[:, columns])
        pre_act[:, columns] = pre
        act = (pre * gelu_cumulative(pre)).astype(BF16)
        active[:, columns] = act
        third_in = third_in + dot_nn(act, w_down[columns, :])
    normed, inverse = normalise(third_in)
    block_out[...] = (normed * norm[4:5, :] + norm[5:6, :]).astype(BF16)
    position = lax.broadcasted_iota(jnp.int32, (SEQ, features), 0)
    slope = jnp.concatenate(
        [
            jnp.where(
                position < lengths[item] + QUERIES,
                out_grad[item * SEQ : (item + 1) * SEQ, :].astype(F32),
                0.0,
            )
            for item in range(items)
        ],
        axis=0,
    )
    norm_grads[...] = jnp.zeros_like(norm_grads)
    norm_grads[4:5, :] = jnp.sum(slope * normed, axis=0, keepdims=True)
    norm_grads[5:6, :] = jnp.sum(slope, axis=0, keepdims=True)
    third_grad = norm_back(slope, normed, inverse, norm[4:5, :])
    grad_rows = third_grad.astype(BF16)
    two_grad[...] = third_grad
    for model in range(MODEL):
        side, y_rel = divmod(model, 2)
        columns = slice(model * hidden_width, (model + 1) * hidden_width)
        grad_down = dot_tn(active[:, columns], grad_rows).astype(BF16)
        for block in range(GROUPS):
            (feed_keep, feed_send)[side][slot_of(place, block, y_rel), up_rows:, :] = grad_down[
                block * down_rows : (block + 1) * down_rows
            ]
        pre = pre_act[:, columns]
        density = jnp.exp(-0.5 * pre * pre) * 0.3989422804014327
        slope_part = gelu_cumulative(pre) + pre * density
        grad_pre = (dot_nt(grad_rows, w_down[columns, :]) * slope_part).astype(BF16)
        grad_up = dot_tn(feed_in, grad_pre).astype(BF16)
        for block in range(GROUPS):
            (feed_keep, feed_send)[side][slot_of(place, block, y_rel), :up_rows, :] = grad_up[
                block * up_rows : (block + 1) * up_rows
            ]
        two_grad[...] += dot_nt(grad_pre, w_up[:, columns])


def cross_backward_kernel(
    two_grad,
    first_in,
    second_in,
    norm,
    w_cross,
    w_cross_out,
    queries,
    heads,
    key_values,
    norm_grads_in,
    grad_key_values,
    grad_cross,
    grad_cross_out,
    one_query_grad,
    norm_grads,
    head_grads,
    query_grads,
):
    features = first_in.shape[1]
    items = key_values.shape[0]
    two_query = query_rows(two_grad[...])
    normed, inverse = normalise(second_in[...])
    norm_grads[...] = norm_grads_in[...]
    norm_grads[2:3, :] = jnp.sum(two_query * normed, axis=0, keepdims=True)
    norm_grads[3:4, :] = jnp.sum(two_query, axis=0, keepdims=True)
    second_grad = norm_back(two_query, normed, inverse, norm[2:3, :])
    grad_rows = second_grad.astype(BF16)
    head_grads[...] = dot_nt(grad_rows, w_cross_out[...]).astype(BF16)
    grad_cross_out[...] = dot_tn(heads[...], grad_rows).astype(BF16)
    head_mask = query_head_mask()
    scale = HEAD ** (-0.5)

    @pl.loop(0, items)
    def _(item):
        span = pl.ds(pl.multiple_of(item * QUERIES, QUERIES), QUERIES)
        for begin in range(0, features, WIDE):
            columns = slice(begin, begin + WIDE)
            value_columns = slice(features + begin, features + begin + WIDE)
            expanded = head_rows(queries[span, columns], head_mask)
            expanded_grad = head_rows(head_grads[span, columns], head_mask)
            keys = key_values[item, :, columns]
            probs = softmax(dot_nt(expanded, keys) * scale)
            grad_probs = dot_nt(expanded_grad, key_values[item, :, value_columns])
            inner = jnp.sum(grad_probs * probs, axis=-1, keepdims=True)
            grad_scores = (probs * (grad_probs - inner)).astype(BF16)
            grad_key_values[item, :, value_columns] = dot_tn(
                probs.astype(BF16), expanded_grad
            ).astype(BF16)
            grad_key_values[item, :, columns] = (dot_tn(grad_scores, expanded) * scale).astype(BF16)
            query_grads[span, columns] = (
                fold_heads(dot_nn(grad_scores, keys), head_mask) * scale
            ).astype(BF16)

    normed_one, _ = normalise(query_rows(first_in[...]))
    query_in = (normed_one * norm[0:1, :] + norm[1:2, :]).astype(BF16)
    grad_cross[...] = dot_tn(query_in, query_grads[...]).astype(BF16)
    one_query_grad[...] = second_grad + dot_nt(query_grads[...], w_cross[...])


def image_backward_kernel(
    place, feats, grad_key_values, grad_cross, grad_cross_out, keep, send, total
):
    features = grad_cross.shape[1]
    width = features // MODEL
    image_rows = feats.shape[2] // GROUPS
    half = image_rows // 2
    block_rows = features // GROUPS
    out_rows = width // GROUPS

    @pl.when(pl.program_id(0) == 0)
    def _():
        total[...] = jnp.zeros_like(total)

    total[...] += dot_tn(feats[0], grad_key_values[0])

    @pl.when(pl.program_id(0) == pl.num_programs(0) - 1)
    def _():
        for block in range(GROUPS):
            cross_rows = grad_cross[block * block_rows : (block + 1) * block_rows, :].astype(F32)
            for model in range(MODEL):
                side, y_rel = divmod(model, 2)
                columns = slice(model * width, (model + 1) * width)
                image_part = [
                    total[begin : begin + half, kind + model * width : kind + (model + 1) * width]
                    for begin in (block * image_rows, block * image_rows + half)
                    for kind in (0, features)
                ]
                cross_part = [
                    cross_rows[part * out_rows : (part + 1) * out_rows, columns]
                    for part in range(MODEL)
                ]
                begin = model * width + (block // 2) * 2 * out_rows
                out_part = grad_cross_out[begin : begin + 2 * out_rows, :].astype(F32)
                begin = (block % 2) * out_rows
                (keep, send)[side][slot_of(place, block, y_rel)] = jnp.concatenate(
                    [
                        jnp.concatenate(image_part, axis=1),
                        jnp.concatenate(cross_part, axis=1),
                        out_part[begin : begin + out_rows],
                    ],
                    axis=0,
                ).astype(BF16)


def self_backward_kernel(
    place,
    lengths,
    one_query_grad,
    two_grad,
    first_in,
    norm,
    hidden,
    qkv,
    heads,
    w_qkv,
    w_self_out,
    norm_grads_in,
    input_grad,
    in_keep,
    in_send,
    one_grad,
    head_grads,
    grad_qkv,
    grad_weights,
):
    rows, features = hidden.shape
    items = rows // SEQ
    width = features // MODEL
    block_rows = features // GROUPS
    out_rows = width // GROUPS
    for item in range(items):
        begin = item * SEQ
        one_grad[begin : begin + QUERIES, :] = one_query_grad[
            item * QUERIES : (item + 1) * QUERIES, :
        ]
        one_grad[begin + QUERIES : begin + SEQ, :] = two_grad[begin + QUERIES : begin + SEQ, :]
    normed, inverse = normalise(first_in[...])
    gradient = one_grad[...]
    norm_total = norm_grads_in[...] + jnp.concatenate(
        [
            jnp.sum(gradient * normed, axis=0, keepdims=True),
            jnp.sum(gradient, axis=0, keepdims=True),
            jnp.zeros((NORM_ROWS - 2, features), F32),
        ],
        axis=0,
    )
    first_grad = norm_back(gradient, normed, inverse, norm[0:1, :])
    one_grad[...] = first_grad
    grad_rows = first_grad.astype(BF16)
    head_grads[...] = dot_nt(grad_rows, w_self_out[...]).astype(BF16)
    scale = HEAD ** (-0.5)
    for begin in range(0, rows, BLOCK):
        span = slice(begin, begin + BLOCK)
        mask = block_mask(lengths, begin // SEQ)
        for pair in range(features // (2 * HEAD)):
            results = [[], [], []]
            for head in (2 * pair, 2 * pair + 1):
                queries, key_rows, value_rows = [
                    qkv[span, kind * features + head * HEAD : kind * features + (head + 1) * HEAD]
                    for kind in range(3)
                ]
                head_grad = head_grads[span, head * HEAD : (head + 1) * HEAD]
                probs = softmax(jnp.where(mask, dot_nt(queries, key_rows) * scale, MASK_VALUE))
                grad_probs = dot_nt(head_grad, value_rows)
                inner = jnp.sum(grad_probs * probs, axis=-1, keepdims=True)
                grad_scores = (probs * (grad_probs - inner)).astype(BF16)
                results[0].append((dot_nn(grad_scores, key_rows) * scale).astype(BF16))
                results[1].append((dot_tn(grad_scores, queries) * scale).astype(BF16))
                results[2].append(dot_tn(probs.astype(BF16), head_grad).astype(BF16))
            for kind in range(3):
                first = kind * features + pair * 2 * HEAD
                grad_qkv[span, first : first + 2 * HEAD] = jnp.concatenate(results[kind], axis=1)
    tokens = hidden[...]
    total = one_grad[...]
    for kind in range(3):
        columns = slice(kind * features, (kind + 1) * features)
        total = total + dot_nt(grad_qkv[:, columns], w_qkv[:, columns])
        grad_weights[:, columns] = dot_tn(tokens, grad_qkv[:, columns]).astype(BF16)
    input_grad[...] = total.astype(BF16)
    grad_out = dot_tn(heads[...], grad_rows)
    norm_rows = norm_total.astype(BF16)
    for block in range(GROUPS):
        span = slice(block * block_rows, (block + 1) * block_rows)
        for model in range(MODEL):
            side, y_rel = divmod(model, 2)
            piece = [
                grad_weights[
                    span, kind * features + model * width : kind * features + (model + 1) * width
                ]
                for kind in range(3)
            ]
            begin = model * width + block * out_rows
            out_part = grad_out[begin : begin + out_rows]
            piece.append(
                jnp.concatenate(
                    [out_part[:, part * width : (part + 1) * width] for part in range(MODEL)],
                    axis=0,
                ).astype(BF16)
            )
            target, slot = (in_keep, in_send)[side], slot_of(place, block, y_rel)
            target[slot, :block_rows, :] = jnp.concatenate(piece, axis=1)
            target[slot, block_rows:, :] = norm_rows


SCALARS = pl.BlockSpec(memory_space=pltpu.SMEM)
WHOLE = pl.BlockSpec(memory_space=pltpu.VMEM)


def local_call(kernel, scalars, arrays, out_shapes, scratch, flops, name, limit):
    size = sum(a.size * a.dtype.itemsize for a in arrays)
    size += sum(a.size * a.dtype.itemsize for a in out_shapes)
    return pl.pallas_call(
        kernel,
        out_shape=tuple(out_shapes),
        in_specs=[SCALARS] * len(scalars) + [WHOLE] * len(arrays),
        out_specs=tuple([WHOLE] * len(out_shapes)),
        scratch_shapes=scratch,
        compiler_params=pltpu.CompilerParams(vmem_limit_bytes=limit * MIB),
        cost_estimate=pl.CostEstimate(flops=flops, bytes_accessed=size, transcendentals=0),
        name=name,
    )(*scalars, *arrays)


def shape_of(*dims, dtype=BF16):
    return jax.ShapeDtypeStruct(dims, dtype)


class Direct:
    def __init__(self, dp, mp):
        self.count = dp * mp
        self.mp = mp
        self.depth = dp // 2
        index = lax.axis_index("dp")
        block = jnp.arange(GROUPS, dtype=jnp.int32)
        along_x = (block % 2) ^ (index % 2)
        along_z = (index // 2 - block // 2) % self.depth
        self.place = jnp.concatenate([along_x, along_z]).astype(jnp.int32)

    def hop(self, values, flip):
        return lax.ppermute(values, AXES, [(i, i ^ flip) for i in range(self.count)])

    def hop_core(self, values):
        return self.hop(values, 1)

    def hop_y(self, values):
        return self.hop(values, 2)

    def hop_x(self, values):
        return self.hop(values, self.mp)

    def hop_z(self, values, distance):
        step = 2 * self.mp * distance
        return lax.ppermute(values, AXES, [(i, (i + step) % self.count) for i in range(self.count)])

    def spread_z(self, piece):
        return jnp.stack([piece] + [self.hop_z(piece, step) for step in range(1, self.depth)])


    def spread_first(self, held, split):
        return self.hop_y(held[:, :split]), self.hop_x(held[:, split:])

    def join_first(self, held, split, others):
        return jnp.stack([held[:, :split], others[0]]), jnp.stack([held[:, split:], others[1]])

    def spread_second(self, parts):
        return self.hop_x(parts[0]), self.hop_y(parts[1])

    def join_second(self, parts, others):
        left = jnp.stack([parts[0], others[0]])
        right = jnp.stack([parts[1], others[1]]).transpose(1, 0, 2, 3, 4)
        whole = jnp.concatenate([left, right], axis=3)
        return whole.reshape(SLOTS, *whole.shape[3:])


    def fold_core(self, keep, send):
        return [keep, self.hop_core(send)]

    def fold_first(self, parts, split):
        parts = [part.reshape(2, 2, 4, *part.shape[1:]) for part in parts]
        left = [part[:, :, :, :split] for part in parts]
        right = [part[:, :, :, split:] for part in parts]
        return (
            [part[0] for part in left] + [self.hop_x(total([part[1] for part in left]))],
            [part[:, 0] for part in right] + [self.hop_y(total([part[:, 1] for part in right]))],
        )

    def fold_second(self, parts):
        left, right = parts
        left_other = self.hop_y(total([part[1] for part in left]))
        right_other = self.hop_x(total([part[1] for part in right]))
        return (
            [part[0] for part in left] + [left_other],
            [part[0] for part in right] + [right_other],
        )

    def fold_z(self, parts):
        left, right = parts
        parts = [
            total([part[step] for part in left], [part[step] for part in right])
            for step in range(self.depth)
        ]
        own = jnp.concatenate(
            [total([part[0] for part in side], dtype=F32) for side in (left, right)], axis=0
        )
        return [own] + [self.hop_z(parts[step], -step) for step in range(1, self.depth)]


def total(*sides, dtype=BF16):
    sums = []
    for parts in sides:
        result = parts[0].astype(F32)
        for part in parts[1:]:
            result = result + part.astype(F32)
        sums.append(result.astype(dtype))
    return sums[0] if len(sums) == 1 else jnp.concatenate(sums, axis=0)


class Plain:
    def __init__(self, dp, mp):
        self.dp = dp
        self.mp = mp
        block = jnp.arange(GROUPS, dtype=jnp.int32)
        self.place = jnp.concatenate([block % 2, block // 2]).astype(jnp.int32)

    def collect(self, piece):
        rows, width = piece.shape
        blocks = lax.all_gather(piece, AXES, axis=0).reshape(self.dp, self.mp, rows, width)
        rows = rows * self.dp // GROUPS
        blocks = blocks.transpose(1, 0, 2, 3).reshape(2, 2, 4, 2, rows, width)
        blocks = blocks.transpose(0, 3, 1, 2, 4, 5).reshape(2, SLOTS, rows, width)
        return blocks

    def scatter(self, both):
        rows, width = both.shape[2:]
        both = both.reshape(2, 2, 2, 4, rows, width).transpose(0, 2, 3, 1, 4, 5)
        both = both.reshape(self.mp, self.dp, rows * GROUPS // self.dp, width)
        both = both.transpose(1, 0, 2, 3).reshape(-1, width)
        return lax.psum_scatter(both.astype(F32), AXES, scatter_dimension=0, tiled=True)


def tie(*arrays):
    return lax.optimization_barrier(arrays)


def tie(*arrays):
    return lax.optimization_barrier(arrays)


def add(left_side, right_side):
    return (left_side.astype(F32) + right_side.astype(F32)).astype(BF16)


def self_forward(place, lengths, hidden, begin):
    rows, features = hidden.shape
    return local_call(
        self_forward_kernel,
        (place, lengths),
        (hidden, *begin),
        (
            shape_of(rows, features, dtype=F32),
            shape_of(rows, 3 * features),
            shape_of(rows, features),
            shape_of(features, 3 * features),
            shape_of(features, features),
            shape_of(features, features),
            shape_of(features, features),
            shape_of(NORM_ROWS, features, dtype=F32),
        ),
        [pltpu.VMEM((features, features), F32), pltpu.VMEM((features, features), F32)],
        10 * rows * features * features,
        "self_forward",
        30,
    )


def image_forward(place, feats, image):
    items, patches, encoded = feats.shape
    features = image[0].shape[2] // 2 * MODEL
    piece_spec = pl.BlockSpec(image[0].shape, lambda item, where: (0, 0, 0))
    return pl.pallas_call(
        image_forward_kernel,
        out_shape=shape_of(items, patches, 2 * features),
        grid_spec=pltpu.PrefetchScalarGridSpec(
            num_scalar_prefetch=1,
            grid=(items,),
            in_specs=[
                pl.BlockSpec((1, patches, encoded), lambda item, where: (item, 0, 0)),
                piece_spec,
                piece_spec,
            ],
            out_specs=pl.BlockSpec((1, patches, 2 * features), lambda item, where: (item, 0, 0)),
            scratch_shapes=[pltpu.VMEM((encoded, 2 * features), BF16)],
        ),
        compiler_params=pltpu.CompilerParams(vmem_limit_bytes=24 * MIB),
        cost_estimate=image_cost(items, patches, encoded, features),
        name="image_forward",
    )(place, feats, *image)


def image_cost(items, patches, encoded, features):
    return pl.CostEstimate(
        flops=4 * items * patches * encoded * features,
        bytes_accessed=2 * items * patches * (encoded + 2 * features) + 4 * encoded * features,
        transcendentals=0,
    )


def image_backward(place, feats, grad_key_values, grad_cross, grad_cross_out):
    items, patches, encoded = feats.shape
    features = grad_cross.shape[1]
    rows = encoded // GROUPS // 2 + 2 * (features // MODEL // GROUPS)
    piece = (SLOTS, rows, features)
    square_spec = pl.BlockSpec((features, features), lambda item, where: (0, 0))
    piece_spec = pl.BlockSpec(piece, lambda item, where: (0, 0, 0))
    return pl.pallas_call(
        image_backward_kernel,
        out_shape=(shape_of(*piece), shape_of(*piece)),
        grid_spec=pltpu.PrefetchScalarGridSpec(
            num_scalar_prefetch=1,
            grid=(items,),
            in_specs=[
                pl.BlockSpec((1, patches, encoded), lambda item, where: (item, 0, 0)),
                pl.BlockSpec((1, patches, 2 * features), lambda item, where: (item, 0, 0)),
                square_spec,
                square_spec,
            ],
            out_specs=(piece_spec, piece_spec),
            scratch_shapes=[pltpu.VMEM((encoded, 2 * features), F32)],
        ),
        compiler_params=pltpu.CompilerParams(vmem_limit_bytes=32 * MIB),
        cost_estimate=image_cost(items, patches, encoded, features),
        name="image_backward",
    )(place, feats, grad_key_values, grad_cross, grad_cross_out)


def cross_forward(first_in, norm, w_cross, w_cross_out, key_values):
    features = first_in.shape[1]
    queries = first_in.shape[0] // SEQ * QUERIES
    return local_call(
        cross_forward_kernel,
        (),
        (first_in, norm, w_cross, w_cross_out, key_values),
        (
            shape_of(queries, features, dtype=F32),
            shape_of(queries, features),
            shape_of(queries, features),
        ),
        [],
        4 * queries * features * features,
        "cross_forward",
        18,
    )


def feed(place, lengths, first_in, second_in, norm, out_grad, weights):
    rows, features = first_in.shape
    hidden_width = weights[0].shape[2] * MODEL
    return local_call(
        feed_kernel,
        (place, lengths),
        (first_in, second_in, norm, out_grad, *weights),
        (
            shape_of(rows, features),
            shape_of(rows, features, dtype=F32),
            shape_of(*weights[0].shape),
            shape_of(*weights[0].shape),
            shape_of(NORM_ROWS, features, dtype=F32),
        ),
        [
            pltpu.VMEM((features, hidden_width), BF16),
            pltpu.VMEM((hidden_width, features), BF16),
            pltpu.VMEM((rows, features), F32),
            pltpu.VMEM((rows, hidden_width), F32),
            pltpu.VMEM((rows, hidden_width), BF16),
        ],
        12 * rows * features * hidden_width,
        "feed",
        60,
    )


def cross_backward(two_grad, first_in, second_in, norm, w_cross, w_cross_out, queries, heads, key_values, norm_grads):
    features = first_in.shape[1]
    query_count = queries.shape[0]
    return local_call(
        cross_backward_kernel,
        (),
        (
            two_grad,
            first_in,
            second_in,
            norm,
            w_cross,
            w_cross_out,
            queries,
            heads,
            key_values,
            norm_grads,
        ),
        (
            shape_of(*key_values.shape),
            shape_of(features, features),
            shape_of(features, features),
            shape_of(query_count, features, dtype=F32),
            shape_of(NORM_ROWS, features, dtype=F32),
        ),
        [pltpu.VMEM((query_count, features), BF16), pltpu.VMEM((query_count, features), BF16)],
        8 * query_count * features * features,
        "cross_backward",
        28,
    )


def self_backward(place, lengths, one_query_grad, two_grad, first_in, norm, hidden, qkv, heads, w_qkv, w_self_out, norm_grads):
    rows, features = hidden.shape
    piece = (SLOTS, features // GROUPS + NORM_ROWS, features)
    return local_call(
        self_backward_kernel,
        (place, lengths),
        (
            one_query_grad,
            two_grad,
            first_in,
            norm,
            hidden,
            qkv,
            heads,
            w_qkv,
            w_self_out,
            norm_grads,
        ),
        (shape_of(rows, features), shape_of(*piece), shape_of(*piece)),
        [
            pltpu.VMEM((rows, features), F32),
            pltpu.VMEM((rows, features), BF16),
            pltpu.VMEM((rows, 3 * features), BF16),
            pltpu.VMEM((features, 3 * features), BF16),
        ],
        20 * rows * features * features,
        "self_backward",
        34,
    )


def run_direct(hidden, feats, lengths, out_grad, image, begin, weights):
    moves = Direct(lax.axis_size("dp"), lax.axis_size("mp"))
    place = moves.place
    begin_split = begin.shape[0] // 2
    image_split = image.shape[0] * 96 // 176
    feed_split = weights.shape[0] // 2

    begin = moves.spread_z(begin)
    begin, image = tie(begin, image)
    begin_others = moves.spread_first(begin, begin_split)
    image = moves.spread_z(image)
    begin_others, image, weights = tie(begin_others, image, weights)
    begin_parts = moves.join_first(begin, begin_split, begin_others)
    begin_others = moves.spread_second(begin_parts)
    image_others = moves.spread_first(image, image_split)
    weights = moves.spread_z(weights)
    begin_others, image_others, weights = tie(begin_others, image_others, weights)

    image_parts = moves.join_first(image, image_split, image_others)
    image_others = moves.spread_second(image_parts)
    weight_others = moves.spread_first(weights, feed_split)
    begin = moves.join_second(begin_parts, begin_others)
    begin_other = moves.hop_core(begin)
    first_in, qkv, heads, w_qkv, w_cross, w_self_out, w_cross_out, norm = self_forward(
        place, lengths, hidden, (begin, begin_other)
    )
    first_in, image_others, weight_others = tie(first_in, image_others, weight_others)
    image = moves.join_second(image_parts, image_others)
    weight_parts = moves.join_first(weights, feed_split, weight_others)
    image_other = moves.hop_core(image)
    image_other, weight_parts, first_in = tie(image_other, weight_parts, first_in)
    weight_others = moves.spread_second(weight_parts)
    key_values = image_forward(place, feats, (image, image_other))
    second_in, cross_queries, cross_heads = cross_forward(
        first_in, norm, w_cross, w_cross_out, key_values
    )
    second_in, weight_others = tie(second_in, weight_others)
    weights = moves.join_second(weight_parts, weight_others)
    weights_other = moves.hop_core(weights)
    block_out, two_grad, feed_keep, feed_send, norm_grads = feed(
        place, lengths, first_in, second_in, norm, out_grad, (weights, weights_other)
    )

    feed_sums = moves.fold_core(feed_keep, feed_send)
    grad_key_values, grad_cross, grad_cross_out, one_query_grad, norm_grads = cross_backward(
        two_grad,
        first_in,
        second_in,
        norm,
        w_cross,
        w_cross_out,
        cross_queries,
        cross_heads,
        key_values,
        norm_grads,
    )
    grad_key_values, feed_sums = tie(grad_key_values, feed_sums)
    feed_sums = moves.fold_first(feed_sums, feed_split)
    image_keep, image_send = image_backward(
        place, feats, grad_key_values, grad_cross, grad_cross_out
    )
    one_query_grad, image_keep, image_send, feed_sums = tie(
        one_query_grad, image_keep, image_send, feed_sums
    )
    image_sums = moves.fold_core(image_keep, image_send)
    one_query_grad, image_sums = tie(one_query_grad, image_sums)
    image_sums = moves.fold_first(image_sums, 64)
    feed_sums = moves.fold_second(feed_sums)
    input_grad, in_keep, in_send = self_backward(
        place,
        lengths,
        one_query_grad,
        two_grad,
        first_in,
        norm,
        hidden,
        qkv,
        heads,
        w_qkv,
        w_self_out,
        norm_grads,
    )
    in_keep, in_send, feed_sums, image_sums = tie(in_keep, in_send, feed_sums, image_sums)
    in_sums = moves.fold_core(in_keep, in_send)
    feed_sums = moves.fold_z(feed_sums)
    image_sums = moves.fold_second(image_sums)
    in_sums, image_sums = tie(in_sums, image_sums)
    in_sums = moves.fold_first(in_sums, 48)
    in_sums, feed_sums, image_sums = tie(in_sums, feed_sums, image_sums)
    image_sums = moves.fold_z(image_sums)
    in_sums = moves.fold_second(in_sums)
    feed_sum = total(feed_sums, dtype=F32)
    in_sums, image_sums = tie(in_sums, image_sums)
    in_sum = total(moves.fold_z(in_sums), dtype=F32)
    image_sum = total(image_sums, dtype=F32)
    return block_out, input_grad, in_sum, image_sum, feed_sum


def run_plain(hidden, feats, lengths, out_grad, image, begin, weights):
    moves = Plain(lax.axis_size("dp"), lax.axis_size("mp"))
    place = moves.place
    features = hidden.shape[1]
    width = features // MODEL
    block_rows, out_rows = features // GROUPS, width // GROUPS
    own_in, own_out = block_rows * GROUPS // moves.dp, out_rows * GROUPS // moves.dp
    half = block_rows // 2
    part = begin.shape[0] - NORM_ROWS
    inward = moves.collect(begin[:own_in])
    cross_out = moves.collect(begin[own_in : own_in + own_out])
    self_out = moves.collect(begin[own_in + own_out : part])
    norm_all = lax.psum(begin[part:].astype(F32), AXES).astype(BF16)
    norm_first = jnp.zeros((2, SLOTS, NORM_ROWS, features), BF16).at[0, 0].set(norm_all)
    begin = jnp.concatenate(
        [
            inward[:, :, :half],
            cross_out,
            jnp.zeros_like(norm_first),
            inward[:, :, half:],
            self_out,
            norm_first,
        ],
        axis=2,
    )
    image = moves.collect(image)
    own_up = weights.shape[0] // 2
    weights = jnp.concatenate(
        [moves.collect(weights[:own_up]), moves.collect(weights[own_up:])], axis=2
    )
    first_in, qkv, heads, w_qkv, w_cross, w_self_out, w_cross_out, norm = self_forward(
        place, lengths, hidden, (begin[0], begin[1])
    )
    key_values = image_forward(place, feats, (image[0], image[1]))
    second_in, cross_queries, cross_heads = cross_forward(
        first_in, norm, w_cross, w_cross_out, key_values
    )
    block_out, two_grad, feed_keep, feed_send, norm_grads = feed(
        place, lengths, first_in, second_in, norm, out_grad, (weights[0], weights[1])
    )
    grad_key_values, grad_cross, grad_cross_out, one_query_grad, norm_grads = cross_backward(
        two_grad,
        first_in,
        second_in,
        norm,
        w_cross,
        w_cross_out,
        cross_queries,
        cross_heads,
        key_values,
        norm_grads,
    )
    image_keep, image_send = image_backward(
        place, feats, grad_key_values, grad_cross, grad_cross_out
    )
    input_grad, in_keep, in_send = self_backward(
        place,
        lengths,
        one_query_grad,
        two_grad,
        first_in,
        norm,
        hidden,
        qkv,
        heads,
        w_qkv,
        w_self_out,
        norm_grads,
    )

    def beside(values):
        count = values.shape[-2] // MODEL
        return jnp.concatenate(
            [values[..., part * count : (part + 1) * count, :] for part in range(MODEL)], axis=-1
        )

    def below(values):
        count = values.shape[-1] // MODEL
        return jnp.concatenate(
            [values[..., part * count : (part + 1) * count] for part in range(MODEL)], axis=-2
        )

    grads = jnp.stack([in_keep, in_send])
    in_part = moves.scatter(grads[:, :, :block_rows, : 3 * width])
    self_out = moves.scatter(beside(grads[:, :, :block_rows, 3 * width :]))
    norm_sum = lax.psum(in_keep[0, block_rows:].astype(F32), AXES)
    in_sum = jnp.concatenate([jnp.concatenate([in_part, below(self_out)], axis=1), norm_sum])
    grads = jnp.stack([image_keep, image_send])
    image_rows = grads.shape[2] - 2 * out_rows
    image_part = grads[:, :, :image_rows]
    image_part = jnp.concatenate(
        [image_part[..., : features // 2], image_part[..., features // 2 :]], axis=2
    )
    image_part = moves.scatter(image_part)
    image_half = image_part.shape[0] // 2
    image_part = jnp.concatenate([image_part[:image_half], image_part[image_half:]], axis=1)
    cross_query = moves.scatter(below(grads[:, :, image_rows : image_rows + out_rows]))
    cross_out = moves.scatter(grads[:, :, image_rows + out_rows :])
    image_sum = jnp.concatenate([image_part, beside(cross_query), cross_out])
    grads = jnp.stack([feed_keep, feed_send])
    feed_half = grads.shape[2] // 2
    feed_sum = jnp.concatenate(
        [moves.scatter(grads[:, :, :feed_half]), moves.scatter(grads[:, :, feed_half:])]
    )
    return block_out, input_grad, in_sum, image_sum, feed_sum


def adam_step(weight, moments, gradient, decay_rate):
    moment_one = BETA_ONE * moments[0] + (1.0 - BETA_ONE) * gradient
    moment_two = BETA_TWO * moments[1] + (1.0 - BETA_TWO) * gradient * gradient
    update = (
        moment_one
        / (1.0 - BETA_ONE**STEP)
        / (jnp.sqrt(moment_two / (1.0 - BETA_TWO**STEP)) + ADAM_EPSILON)
        + decay_rate * weight
    )
    return (moment_one, moment_two, update)


def tensor_squares(values, per_slice):
    if per_slice:
        return jnp.sum(values * values, axis=tuple(range(1, values.ndim)))
    return jnp.sum(values * values)[None]


def per_device(
    hidden_in,
    image_feats,
    caption_lengths,
    out_grad,
    proj_in,
    proj_in_moments,
    proj_in_average,
    proj_out,
    proj_out_moments,
    proj_out_average,
    image_kv,
    image_kv_moments,
    image_kv_average,
    feed_up,
    feed_up_moments,
    feed_up_average,
    feed_down,
    feed_down_moments,
    feed_down_average,
    norm_params,
    norm_params_moments,
    norm_params_average,
):
    data_ways, model_ways = lax.axis_size("dp"), lax.axis_size("mp")
    data_index, model_index = lax.axis_index("dp"), lax.axis_index("mp")
    rows, features = hidden_in.shape
    items = rows // SEQ
    width = features // model_ways
    own_norm = norm_params.shape[1]
    norm_begin = (model_index * data_ways + data_index) * own_norm
    lengths = lax.dynamic_slice_in_dim(caption_lengths, model_index * items, items, 0)
    feats = lax.dynamic_slice_in_dim(image_feats, model_index * items, items, 0)
    image_piece = jnp.concatenate([image_kv[0], image_kv[1]], axis=1).astype(BF16)
    in_piece = jnp.concatenate([proj_in[kind] for kind in range(4)], axis=1).astype(BF16)
    out_pieces = [proj_out[kind].astype(BF16) for kind in range(2)]
    feed_piece = jnp.concatenate([feed_up, feed_down], axis=0).astype(BF16)
    norm_rows = lax.dynamic_update_slice(
        jnp.zeros((NORM_ROWS, features), F32), norm_params, (0, norm_begin)
    ).astype(BF16)
    own_in, own_out, own_image = proj_in.shape[1], proj_out.shape[1], image_kv.shape[1]
    direct = data_ways == GROUPS and model_ways == MODEL
    if direct:
        run, half = run_direct, own_in // 2
        begin_piece = jnp.concatenate(
            [
                in_piece[:half],
                out_pieces[1],
                jnp.zeros_like(norm_rows),
                in_piece[half:],
                out_pieces[0],
                norm_rows,
            ],
            axis=0,
        )
    else:
        run = run_plain
        begin_piece = jnp.concatenate(
            [in_piece, out_pieces[1], out_pieces[0], norm_rows], axis=0
        )
    block_out, input_grad, in_sum, image_sum, feed_sum = run(
        hidden_in, feats, lengths, out_grad, image_piece, begin_piece, feed_piece
    )
    half = own_image // 2
    image_shard = jnp.stack(
        [
            jnp.concatenate(
                [
                    image_sum[:half, (2 * part + kind) * width : (2 * part + kind + 1) * width]
                    for part in range(2)
                ],
                axis=0,
            )
            for kind in range(2)
        ]
    )
    cross_query = image_sum[half : half + own_out]
    in_shard = jnp.stack(
        [in_sum[:own_in, kind * width : (kind + 1) * width] for kind in range(3)]
        + [
            jnp.concatenate(
                [cross_query[:, part * width : (part + 1) * width] for part in range(MODEL)],
                axis=0,
            )
        ]
    )
    self_out = jnp.concatenate(
        [in_sum[part * own_out : (part + 1) * own_out, 3 * width :] for part in range(MODEL)],
        axis=1,
    )
    out_shard = jnp.stack([self_out, image_sum[half + own_out :]])
    up_shard, down_shard = feed_sum[: feed_up.shape[0]], feed_sum[feed_up.shape[0] :]
    norm_shard = lax.dynamic_slice(in_sum[own_in:], (0, norm_begin), norm_params.shape)

    groups = [
        (proj_in, proj_in_moments, proj_in_average, in_shard, DECAY_RATE, True),
        (proj_out, proj_out_moments, proj_out_average, out_shard, DECAY_RATE, True),
        (image_kv, image_kv_moments, image_kv_average, image_shard, DECAY_RATE, True),
        (feed_up, feed_up_moments, feed_up_average, up_shard, DECAY_RATE, False),
        (feed_down, feed_down_moments, feed_down_average, down_shard, DECAY_RATE, False),
        (norm_params, norm_params_moments, norm_params_average, norm_shard, 0.0, True),
    ]
    updates = []
    weight_squares = []
    update_squares = []
    for weight, moments, average, gradient, decay_rate, per_slice in groups:
        moment_one, moment_two, update = adam_step(weight, moments, gradient, decay_rate)
        updates.append((moment_one, moment_two, update))
        weight_squares.append(tensor_squares(weight, per_slice))
        update_squares.append(tensor_squares(update, per_slice))
    own_squares = jnp.stack([jnp.concatenate(weight_squares), jnp.concatenate(update_squares)])
    ways = data_ways * model_ways
    copies = jnp.broadcast_to(own_squares[None], (ways,) + own_squares.shape)
    squares = jnp.sum(lax.all_to_all(copies, AXES, 0, 0, tiled=True), axis=0)
    trust = jnp.sqrt(squares[0]) * lax.rsqrt(squares[1] + SQUARE_EPSILON)
    outputs = []
    offset = 0
    for group, stepped in zip(groups, updates):
        weight, moments, average, gradient, decay_rate, per_slice = group
        moment_one, moment_two, update = stepped
        slices = weight.shape[0] if per_slice else 1
        trust_part = trust[offset : offset + slices]
        if per_slice:
            trust_part = trust_part.reshape((slices,) + (1,) * (weight.ndim - 1))
        else:
            trust_part = trust_part[0]
        new_weight = weight - LEARN_RATE * trust_part * update
        outputs.append(new_weight)
        outputs.append(jnp.stack([moment_one, moment_two]))
        outputs.append(AVERAGE_RATE * average + (1.0 - AVERAGE_RATE) * new_weight)
        offset += slices
    return (block_out, input_grad, *outputs, trust, jnp.sqrt(squares))


def solution(mesh):
    rows = P(AXES, None)
    by_column = P(None, "dp", "mp")
    by_row = P(None, ("mp", "dp"), None)
    weights = (
        by_column,
        P(None, None, "dp", "mp"),
        by_column,
        by_row,
        P(None, None, ("mp", "dp"), None),
        by_row,
        by_column,
        P(None, None, "dp", "mp"),
        by_column,
        P("dp", "mp"),
        P(None, "dp", "mp"),
        P("dp", "mp"),
        P(("mp", "dp"), None),
        P(None, ("mp", "dp"), None),
        P(("mp", "dp"), None),
        P(None, ("mp", "dp")),
        P(None, None, ("mp", "dp")),
        P(None, ("mp", "dp")),
    )
    return jax.shard_map(
        per_device,
        mesh=mesh,
        in_specs=(rows, P("dp", None, None), P("dp"), rows, *weights),
        out_specs=(rows, rows, *weights, P(), P()),
        check_vma=False,
    )
```

```python
import functools

import jax
import jax.numpy as jnp
from jax import lax
from jax.experimental import pallas as pl
from jax.experimental.pallas import tpu as pltpu
from jax.sharding import PartitionSpec as P

HEAD = 64
PATCHES = 257
QUERIES = 32
TEXT = 32
SEQ = QUERIES + TEXT
STEP = 10


NORM_EPSILON = 1e-06
ADAM_EPSILON = 1e-06
SQUARE_EPSILON = 1e-06
BETA_ONE = 0.9
BETA_TWO = 0.999
LEARN_RATE = 0.5
DECAY_RATE = 0.01
AVERAGE_RATE = 0.6
MASK_VALUE = -1e30

AXES = ("dp", "mp")
GROUPS = 8
MODEL = 4
SLOTS = 16
NORM_ROWS = 8
LANES = 128
IMAGE_SPLIT = 64
SELF_SPLIT = 48
BLOCK = 256
WIDE = 256
SLOT = 272
MIB = 1024 * 1024

BF16 = jnp.bfloat16
F32 = jnp.float32


def dot_nn(left_side, right_side):
    return lax.dot_general(
        left_side, right_side, (((1,), (0,)), ((), ())), preferred_element_type=F32
    )


def dot_nt(left_side, right_side):
    return lax.dot_general(
        left_side, right_side, (((1,), (1,)), ((), ())), preferred_element_type=F32
    )


def dot_tn(left_side, right_side):
    return lax.dot_general(
        left_side, right_side, (((0,), (0,)), ((), ())), preferred_element_type=F32
    )


def normalise(inputs):
    centred = inputs - jnp.mean(inputs, axis=-1, keepdims=True)
    inverse = lax.rsqrt(jnp.mean(centred * centred, axis=-1, keepdims=True) + NORM_EPSILON)
    return centred * inverse, inverse


def norm_back(gradient, normed, inverse, gain):
    scaled = gradient * gain
    centre_term = jnp.mean(scaled, axis=-1, keepdims=True)
    normed_term = jnp.mean(scaled * normed, axis=-1, keepdims=True)
    return inverse * (scaled - centre_term - normed * normed_term)


def slot_of(place, block, y_rel):
    return place[block] * 8 + y_rel * 4 + place[GROUPS + block]


def softmax(scores):
    exponents = jnp.exp(scores - jnp.max(scores, axis=-1, keepdims=True))
    return exponents / jnp.sum(exponents, axis=-1, keepdims=True)


def block_mask(lengths, first_item):
    per_block = BLOCK // SEQ
    row = lax.broadcasted_iota(jnp.int32, (BLOCK, BLOCK), 0)
    column = lax.broadcasted_iota(jnp.int32, (BLOCK, BLOCK), 1)
    row_item, column_item = lax.shift_right_logical(row, 6), lax.shift_right_logical(column, 6)
    slot = column - column_item * SEQ
    limit = jnp.zeros((BLOCK, BLOCK), jnp.int32)
    for item in range(per_block):
        limit = jnp.where(column_item == item, lengths[first_item + item] + QUERIES, limit)
    return (row_item == column_item) & (slot < limit)


def self_forward_kernel(
    place,
    lengths,
    hidden,
    begin_own,
    begin_other,
    first_in,
    qkv,
    heads,
    w_qkv,
    w_cross,
    w_self_out,
    w_cross_out,
    norm,
    self_rows,
    cross_rows,
):
    rows, features = hidden.shape
    width = features // MODEL
    block_rows = features // GROUPS
    out_rows = width // GROUPS
    half, part = block_rows // 2, begin_own.shape[1] // 2
    norm_sum = jnp.zeros((NORM_ROWS, features), F32)
    for block in range(GROUPS):
        pieces = []
        for model in range(MODEL):
            side, y_rel = divmod(model, 2)
            source, slot = (begin_own, begin_other)[side], slot_of(place, block, y_rel)
            pieces.append(
                jnp.concatenate(
                    [source[slot, :half, :], source[slot, part : part + half, :]], axis=0
                )
            )
            cross_part = source[slot, half:part, :].astype(F32)
            self_part = source[slot, part + half :, :].astype(F32)
            begin = model * width + block * out_rows
            cross_rows[begin : begin + out_rows, :] = cross_part[:out_rows]
            self_rows[begin : begin + out_rows, :] = self_part[:out_rows]
            norm_sum = norm_sum + self_part[out_rows:]
        begin = block * block_rows
        for kind in range(4):
            joined = jnp.concatenate(
                [piece[:, kind * width : (kind + 1) * width] for piece in pieces], axis=1
            )
            if kind < 3:
                w_qkv[begin : begin + block_rows, kind * features : (kind + 1) * features] = joined
            else:
                w_cross[begin : begin + block_rows, :] = joined
    norm[...] = norm_sum
    w_self_out[...] = self_rows[...].astype(BF16)
    w_cross_out[...] = cross_rows[...].astype(BF16)
    tokens = hidden[...]
    for kind in range(3):
        columns = slice(kind * features, (kind + 1) * features)
        qkv[:, columns] = dot_nn(tokens, w_qkv[:, columns]).astype(BF16)
    scale = HEAD ** (-0.5)
    for begin in range(0, rows, BLOCK):
        span = slice(begin, begin + BLOCK)
        mask = block_mask(lengths, begin // SEQ)
        for pair in range(features // (2 * HEAD)):
            results = []
            for head in (2 * pair, 2 * pair + 1):
                parts = [
                    qkv[span, kind * features + head * HEAD : kind * features + (head + 1) * HEAD]
                    for kind in range(3)
                ]
                scores = jnp.where(mask, dot_nt(parts[0], parts[1]) * scale, MASK_VALUE)
                results.append(dot_nn(softmax(scores).astype(BF16), parts[2]).astype(BF16))
            heads[span, pair * 2 * HEAD : (pair + 1) * 2 * HEAD] = jnp.concatenate(results, axis=1)
    first_in[...] = tokens.astype(F32) + dot_nn(heads[...], w_self_out[...])


def assemble_image(place, image_own, image_other, weight):
    block_rows = image_own.shape[1]
    width = image_own.shape[2] // 2
    features = width * MODEL
    for block in range(GROUPS):
        pieces = []
        for model in range(MODEL):
            side, y_rel = divmod(model, 2)
            pieces.append((image_own, image_other)[side][slot_of(place, block, y_rel)])
        begin = block * block_rows
        for kind in range(2):
            weight[begin : begin + block_rows, kind * features : (kind + 1) * features] = (
                jnp.concatenate(
                    [piece[:, kind * width : (kind + 1) * width] for piece in pieces], axis=1
                )
            )


def image_forward_kernel(place, feats, image_own, image_other, key_values, weight):
    @pl.when(pl.program_id(0) == 0)
    def _():
        assemble_image(place, image_own, image_other, weight)

    patches = feats.shape[1]
    key_values[:patches, :] = dot_nn(feats[0], weight[...]).astype(BF16)
    key_values[patches:, :] = jnp.zeros((SLOT - patches, weight.shape[1]), BF16)


def head_rows(values, head_mask):
    stacked = jnp.concatenate([values] * (WIDE // HEAD), axis=0)
    return jnp.where(head_mask, stacked, jnp.zeros_like(stacked))


def fold_heads(values, head_mask):
    kept = jnp.where(head_mask, values, 0.0)
    count = WIDE // HEAD
    size = values.shape[0] // count
    total = kept[:size]
    for index in range(1, count):
        total = total + kept[index * size : (index + 1) * size]
    return total


def query_head_mask():
    shape = (QUERIES * (WIDE // HEAD), WIDE)
    row = lax.broadcasted_iota(jnp.int32, shape, 0)
    column = lax.broadcasted_iota(jnp.int32, shape, 1)
    return lax.shift_right_logical(row, 5) == lax.shift_right_logical(column, 6)


def patch_softmax(queries, keys):
    scores = dot_nt(queries, keys) * HEAD ** (-0.5)
    column = lax.broadcasted_iota(jnp.int32, scores.shape, 1)
    return softmax(jnp.where(column < PATCHES, scores, MASK_VALUE))


def query_rows(values):
    items = values.shape[0] // SEQ
    return jnp.concatenate(
        [values[item * SEQ : item * SEQ + QUERIES] for item in range(items)], axis=0
    )


def cross_forward_kernel(first_in, norm, w_cross, w_cross_out, key_values, second_in, queries, heads):
    features = first_in.shape[1]
    items = key_values.shape[0] // SLOT
    normed, _ = normalise(query_rows(first_in[...]))
    one_query = normed * norm[0:1, :] + norm[1:2, :]
    queries[...] = dot_nn(one_query.astype(BF16), w_cross[...]).astype(BF16)
    head_mask = query_head_mask()

    @pl.loop(0, items)
    def _(item):
        span = pl.ds(pl.multiple_of(item * QUERIES, QUERIES), QUERIES)
        rows = pl.ds(pl.multiple_of(item * SLOT, 16), SLOT)
        for begin in range(0, features, WIDE):
            columns = slice(begin, begin + WIDE)
            value_columns = slice(features + begin, features + begin + WIDE)
            probs = patch_softmax(head_rows(queries[span, columns], head_mask), key_values[rows, columns])
            mixed = dot_nn(probs.astype(BF16), key_values[rows, value_columns])
            heads[span, columns] = fold_heads(mixed, head_mask).astype(BF16)

    second_in[...] = one_query + dot_nn(heads[...], w_cross_out[...])


def gelu_cumulative(inputs):
    return 0.5 * (1.0 + lax.erf(inputs * 0.7071067811865476))


def feed_kernel(
    place,
    lengths,
    first_in,
    second_in,
    norm,
    out_grad,
    feed_own,
    feed_other,
    block_out,
    two_grad,
    keep,
    send,
    norm_grads,
    w_up,
    w_down,
    two_rows,
    pre_act,
    up_sem,
    down_sem,
):
    rows, features = first_in.shape
    items = rows // SEQ
    hidden_width = feed_own.shape[2]
    piece_rows = feed_own.shape[1] // 2
    half = 2 * hidden_width
    for model in range(MODEL):
        side, y_rel = divmod(model, 2)
        source = (feed_own, feed_other)[side]
        for block in range(GROUPS):
            slot = slot_of(place, block, y_rel)
            pltpu.make_async_copy(
                source.at[slot, :piece_rows, :],
                w_up.at[model, pl.ds(block * piece_rows, piece_rows), :],
                up_sem.at[model],
            ).start()
            pltpu.make_async_copy(
                source.at[slot, piece_rows:, :],
                w_down.at[model, pl.ds(block * piece_rows, piece_rows), :],
                down_sem.at[model],
            ).start()
    normed_one, _ = normalise(first_in[...])
    after_one = normed_one * norm[0:1, :] + norm[1:2, :]
    normed_two, _ = normalise(second_in[...])
    after_two = normed_two * norm[2:3, :] + norm[3:4, :]
    for item in range(items):
        begin = item * SEQ
        two_rows[begin : begin + QUERIES, :] = after_two[item * QUERIES : (item + 1) * QUERIES]
        two_rows[begin + QUERIES : begin + SEQ, :] = after_one[begin + QUERIES : begin + SEQ]
    feed_in = two_rows[...].astype(BF16)
    send[:, 2 * half : 2 * half + features] = feed_in
    third_in = two_rows[...]
    for model in range(MODEL):
        target, y_rel = (keep, send)[model // 2], model % 2
        pltpu.make_async_copy(w_up.at[model], w_up.at[model], up_sem.at[model]).wait()
        pre = dot_nn(feed_in, w_up[model])
        pre_act[:, model * hidden_width : (model + 1) * hidden_width] = pre
        act = (pre * gelu_cumulative(pre)).astype(BF16)
        target[:, y_rel * hidden_width : (y_rel + 1) * hidden_width] = act
        pltpu.make_async_copy(w_down.at[model], w_down.at[model], down_sem.at[model]).wait()
        third_in = third_in + dot_nn(act, w_down[model])
    normed, inverse = normalise(third_in)
    block_out[...] = (normed * norm[4:5, :] + norm[5:6, :]).astype(BF16)
    position = lax.broadcasted_iota(jnp.int32, (SEQ, features), 0)
    slope = jnp.concatenate(
        [
            jnp.where(
                position < lengths[item] + QUERIES,
                out_grad[item * SEQ : (item + 1) * SEQ, :].astype(F32),
                0.0,
            )
            for item in range(items)
        ],
        axis=0,
    )
    norm_grads[...] = jnp.zeros_like(norm_grads)
    norm_grads[4:5, :] = jnp.sum(slope * normed, axis=0, keepdims=True)
    norm_grads[5:6, :] = jnp.sum(slope, axis=0, keepdims=True)
    third_grad = norm_back(slope, normed, inverse, norm[4:5, :])
    grad_rows = third_grad.astype(BF16)
    send[:, 2 * half + features :] = grad_rows
    total = third_grad
    for model in range(MODEL):
        target, y_rel = (keep, send)[model // 2], model % 2
        pre = pre_act[:, model * hidden_width : (model + 1) * hidden_width]
        density = jnp.exp(-0.5 * pre * pre) * 0.3989422804014327
        slope_part = gelu_cumulative(pre) + pre * density
        grad_pre = (dot_nt(grad_rows, w_down[model]) * slope_part).astype(BF16)
        target[:, half + y_rel * hidden_width : half + (y_rel + 1) * hidden_width] = grad_pre
        total = total + dot_nt(grad_pre, w_up[model])
    two_grad[...] = total


def put_left(place, block, y_rel, keep, send, value):
    for along_x, target in ((0, keep), (1, send)):

        @pl.when(place[block] == along_x)
        def _(target=target):
            target[y_rel, place[GROUPS + block]] = value


def put_right(place, block, y_rel, keep, send, value):
    (keep, send)[y_rel][place[block], place[GROUPS + block]] = value


def feed_grad_kernel(
    place, hidden, rows, hidden_other, rows_other, left_keep, left_send, right_keep, right_send
):
    piece_rows = left_keep.shape[2]
    kind, y_step = pl.program_id(0), pl.program_id(1)

    @pl.when(kind == 0)
    def _():
        grad_up = dot_tn(rows[...], hidden[...])
        grad_up = (grad_up + dot_tn(rows_other[...], hidden_other[...])).astype(BF16)
        for block in range(GROUPS):
            span = slice(block * piece_rows, (block + 1) * piece_rows)
            put_left(place, block, y_step, left_keep, left_send, grad_up[span])

    for y_rel in range(2):

        @pl.when((kind == 1) & (y_step == y_rel))
        def _(y_rel=y_rel):
            grad_down = dot_tn(hidden[...], rows[...])
            grad_down = (grad_down + dot_tn(hidden_other[...], rows_other[...])).astype(BF16)
            for block in range(GROUPS):
                span = slice(block * piece_rows, (block + 1) * piece_rows)
                put_right(place, block, y_rel, right_keep, right_send, grad_down[span])


def cross_backward_kernel(
    two_grad,
    first_in,
    second_in,
    norm,
    w_cross,
    w_cross_out,
    queries,
    heads,
    key_values,
    norm_grads_in,
    keep,
    send,
    one_query_grad,
    norm_grads,
    head_grads,
    query_grads,
    grad_rows,
):
    features = first_in.shape[1]
    half = features // 2
    count = queries.shape[0]
    step = pl.program_id(0)
    items = pl.num_programs(0) - 3
    scale = HEAD ** (-0.5)

    @pl.when(step == 0)
    def _():
        two_query = query_rows(two_grad[...])
        normed, inverse = normalise(second_in[...])
        norm_grads[...] = norm_grads_in[...]
        norm_grads[2:3, :] = jnp.sum(two_query * normed, axis=0, keepdims=True)
        norm_grads[3:4, :] = jnp.sum(two_query, axis=0, keepdims=True)
        second_grad = norm_back(two_query, normed, inverse, norm[2:3, :])
        one_query_grad[...] = second_grad
        grad_rows[...] = second_grad.astype(BF16)
        head_grads[...] = dot_nt(grad_rows[...], w_cross_out[...]).astype(BF16)

    @pl.when(step < items)
    def _():
        head_mask = query_head_mask()
        span = pl.ds(pl.multiple_of(step * QUERIES, QUERIES), QUERIES)
        for begin in range(0, features, WIDE):
            columns = slice(begin, begin + WIDE)
            value_columns = slice(features + begin, features + begin + WIDE)
            expanded = head_rows(queries[span, columns], head_mask)
            expanded_grad = head_rows(head_grads[span, columns], head_mask)
            keys = key_values[:, columns]
            probs = patch_softmax(expanded, keys)
            grad_probs = dot_nt(expanded_grad, key_values[:, value_columns])
            inner = jnp.sum(grad_probs * probs, axis=-1, keepdims=True)
            grad_scores = (probs * (grad_probs - inner)).astype(BF16)
            grad_values = dot_tn(probs.astype(BF16), expanded_grad).astype(BF16)
            grad_keys = (dot_tn(grad_scores, expanded) * scale).astype(BF16)
            query_grads[span, columns] = (
                fold_heads(dot_nn(grad_scores, keys), head_mask) * scale
            ).astype(BF16)
            for part in range(0, WIDE, WIDE // 2):
                side, place_at = divmod(begin + part, half)
                target, lanes = (keep, send)[side], slice(part, part + WIDE // 2)
                target[:, place_at : place_at + WIDE // 2] = grad_keys[:, lanes]
                place_at += half
                target[:, place_at : place_at + WIDE // 2] = grad_values[:, lanes]

    @pl.when(step >= items)
    def _():
        for target in (keep, send):
            target[count:, :] = jnp.zeros((SLOT - count, features), BF16)

    @pl.when(step == items)
    def _():
        normed_one, _ = normalise(query_rows(first_in[...]))
        query_in = (normed_one * norm[0:1, :] + norm[1:2, :]).astype(BF16)
        for target in (keep, send):
            target[:count, :] = query_in

    @pl.when(step == items + 1)
    def _():
        for target in (keep, send):
            target[:count, :] = grad_rows[...]

    @pl.when(step == items + 2)
    def _():
        for side, target in enumerate((keep, send)):
            columns = slice(side * half, (side + 1) * half)
            target[:count, :half] = query_grads[:, columns]
            target[:count, half:] = heads[:, columns]
        one_query_grad[...] += dot_nt(query_grads[...], w_cross[...])


def image_grad_kernel(
    count,
    place,
    feats,
    keep_rows,
    other_rows,
    keep,
    other,
    left_keep,
    left_send,
    right_keep,
    right_send,
    total,
    spread,
):
    features = keep.shape[1]
    half = features // 2
    width = half // 2
    image_rows = feats.shape[2] // GROUPS
    image_half = image_rows // 2
    block_rows = features // GROUPS
    out_rows = width // GROUPS
    split = left_keep.shape[2]
    step, steps = pl.program_id(0), pl.num_programs(0)

    @pl.when(step == 0)
    def _():
        spread[...] = jnp.zeros_like(spread)

    for item in range(feats.shape[0]):
        spread[item * SLOT : item * SLOT + feats.shape[1], :] = feats[item]

    @pl.when(step == 0)
    def _():
        total[...] = dot_tn(spread[...], keep_rows[...])

    @pl.when((step > 0) & (step < steps // 2))
    def _():
        total[...] += dot_tn(spread[...], keep_rows[...])

    @pl.when(step >= steps // 2)
    def _():
        total[...] += dot_tn(spread[...], other_rows[...])

    @pl.when(step == steps - 1)
    def _():
        inputs, slopes = slice(0, count), slice(SLOT, SLOT + count)
        parts = slice(2 * SLOT, 2 * SLOT + count)
        grad_query = dot_tn(keep[inputs, :], keep[parts, :half]) + dot_tn(
            other[inputs, :], other[parts, :half]
        )
        grad_out = dot_tn(keep[parts, half:], keep[slopes, :]) + dot_tn(
            other[parts, half:], other[slopes, :]
        )
        for block in range(GROUPS):
            for y_rel in range(2):
                columns = slice(y_rel * width, (y_rel + 1) * width)
                image_part = [
                    total[
                        begin : begin + image_half,
                        kind + y_rel * width : kind + (y_rel + 1) * width,
                    ]
                    for begin in (block * image_rows, block * image_rows + image_half)
                    for kind in (0, half)
                ]
                begin = block * block_rows
                cross_part = [
                    grad_query[begin + part * out_rows : begin + (part + 1) * out_rows, columns]
                    for part in range(MODEL)
                ]
                begin = y_rel * width + block * out_rows
                piece = jnp.concatenate(
                    [
                        jnp.concatenate(image_part, axis=1),
                        jnp.concatenate(cross_part, axis=1),
                        grad_out[begin : begin + out_rows],
                    ],
                    axis=0,
                )
                put_left(place, block, y_rel, left_keep, left_send, piece[:split].astype(BF16))
                put_right(place, block, y_rel, right_keep, right_send, piece[split:].astype(BF16))


def self_backward_kernel(
    lengths,
    one_query_grad,
    two_grad,
    first_in,
    norm,
    hidden,
    qkv,
    heads,
    w_qkv,
    w_self_out,
    norm_grads_in,
    input_grad,
    keep,
    send,
    norm_total,
    one_grad,
    head_grads,
    grad_qkv,
):
    rows, features = hidden.shape
    items = rows // SEQ
    half = features // 2
    for item in range(items):
        begin = item * SEQ
        one_grad[begin : begin + QUERIES, :] = one_query_grad[
            item * QUERIES : (item + 1) * QUERIES, :
        ]
        one_grad[begin + QUERIES : begin + SEQ, :] = two_grad[begin + QUERIES : begin + SEQ, :]
    normed, inverse = normalise(first_in[...])
    gradient = one_grad[...]
    norm_sum = norm_grads_in[...] + jnp.concatenate(
        [
            jnp.sum(gradient * normed, axis=0, keepdims=True),
            jnp.sum(gradient, axis=0, keepdims=True),
            jnp.zeros((NORM_ROWS - 2, features), F32),
        ],
        axis=0,
    )
    norm_total[...] = norm_sum
    first_grad = norm_back(gradient, normed, inverse, norm[0:1, :])
    one_grad[...] = first_grad
    grad_rows = first_grad.astype(BF16)
    head_grads[...] = dot_nt(grad_rows, w_self_out[...]).astype(BF16)
    scale = HEAD ** (-0.5)
    for begin in range(0, rows, BLOCK):
        span = slice(begin, begin + BLOCK)
        mask = block_mask(lengths, begin // SEQ)
        for pair in range(features // (2 * HEAD)):
            results = [[], [], []]
            for head in (2 * pair, 2 * pair + 1):
                queries, key_rows, value_rows = [
                    qkv[span, kind * features + head * HEAD : kind * features + (head + 1) * HEAD]
                    for kind in range(3)
                ]
                head_grad = head_grads[span, head * HEAD : (head + 1) * HEAD]
                probs = softmax(jnp.where(mask, dot_nt(queries, key_rows) * scale, MASK_VALUE))
                grad_probs = dot_nt(head_grad, value_rows)
                inner = jnp.sum(grad_probs * probs, axis=-1, keepdims=True)
                grad_scores = (probs * (grad_probs - inner)).astype(BF16)
                results[0].append((dot_nn(grad_scores, key_rows) * scale).astype(BF16))
                results[1].append((dot_tn(grad_scores, queries) * scale).astype(BF16))
                results[2].append(dot_tn(probs.astype(BF16), head_grad).astype(BF16))
            for kind in range(3):
                first = kind * features + pair * 2 * HEAD
                grad_qkv[span, first : first + 2 * HEAD] = jnp.concatenate(results[kind], axis=1)
    total = one_grad[...]
    for kind in range(3):
        columns = slice(kind * features, (kind + 1) * features)
        total = total + dot_nt(grad_qkv[:, columns], w_qkv[:, columns])
        first = kind * features
        keep[:, kind * half : (kind + 1) * half] = grad_qkv[:, first : first + half]
        send[:rows, kind * half : (kind + 1) * half] = grad_qkv[:, first + half : first + features]
    input_grad[...] = total.astype(BF16)
    keep[:, 3 * half :] = heads[:, :half]
    send[:rows, 3 * half : 4 * half] = heads[:, half:]
    send[:rows, 4 * half : 6 * half] = hidden[...]
    send[:rows, 6 * half :] = grad_rows
    send[rows:, :] = jnp.zeros((send.shape[0] - rows, send.shape[1]), BF16)
    send[rows : rows + 16, :features] = jnp.concatenate(
        [norm_sum, jnp.zeros_like(norm_sum)], axis=0
    ).astype(BF16)


def self_grad_kernel(
    place, keep, send, other, norm_total, left_keep, left_send, right_keep, right_send
):
    features = norm_total.shape[1]
    rows = keep.shape[0]
    half = features // 2
    width = half // 2
    block_rows = features // GROUPS
    out_rows = width // GROUPS
    split = left_keep.shape[2]
    inputs, slopes = slice(4 * half, 6 * half), slice(6 * half, 8 * half)
    columns = slice(0, 3 * half)
    grad_in = dot_tn(send[:rows, inputs], keep[:, columns])
    grad_in = grad_in + dot_tn(other[:rows, inputs], other[:rows, columns])
    columns = slice(3 * half, 4 * half)
    grad_out = dot_tn(keep[:, columns], send[:rows, slopes])
    grad_out = grad_out + dot_tn(other[:rows, columns], other[:rows, slopes])
    norm_rows = norm_total[...] + other[rows : rows + 16, :features].astype(F32)[:NORM_ROWS]
    for block in range(GROUPS):
        span = slice(block * block_rows, (block + 1) * block_rows)
        for y_rel in range(2):
            pieces = [
                grad_in[span, kind * half + y_rel * width : kind * half + (y_rel + 1) * width]
                for kind in range(3)
            ]
            begin = y_rel * width + block * out_rows
            out_part = grad_out[begin : begin + out_rows]
            pieces.append(
                jnp.concatenate(
                    [out_part[:, part * width : (part + 1) * width] for part in range(MODEL)],
                    axis=0,
                )
            )
            piece = jnp.concatenate([jnp.concatenate(pieces, axis=1), norm_rows], axis=0)
            put_left(place, block, y_rel, left_keep, left_send, piece[:split].astype(BF16))
            put_right(place, block, y_rel, right_keep, right_send, piece[split:].astype(BF16))


def adam_step(weight, moment_one, moment_two, gradient, decay_rate):
    moment_one = BETA_ONE * moment_one + (1.0 - BETA_ONE) * gradient
    moment_two = BETA_TWO * moment_two + (1.0 - BETA_TWO) * gradient * gradient
    update = (
        moment_one
        / (1.0 - BETA_ONE**STEP)
        / (jnp.sqrt(moment_two / (1.0 - BETA_TWO**STEP)) + ADAM_EPSILON)
        + decay_rate * weight
    )
    return moment_one, moment_two, update


def place_sums(target, sums):
    column = lax.broadcasted_iota(jnp.int32, (1, LANES), 1)
    rows = []
    for kind in range(2):
        row = jnp.zeros((1, LANES), F32)
        for index, pair in sums.items():
            row = jnp.where(column == index, pair[kind], row)
        rows.append(row)
    target[...] = jnp.concatenate(rows, axis=0)


def sum_pair(weight, update):
    return jnp.sum(weight * weight), jnp.sum(update * update)


def feed_update_kernel(
    gradient,
    up,
    up_moments,
    down,
    down_moments,
    up_next,
    down_next,
    up_update,
    down_update,
    squares,
):
    rows = up.shape[0]
    sums = {}
    for index, weight, moments, following, result, span in (
        (8, up, up_moments, up_next, up_update, slice(0, rows)),
        (9, down, down_moments, down_next, down_update, slice(rows, None)),
    ):
        following[0], following[1], update = adam_step(
            weight[...], moments[0], moments[1], gradient[span, :], DECAY_RATE
        )
        result[...] = update
        sums[index] = sum_pair(weight[...], update)
    place_sums(squares, sums)


def image_update_kernel(gradient, weight, moments, following, result, squares):
    width = weight.shape[2]
    half = weight.shape[1] // 2
    sums = {}
    for kind in range(2):
        parts = []
        for part in range(2):
            span = slice(part * half, (part + 1) * half)
            lanes = slice((2 * part + kind) * width, (2 * part + kind + 1) * width)
            following[0, kind, span, :], following[1, kind, span, :], update = adam_step(
                weight[kind, span, :],
                moments[0, kind, span, :],
                moments[1, kind, span, :],
                gradient[:half, lanes],
                DECAY_RATE,
            )
            result[kind, span, :] = update
            parts.append(sum_pair(weight[kind, span, :], update))
        sums[6 + kind] = tuple(left + right for left, right in zip(*parts))
    place_sums(squares, sums)


def last_update_kernel(
    gradient,
    cross_gradient,
    norm_gradient,
    inward,
    inward_moments,
    outward,
    outward_moments,
    norm,
    norm_moments,
    inward_next,
    outward_next,
    norm_next,
    inward_update,
    outward_update,
    norm_update,
    squares,
):
    own_in, width = inward.shape[1:]
    own_out = outward.shape[1]
    cross_rows = cross_gradient.shape[0] - 2 * own_out
    cross_query = cross_gradient[cross_rows : cross_rows + own_out, :]
    gradients = [gradient[:own_in, kind * width : (kind + 1) * width] for kind in range(3)]
    gradients.append(
        jnp.concatenate(
            [cross_query[:, part * width : (part + 1) * width] for part in range(MODEL)], axis=0
        )
    )
    sums = {}
    for kind in range(4):
        inward_next[0, kind], inward_next[1, kind], update = adam_step(
            inward[kind],
            inward_moments[0, kind],
            inward_moments[1, kind],
            gradients[kind],
            DECAY_RATE,
        )
        inward_update[kind] = update
        sums[kind] = sum_pair(inward[kind], update)
    folded = gradient[:own_in, 3 * width :]
    self_out = jnp.concatenate(
        [folded[part * own_out : (part + 1) * own_out] for part in range(MODEL)], axis=1
    )
    for kind, part in enumerate((self_out, cross_gradient[cross_rows + own_out :, :])):
        outward_next[0, kind], outward_next[1, kind], update = adam_step(
            outward[kind], outward_moments[0, kind], outward_moments[1, kind], part, DECAY_RATE
        )
        outward_update[kind] = update
        sums[4 + kind] = sum_pair(outward[kind], update)
    norm_next[0], norm_next[1], update = adam_step(
        norm[...], norm_moments[0], norm_moments[1], norm_gradient[...], 0.0
    )
    norm_update[...] = update
    for kind in range(norm.shape[0]):
        sums[10 + kind] = sum_pair(norm[kind : kind + 1, :], update[kind : kind + 1, :])
    place_sums(squares, sums)


def apply_kernel(squares, *refs):
    groups = len(refs) // 5
    weights, averages, updates = refs[:groups], refs[groups : 2 * groups], refs[2 * groups : 3 * groups]
    new_weights, new_averages = refs[3 * groups : 4 * groups], refs[4 * groups : 5 * groups]
    trust_out, norms_out = refs[5 * groups :]
    sums = jnp.sum(squares[...], axis=0)
    trust = jnp.sqrt(sums[0:1]) * lax.rsqrt(sums[1:2] + SQUARE_EPSILON)
    trust_out[...] = trust
    norms_out[...] = jnp.sqrt(sums)
    column = lax.broadcasted_iota(jnp.int32, trust.shape, 1)

    def ratio(index):
        return jnp.sum(jnp.where(column == index, trust, 0.0), axis=1, keepdims=True)

    index = 0
    for weight, average, update, new_weight, new_average in zip(
        weights, averages, updates, new_weights, new_averages
    ):
        if len(weight.shape) == 3:
            spans = list(range(weight.shape[0]))
        elif weight.shape[0] == 6:
            spans = [slice(row, row + 1) for row in range(6)]
        else:
            spans = [slice(None)]
        for span in spans:
            value = weight[span] - LEARN_RATE * ratio(index) * update[span]
            new_weight[span] = value
            new_average[span] = AVERAGE_RATE * average[span] + (1.0 - AVERAGE_RATE) * value
            index += 1


SCALARS = pl.BlockSpec(memory_space=pltpu.SMEM)
WHOLE = pl.BlockSpec(memory_space=pltpu.VMEM)
ANYWHERE = pl.BlockSpec(memory_space=pl.ANY)


def local_call(kernel, scalars, arrays, out_shapes, scratch, flops, name, limit, loose=()):
    size = sum(a.size * a.dtype.itemsize for a in (*arrays, *loose))
    size += sum(a.size * a.dtype.itemsize for a in out_shapes)
    return pl.pallas_call(
        kernel,
        out_shape=tuple(out_shapes),
        in_specs=[SCALARS] * len(scalars) + [WHOLE] * len(arrays) + [ANYWHERE] * len(loose),
        out_specs=tuple([WHOLE] * len(out_shapes)),
        scratch_shapes=scratch,
        compiler_params=pltpu.CompilerParams(vmem_limit_bytes=limit * MIB),
        cost_estimate=pl.CostEstimate(flops=flops, bytes_accessed=size, transcendentals=0),
        name=name,
    )(*scalars, *arrays, *loose)


def shape_of(*dims, dtype=BF16):
    return jax.ShapeDtypeStruct(dims, dtype)


def part_shapes(left_rows, right_rows, features):
    left, right = shape_of(2, 4, left_rows, features), shape_of(2, 4, right_rows, features)
    return left, left, right, right


def like(array):
    return jax.ShapeDtypeStruct(array.shape, array.dtype)


def update_call(kernel, arrays, moments, weights, name):
    shapes = [like(each) for each in (*moments, *weights)] + [shape_of(2, LANES, dtype=F32)]
    return local_call(kernel, (), arrays, shapes, [], 0, name, 20)


def apply_call(squares, weights, averages, updates):
    shapes = [like(each) for each in (*weights, *averages)]
    shapes += [shape_of(1, LANES, dtype=F32), shape_of(2, LANES, dtype=F32)]
    return local_call(
        apply_kernel, (), (squares, *weights, *averages, *updates), shapes, [], 0, "apply", 60
    )


class Direct:
    def __init__(self, dp, mp):
        self.count = dp * mp
        self.mp = mp
        self.depth = dp // 2
        index = lax.axis_index("dp")
        block = jnp.arange(GROUPS, dtype=jnp.int32)
        along_x = (block % 2) ^ (index % 2)
        along_z = (index // 2 - block // 2) % self.depth
        self.place = jnp.concatenate([along_x, along_z]).astype(jnp.int32)

    def hop(self, values, flip):
        return lax.ppermute(values, AXES, [(i, i ^ flip) for i in range(self.count)])

    def hop_core(self, values):
        return self.hop(values, 1)

    def hop_y(self, values):
        return self.hop(values, 2)

    def hop_x(self, values):
        return self.hop(values, self.mp)

    def hop_z(self, values, distance):
        step = 2 * self.mp * distance
        return lax.ppermute(values, AXES, [(i, (i + step) % self.count) for i in range(self.count)])

    def spread_z(self, piece):
        return jnp.stack([piece] + [self.hop_z(piece, step) for step in range(1, self.depth)])


    def spread_first(self, held, split):
        return self.hop_y(held[:, :split]), self.hop_x(held[:, split:])

    def join_first(self, held, split, others):
        return jnp.stack([held[:, :split], others[0]]), jnp.stack([held[:, split:], others[1]])

    def spread_second(self, parts):
        return self.hop_x(parts[0]), self.hop_y(parts[1])

    def join_second(self, parts, others):
        left = jnp.stack([parts[0], others[0]])
        right = jnp.stack([parts[1], others[1]]).transpose(1, 0, 2, 3, 4)
        whole = jnp.concatenate([left, right], axis=3)
        return whole.reshape(SLOTS, *whole.shape[3:])


    def fold_first(self, grads):
        return self.hop_x(grads[1]), self.hop_y(grads[3])

    def fold_second(self, grads, others):
        return (
            self.hop_y(total([grads[0][1], others[0][1]])),
            self.hop_x(total([grads[2][1], others[1][1]])),
        )

    def kept(self, grads, others, last):
        return [[grads[2 * side][0], others[side][0], last[side]] for side in range(2)]

    def fold_z(self, sides):
        return [
            self.hop_z(total(*[[part[step] for part in parts] for parts in sides]), -step)
            for step in range(1, self.depth)
        ]

    def ring_z(self, sides, step, carried=None):
        addends = [[part[step] for part in parts] for parts in sides]
        own = total(*addends, dtype=F32)
        if carried is not None:
            own = own + carried.astype(F32)
        return self.hop_z(own.astype(BF16), 1)

    def finish(self, sides, others):
        own = total(*[[part[0] for part in parts] for parts in sides], dtype=F32)
        return total([own, *others], dtype=F32)


def total(*sides, dtype=BF16):
    sums = []
    for parts in sides:
        result = parts[0].astype(F32)
        for part in parts[1:]:
            result = result + part.astype(F32)
        sums.append(result.astype(dtype))
    return sums[0] if len(sums) == 1 else jnp.concatenate(sums, axis=0)


class Plain:
    def __init__(self, dp, mp):
        self.dp = dp
        self.mp = mp
        self.side = lax.axis_index("mp") // 2
        block = jnp.arange(GROUPS, dtype=jnp.int32)
        self.place = jnp.concatenate([block % 2, block // 2]).astype(jnp.int32)

    def hop_core(self, values):
        count = self.dp * self.mp
        return lax.ppermute(values, AXES, [(i, i ^ 2) for i in range(count)])

    def collect(self, piece):
        rows, width = piece.shape
        blocks = lax.all_gather(piece, AXES, axis=0).reshape(self.dp, self.mp, rows, width)
        rows = rows * self.dp // GROUPS
        blocks = blocks.transpose(1, 0, 2, 3).reshape(2, 2, 4, 2, rows, width)
        blocks = blocks.transpose(0, 3, 1, 2, 4, 5).reshape(2, SLOTS, rows, width)
        return jnp.where(self.side == 0, blocks, blocks[::-1])

    def joined(self, grads):
        left = jnp.stack(grads[:2])
        right = jnp.stack(grads[2:]).transpose(1, 0, 2, 3, 4)
        return jnp.concatenate([left, right], axis=3)

    def scatter(self, own):
        rows, width = own.shape[3:]
        own = own.transpose(1, 2, 0, 3, 4).reshape(1, 2, GROUPS, rows, width)
        both = jnp.zeros((2, *own.shape[1:]), F32)
        both = lax.dynamic_update_slice_in_dim(both, own.astype(F32), self.side, 0)
        both = both.reshape(self.mp, self.dp, rows * GROUPS // self.dp, width)
        both = both.transpose(1, 0, 2, 3).reshape(-1, width)
        return lax.psum_scatter(both, AXES, scatter_dimension=0, tiled=True)


def tie(*arrays):
    return lax.optimization_barrier(arrays)


def padded(feats):
    pad = ((0, 0), (0, SLOT - PATCHES), (0, 0))
    return jnp.pad(feats, pad).reshape(-1, feats.shape[2])


def tie(*arrays):
    return lax.optimization_barrier(arrays)


def add(left_side, right_side):
    return (left_side.astype(F32) + right_side.astype(F32)).astype(BF16)


def self_forward(place, lengths, hidden, begin):
    rows, features = hidden.shape
    return local_call(
        self_forward_kernel,
        (place, lengths),
        (hidden, *begin),
        (
            shape_of(rows, features, dtype=F32),
            shape_of(rows, 3 * features),
            shape_of(rows, features),
            shape_of(features, 3 * features),
            shape_of(features, features),
            shape_of(features, features),
            shape_of(features, features),
            shape_of(NORM_ROWS, features, dtype=F32),
        ),
        [pltpu.VMEM((features, features), F32), pltpu.VMEM((features, features), F32)],
        10 * rows * features * features,
        "self_forward",
        28,
    )


def image_forward(place, feats, image):
    items, patches, encoded = feats.shape
    items = items // 2
    rows = items * SLOT
    features = image[0].shape[2] // 2 * MODEL
    piece_spec = pl.BlockSpec(image[0].shape, lambda item, where: (0, 0, 0))
    return pl.pallas_call(
        image_forward_kernel,
        out_shape=shape_of(rows, 2 * features),
        grid_spec=pltpu.PrefetchScalarGridSpec(
            num_scalar_prefetch=1,
            grid=(items,),
            in_specs=[
                pl.BlockSpec(
                    (1, patches, encoded), lambda item, where: (where[2 * GROUPS] + item, 0, 0)
                ),
                piece_spec,
                piece_spec,
            ],
            out_specs=pl.BlockSpec((SLOT, 2 * features), lambda item, where: (item, 0)),
            scratch_shapes=[pltpu.VMEM((encoded, 2 * features), BF16)],
        ),
        compiler_params=pltpu.CompilerParams(vmem_limit_bytes=24 * MIB),
        cost_estimate=pl.CostEstimate(
            flops=4 * rows * encoded * features,
            bytes_accessed=2 * rows * (encoded + 2 * features) + 4 * encoded * features,
            transcendentals=0,
        ),
        name="image_forward",
    )(place, feats, *image)


def cross_forward(first_in, norm, w_cross, w_cross_out, key_values):
    features = first_in.shape[1]
    queries = first_in.shape[0] // SEQ * QUERIES
    return local_call(
        cross_forward_kernel,
        (),
        (first_in, norm, w_cross, w_cross_out, key_values),
        (
            shape_of(queries, features, dtype=F32),
            shape_of(queries, features),
            shape_of(queries, features),
        ),
        [],
        4 * queries * features * features,
        "cross_forward",
        18,
    )


def feed(place, lengths, first_in, second_in, norm, out_grad, weights):
    rows, features = first_in.shape
    width = weights[0].shape[2]
    return local_call(
        feed_kernel,
        (place, lengths),
        (first_in, second_in, norm, out_grad),
        (
            shape_of(rows, features),
            shape_of(rows, features, dtype=F32),
            shape_of(rows, 4 * width),
            shape_of(rows, 4 * width + 2 * features),
            shape_of(NORM_ROWS, features, dtype=F32),
        ),
        [
            pltpu.VMEM((MODEL, features, width), BF16),
            pltpu.VMEM((MODEL, width, features), BF16),
            pltpu.VMEM((rows, features), F32),
            pltpu.VMEM((rows, MODEL * width), F32),
            pltpu.SemaphoreType.DMA((MODEL,)),
            pltpu.SemaphoreType.DMA((MODEL,)),
        ],
        8 * rows * features * MODEL * width,
        "feed",
        40,
        loose=weights,
    )


def feed_grad(place, keep, send, other, rows):
    features = (send.shape[1] - keep.shape[1]) // 2
    width = keep.shape[1] // 4
    tokens = keep.shape[0]
    shapes = part_shapes(rows, rows, features)
    hidden_spec = pl.BlockSpec(
        (tokens, width), lambda kind, y_step, where: (0, 2 * (1 - kind) + y_step)
    )
    row_spec = pl.BlockSpec(
        (tokens, features), lambda kind, y_step, where: (0, 4 * width // features + kind)
    )
    return pl.pallas_call(
        feed_grad_kernel,
        out_shape=shapes,
        grid_spec=pltpu.PrefetchScalarGridSpec(
            num_scalar_prefetch=1,
            grid=(2, 2),
            in_specs=[hidden_spec, row_spec, hidden_spec, row_spec],
            out_specs=[fixed(shape.shape) for shape in shapes],
        ),
        compiler_params=pltpu.CompilerParams(vmem_limit_bytes=36 * MIB),
        cost_estimate=pl.CostEstimate(
            flops=4 * tokens * features * keep.shape[1],
            bytes_accessed=24 * tokens * features,
            transcendentals=0,
        ),
        name="feed_grad",
    )(place, keep, send, other, other)


def fixed(shape):
    return pl.BlockSpec(shape, lambda *_: (0,) * len(shape))


def cross_backward(
    two_grad,
    first_in,
    second_in,
    norm,
    w_cross,
    w_cross_out,
    queries,
    heads,
    key_values,
    norm_grads,
):
    features = first_in.shape[1]
    count = queries.shape[0]
    items = key_values.shape[0] // SLOT
    rows = (items + 3) * SLOT
    arrays = (
        two_grad,
        first_in,
        second_in,
        norm,
        w_cross,
        w_cross_out,
        queries,
        heads,
        key_values,
        norm_grads,
    )
    specs = [fixed(each.shape) for each in arrays]
    specs[8] = pl.BlockSpec(
        (SLOT, 2 * features), lambda item: (jnp.minimum(item, items - 1), 0)
    )
    row_spec = pl.BlockSpec((SLOT, features), lambda item: (item, 0))
    return pl.pallas_call(
        cross_backward_kernel,
        grid=(items + 3,),
        out_shape=(
            shape_of(rows, features),
            shape_of(rows, features),
            shape_of(count, features, dtype=F32),
            shape_of(NORM_ROWS, features, dtype=F32),
        ),
        in_specs=specs,
        out_specs=(row_spec, row_spec, fixed((count, features)), fixed((NORM_ROWS, features))),
        scratch_shapes=[pltpu.VMEM((count, features), BF16)] * 3,
        compiler_params=pltpu.CompilerParams(vmem_limit_bytes=36 * MIB),
        cost_estimate=pl.CostEstimate(
            flops=20 * count * features * features,
            bytes_accessed=12 * rows * features,
            transcendentals=0,
        ),
        name="cross_backward",
    )(*arrays)


def image_grad(place, feats, keep, other):
    features = keep.shape[1]
    items, patches, encoded = feats.shape
    rows = items * SLOT
    piece = encoded // GROUPS // 2 + 2 * (features // MODEL // GROUPS)
    steps = 4
    block = rows // steps
    last = steps // 2 - 1
    shapes = part_shapes(IMAGE_SPLIT, piece - IMAGE_SPLIT, features)
    out_specs = [pl.BlockSpec(shape.shape, lambda step, where: (0, 0, 0, 0)) for shape in shapes]
    rest = pl.BlockSpec((block, features), lambda step, where: (steps // 2, 0))
    return pl.pallas_call(
        functools.partial(image_grad_kernel, items // 2 * QUERIES),
        out_shape=shapes,
        grid_spec=pltpu.PrefetchScalarGridSpec(
            num_scalar_prefetch=1,
            grid=(steps,),
            in_specs=[
                pl.BlockSpec(
                    (items // steps, patches, encoded),
                    lambda step, where: (
                        (step + where[2 * GROUPS] // (items // steps)) % steps,
                        0,
                        0,
                    ),
                ),
                pl.BlockSpec((block, features), lambda step, where: (jnp.minimum(step, last), 0)),
                pl.BlockSpec(
                    (block, features), lambda step, where: (jnp.maximum(step - last - 1, 0), 0)
                ),
                rest,
                rest,
            ],
            out_specs=out_specs,
            scratch_shapes=[pltpu.VMEM((encoded, features), F32), pltpu.VMEM((block, encoded), BF16)],
        ),
        compiler_params=pltpu.CompilerParams(vmem_limit_bytes=34 * MIB),
        cost_estimate=pl.CostEstimate(
            flops=2 * rows * encoded * features,
            bytes_accessed=2 * rows * (encoded + features),
            transcendentals=0,
        ),
        name="image_grad",
    )(place, feats, keep, other, keep, other)


def self_backward(
    lengths,
    one_query_grad,
    two_grad,
    first_in,
    norm,
    hidden,
    qkv,
    heads,
    w_qkv,
    w_self_out,
    norm_grads,
):
    rows, features = hidden.shape
    return local_call(
        self_backward_kernel,
        (lengths,),
        (
            one_query_grad,
            two_grad,
            first_in,
            norm,
            hidden,
            qkv,
            heads,
            w_qkv,
            w_self_out,
            norm_grads,
        ),
        (
            shape_of(rows, features),
            shape_of(rows, 2 * features),
            shape_of(rows + 16, 4 * features),
            shape_of(NORM_ROWS, features, dtype=F32),
        ),
        [
            pltpu.VMEM((rows, features), F32),
            pltpu.VMEM((rows, features), BF16),
            pltpu.VMEM((rows, 3 * features), BF16),
        ],
        16 * rows * features * features,
        "self_backward",
        30,
    )


def self_grad(place, keep, send, other, norm_total):
    features = norm_total.shape[1]
    rows = features // GROUPS + NORM_ROWS
    return local_call(
        self_grad_kernel,
        (place,),
        (keep, send, other, norm_total),
        part_shapes(SELF_SPLIT, rows - SELF_SPLIT, features),
        [],
        8 * keep.shape[0] * features * features,
        "self_grad",
        24,
    )


def run_direct(hidden, feats, first_item, lengths, out_grad, image, begin, weights):
    moves = Direct(lax.axis_size("dp"), lax.axis_size("mp"))
    place = moves.place
    feats_place = jnp.concatenate([place, first_item[None].astype(jnp.int32)])
    begin_split = begin.shape[0] // 2
    image_split = image.shape[0] * 96 // 176
    feed_split = weights.shape[0] // 2

    begin = moves.spread_z(begin)
    begin, image, feats = tie(begin, image, feats)
    begin_others = moves.spread_first(begin, begin_split)
    image = moves.spread_z(image)
    begin_others, image, weights, feats = tie(begin_others, image, weights, feats)
    begin_parts = moves.join_first(begin, begin_split, begin_others)
    begin_others = moves.spread_second(begin_parts)
    image_others = moves.spread_first(image, image_split)
    weights = moves.spread_z(weights)
    begin_others, image_others, weights = tie(begin_others, image_others, weights)

    image_parts = moves.join_first(image, image_split, image_others)
    image_others = moves.spread_second(image_parts)
    weight_others = moves.spread_first(weights, feed_split)
    begin = moves.join_second(begin_parts, begin_others)
    begin_other = moves.hop_core(begin)
    first_in, qkv, heads, w_qkv, w_cross, w_self_out, w_cross_out, norm = self_forward(
        place, lengths, hidden, (begin, begin_other)
    )
    first_in, image_others, weight_others = tie(first_in, image_others, weight_others)
    image = moves.join_second(image_parts, image_others)
    weight_parts = moves.join_first(weights, feed_split, weight_others)
    image_other = moves.hop_core(image)
    image_other, weight_parts, first_in = tie(image_other, weight_parts, first_in)
    weight_others = moves.spread_second(weight_parts)
    key_values = image_forward(feats_place, feats, (image, image_other))
    second_in, cross_queries, cross_heads = cross_forward(
        first_in, norm, w_cross, w_cross_out, key_values
    )
    second_in, weight_others = tie(second_in, weight_others)
    weights = moves.join_second(weight_parts, weight_others)
    weights_other = moves.hop_core(weights)
    block_out, two_grad, feed_keep, feed_send, norm_grads = feed(
        place, lengths, first_in, second_in, norm, out_grad, (weights, weights_other)
    )

    feed_other = moves.hop_core(feed_send)
    cross_keep, cross_send, one_query_grad, norm_grads = cross_backward(
        two_grad,
        first_in,
        second_in,
        norm,
        w_cross,
        w_cross_out,
        cross_queries,
        cross_heads,
        key_values,
        norm_grads,
    )
    cross_send, feed_other = tie(cross_send, feed_other)
    cross_other = moves.hop_core(cross_send)
    feed_grads = feed_grad(place, feed_keep, feed_send, feed_other, feed_split)
    cross_other, feed_grads = tie(cross_other, feed_grads)
    feed_first = moves.fold_first(feed_grads)
    image_grads = image_grad(feats_place, feats, cross_keep, cross_other)
    one_query_grad, image_grads, feed_first = tie(one_query_grad, image_grads, feed_first)
    feed_second = moves.fold_second(feed_grads, feed_first)
    image_first = moves.fold_first(image_grads)
    input_grad, self_keep, self_send, norm_total = self_backward(
        lengths,
        one_query_grad,
        two_grad,
        first_in,
        norm,
        hidden,
        qkv,
        heads,
        w_qkv,
        w_self_out,
        norm_grads,
    )
    self_send, image_first, feed_second = tie(self_send, image_first, feed_second)
    self_other = moves.hop_core(self_send)
    feed_kept = moves.kept(feed_grads, feed_first, feed_second)
    feed_other = moves.ring_z(feed_kept, 1)
    image_second = moves.fold_second(image_grads, image_first)
    self_grads = self_grad(place, self_keep, self_send, self_other, norm_total)
    self_grads, feed_other = tie(self_grads, feed_other)
    self_first = moves.fold_first(self_grads)
    feed_other = moves.ring_z(feed_kept, 2, feed_other)
    feed_other, image_second = tie(feed_other, image_second)
    image_kept = moves.kept(image_grads, image_first, image_second)
    feed_other = moves.ring_z(feed_kept, 3, feed_other)
    image_other = moves.ring_z(image_kept, 1)
    self_first, image_other, feed_other = tie(self_first, image_other, feed_other)
    self_second = moves.fold_second(self_grads, self_first)
    image_other = moves.ring_z(image_kept, 2, image_other)
    feed_sum = moves.finish(feed_kept, [feed_other])
    image_other, self_second = tie(image_other, self_second)
    image_other = moves.ring_z(image_kept, 3, image_other)
    self_kept = moves.kept(self_grads, self_first, self_second)
    self_others = moves.fold_z(self_kept)
    image_sum = moves.finish(image_kept, [image_other])
    in_sum = moves.finish(self_kept, self_others)
    return block_out, input_grad, in_sum, image_sum, feed_sum


def run_plain(hidden, feats, first_item, lengths, out_grad, image, begin, weights):
    moves = Plain(lax.axis_size("dp"), lax.axis_size("mp"))
    place = moves.place
    feats_place = jnp.concatenate([place, first_item[None].astype(jnp.int32)])
    features = hidden.shape[1]
    width = features // MODEL
    block_rows, out_rows = features // GROUPS, width // GROUPS
    own_in, own_out = block_rows * GROUPS // moves.dp, out_rows * GROUPS // moves.dp
    half = block_rows // 2
    part = begin.shape[0] - NORM_ROWS
    inward = moves.collect(begin[:own_in])
    cross_out = moves.collect(begin[own_in : own_in + own_out])
    self_out = moves.collect(begin[own_in + own_out : part])
    norm_all = lax.psum(begin[part:].astype(F32), AXES).astype(BF16)
    norm_first = jnp.zeros((2, SLOTS, NORM_ROWS, features), BF16).at[0, 0].set(norm_all)
    begin = jnp.concatenate(
        [
            inward[:, :, :half],
            cross_out,
            jnp.zeros_like(norm_first),
            inward[:, :, half:],
            self_out,
            norm_first,
        ],
        axis=2,
    )
    image = moves.collect(image)
    own_up = weights.shape[0] // 2
    weights = jnp.concatenate(
        [moves.collect(weights[:own_up]), moves.collect(weights[own_up:])], axis=2
    )
    first_in, qkv, heads, w_qkv, w_cross, w_self_out, w_cross_out, norm = self_forward(
        place, lengths, hidden, (begin[0], begin[1])
    )
    key_values = image_forward(feats_place, feats, (image[0], image[1]))
    second_in, cross_queries, cross_heads = cross_forward(
        first_in, norm, w_cross, w_cross_out, key_values
    )
    block_out, two_grad, feed_keep, feed_send, norm_grads = feed(
        place, lengths, first_in, second_in, norm, out_grad, (weights[0], weights[1])
    )
    feed_half = weights.shape[2] // 2
    feed_grads = feed_grad(place, feed_keep, feed_send, moves.hop_core(feed_send), feed_half)
    cross_keep, cross_send, one_query_grad, norm_grads = cross_backward(
        two_grad,
        first_in,
        second_in,
        norm,
        w_cross,
        w_cross_out,
        cross_queries,
        cross_heads,
        key_values,
        norm_grads,
    )
    image_grads = image_grad(feats_place, feats, cross_keep, moves.hop_core(cross_send))
    input_grad, self_keep, self_send, norm_total = self_backward(
        lengths,
        one_query_grad,
        two_grad,
        first_in,
        norm,
        hidden,
        qkv,
        heads,
        w_qkv,
        w_self_out,
        norm_grads,
    )
    self_grads = self_grad(place, self_keep, self_send, moves.hop_core(self_send), norm_total)

    def beside(values):
        count = values.shape[-2] // MODEL
        return jnp.concatenate(
            [values[..., part * count : (part + 1) * count, :] for part in range(MODEL)], axis=-1
        )

    def below(values):
        count = values.shape[-1] // MODEL
        return jnp.concatenate(
            [values[..., part * count : (part + 1) * count] for part in range(MODEL)], axis=-2
        )

    grads = moves.joined(self_grads)
    in_part = moves.scatter(grads[..., :block_rows, : 3 * width])
    self_out = moves.scatter(beside(grads[..., :block_rows, 3 * width :]))
    norm_sum = lax.psum(norm_total, AXES)
    in_sum = jnp.concatenate([jnp.concatenate([in_part, below(self_out)], axis=1), norm_sum])
    grads = moves.joined(image_grads)
    image_rows = grads.shape[3] - 2 * out_rows
    image_part = grads[..., :image_rows, :]
    image_part = jnp.concatenate(
        [image_part[..., : features // 2], image_part[..., features // 2 :]], axis=3
    )
    image_part = moves.scatter(image_part)
    image_half = image_part.shape[0] // 2
    image_part = jnp.concatenate([image_part[:image_half], image_part[image_half:]], axis=1)
    cross_query = moves.scatter(below(grads[..., image_rows : image_rows + out_rows, :]))
    cross_out = moves.scatter(grads[..., image_rows + out_rows :, :])
    image_sum = jnp.concatenate([image_part, beside(cross_query), cross_out])
    grads = moves.joined(feed_grads)
    feed_sum = jnp.concatenate(
        [moves.scatter(jnp.stack(feed_grads[:2])), moves.scatter(grads[..., feed_half:, :])]
    )
    return block_out, input_grad, in_sum, image_sum, feed_sum


def per_device(
    hidden_in,
    image_feats,
    caption_lengths,
    out_grad,
    proj_in,
    proj_in_moments,
    proj_in_average,
    proj_out,
    proj_out_moments,
    proj_out_average,
    image_kv,
    image_kv_moments,
    image_kv_average,
    feed_up,
    feed_up_moments,
    feed_up_average,
    feed_down,
    feed_down_moments,
    feed_down_average,
    norm_params,
    norm_params_moments,
    norm_params_average,
):
    data_ways, model_ways = lax.axis_size("dp"), lax.axis_size("mp")
    data_index, model_index = lax.axis_index("dp"), lax.axis_index("mp")
    rows, features = hidden_in.shape
    items = rows // SEQ
    width = features // model_ways
    own_norm = norm_params.shape[1]
    norm_begin = (model_index * data_ways + data_index) * own_norm
    lengths = lax.dynamic_slice_in_dim(caption_lengths, model_index * items, items, 0)
    direct = data_ways == GROUPS and model_ways == MODEL
    if direct:
        feats = lax.dynamic_slice_in_dim(image_feats, model_index // 2 * 2 * items, 2 * items, 0)
        first_item = model_index % 2 * items
    else:
        feats = jnp.concatenate(
            [
                lax.dynamic_slice_in_dim(image_feats, (model_index % 2 + 2 * side) * items, items, 0)
                for side in range(2)
            ]
        )
        first_item = model_index // 2 * items
    image_piece = jnp.concatenate([image_kv[0], image_kv[1]], axis=1).astype(BF16)
    in_piece = jnp.concatenate([proj_in[kind] for kind in range(4)], axis=1).astype(BF16)
    out_pieces = [proj_out[kind].astype(BF16) for kind in range(2)]
    feed_piece = jnp.concatenate([feed_up, feed_down], axis=0).astype(BF16)
    norm_rows = lax.dynamic_update_slice(
        jnp.zeros((NORM_ROWS, features), F32), norm_params, (0, norm_begin)
    ).astype(BF16)
    own_in, own_out, own_image = proj_in.shape[1], proj_out.shape[1], image_kv.shape[1]
    if direct:
        run, half = run_direct, own_in // 2
        begin_piece = jnp.concatenate(
            [
                in_piece[:half],
                out_pieces[1],
                jnp.zeros_like(norm_rows),
                in_piece[half:],
                out_pieces[0],
                norm_rows,
            ],
            axis=0,
        )
    else:
        run = run_plain
        begin_piece = jnp.concatenate(
            [in_piece, out_pieces[1], out_pieces[0], norm_rows], axis=0
        )
    block_out, input_grad, in_sum, image_sum, feed_sum = run(
        hidden_in, feats, first_item, lengths, out_grad, image_piece, begin_piece, feed_piece
    )
    norm_shard = lax.dynamic_slice(in_sum[own_in:], (0, norm_begin), norm_params.shape)
    up_next, down_next, up_update, down_update, feed_squares = update_call(
        feed_update_kernel,
        (feed_sum, feed_up, feed_up_moments, feed_down, feed_down_moments),
        (feed_up_moments, feed_down_moments),
        (feed_up, feed_down),
        "feed_update",
    )
    image_next, image_update, image_squares = update_call(
        image_update_kernel,
        (image_sum, image_kv, image_kv_moments),
        (image_kv_moments,),
        (image_kv,),
        "image_update",
    )
    in_next, out_next, norm_next, in_update, out_update, norm_update, last_squares = update_call(
        last_update_kernel,
        (
            in_sum,
            image_sum,
            norm_shard,
            proj_in,
            proj_in_moments,
            proj_out,
            proj_out_moments,
            norm_params,
            norm_params_moments,
        ),
        (proj_in_moments, proj_out_moments, norm_params_moments),
        (proj_in, proj_out, norm_params),
        "last_update",
    )
    own_squares = feed_squares + image_squares + last_squares
    ways = data_ways * model_ways
    copies = jnp.broadcast_to(own_squares[None], (ways,) + own_squares.shape)
    squares = lax.all_to_all(copies, AXES, 0, 0, tiled=True)
    results = apply_call(
        squares,
        (proj_in, proj_out, image_kv, feed_up, feed_down, norm_params),
        (
            proj_in_average,
            proj_out_average,
            image_kv_average,
            feed_up_average,
            feed_down_average,
            norm_params_average,
        ),
        (in_update, out_update, image_update, up_update, down_update, norm_update),
    )
    new_weights, new_averages, (trust, norms) = results[:6], results[6:12], results[12:]
    moments = (in_next, out_next, image_next, up_next, down_next, norm_next)
    outputs = [
        each for group in zip(new_weights, moments, new_averages) for each in group
    ]
    tensors = sum(each.shape[0] for each in (proj_in, proj_out, image_kv, norm_params)) + 2
    return (block_out, input_grad, *outputs, trust[0, :tensors], norms[:, :tensors])


def solution(mesh):
    rows = P(AXES, None)
    by_column = P(None, "dp", "mp")
    by_row = P(None, ("mp", "dp"), None)
    weights = (
        by_column,
        P(None, None, "dp", "mp"),
        by_column,
        by_row,
        P(None, None, ("mp", "dp"), None),
        by_row,
        by_column,
        P(None, None, "dp", "mp"),
        by_column,
        P("dp", "mp"),
        P(None, "dp", "mp"),
        P("dp", "mp"),
        P(("mp", "dp"), None),
        P(None, ("mp", "dp"), None),
        P(("mp", "dp"), None),
        P(None, ("mp", "dp")),
        P(None, None, ("mp", "dp")),
        P(None, ("mp", "dp")),
    )
    return jax.shard_map(
        per_device,
        mesh=mesh,
        in_specs=(rows, P("dp", None, None), P("dp"), rows, *weights),
        out_specs=(rows, rows, *weights, P(), P()),
        check_vma=False,
    )
```

```python
import functools

import jax
import jax.numpy as jnp
from jax import lax
from jax.experimental import pallas as pl
from jax.experimental.pallas import tpu as pltpu
from jax.sharding import PartitionSpec as P

HEAD = 64
PATCHES = 257
QUERIES = 32
TEXT = 32
SEQ = QUERIES + TEXT
STEP = 10


NORM_EPSILON = 1e-06
ADAM_EPSILON = 1e-06
SQUARE_EPSILON = 1e-06
BETA_ONE = 0.9
BETA_TWO = 0.999
LEARN_RATE = 0.5
DECAY_RATE = 0.01
AVERAGE_RATE = 0.6
MASK_VALUE = -1e30

AXES = ("dp", "mp")
GROUPS = 8
MODEL = 4
SLOTS = 16
NORM_ROWS = 8
LANES = 128
IMAGE_SPLIT = 64
SELF_SPLIT = 48
BLOCK = 128
WIDE = 256
HEADS_AT_ONCE = 12
SLOT = 272
MIB = 1024 * 1024

BF16 = jnp.bfloat16
F32 = jnp.float32


def dot_nn(left_side, right_side):
    return lax.dot_general(
        left_side, right_side, (((1,), (0,)), ((), ())), preferred_element_type=F32
    )


def dot_nt(left_side, right_side):
    return lax.dot_general(
        left_side, right_side, (((1,), (1,)), ((), ())), preferred_element_type=F32
    )


def dot_tn(left_side, right_side):
    return lax.dot_general(
        left_side, right_side, (((0,), (0,)), ((), ())), preferred_element_type=F32
    )


def normalise(inputs):
    centred = inputs - jnp.mean(inputs, axis=-1, keepdims=True)
    inverse = lax.rsqrt(jnp.mean(centred * centred, axis=-1, keepdims=True) + NORM_EPSILON)
    return centred * inverse, inverse


def norm_back(gradient, normed, inverse, gain):
    scaled = gradient * gain
    centre_term = jnp.mean(scaled, axis=-1, keepdims=True)
    normed_term = jnp.mean(scaled * normed, axis=-1, keepdims=True)
    return inverse * (scaled - centre_term - normed * normed_term)


def slot_of(place, block, y_rel):
    return place[block] * 8 + y_rel * 4 + place[GROUPS + block]


def softmax(scores):
    tops = [jnp.max(each, axis=-1, keepdims=True) for each in scores]
    exponents = [jnp.exp(each - top) for each, top in zip(scores, tops)]
    totals = [jnp.sum(each, axis=-1, keepdims=True) for each in exponents]
    return [each / total for each, total in zip(exponents, totals)]


def block_mask(lengths, first_item):
    per_block = BLOCK // SEQ
    row = lax.broadcasted_iota(jnp.int32, (BLOCK, BLOCK), 0)
    column = lax.broadcasted_iota(jnp.int32, (BLOCK, BLOCK), 1)
    row_item, column_item = lax.shift_right_logical(row, 6), lax.shift_right_logical(column, 6)
    slot = column - column_item * SEQ
    limit = jnp.zeros((BLOCK, BLOCK), jnp.int32)
    for item in range(per_block):
        limit = jnp.where(column_item == item, lengths[first_item + item] + QUERIES, limit)
    return (row_item == column_item) & (slot < limit)


def self_forward_kernel(
    place,
    lengths,
    hidden,
    begin_own,
    begin_other,
    first_in,
    qkv,
    heads,
    w_qkv,
    w_cross,
    w_self_out,
    w_cross_out,
    norm,
    self_rows,
    cross_rows,
):
    rows, features = hidden.shape
    width = features // MODEL
    block_rows = features // GROUPS
    out_rows = width // GROUPS
    half, part = block_rows // 2, begin_own.shape[1] // 2
    norm_sum = jnp.zeros((NORM_ROWS, features), F32)
    for block in range(GROUPS):
        pieces = []
        for model in range(MODEL):
            side, y_rel = divmod(model, 2)
            source, slot = (begin_own, begin_other)[side], slot_of(place, block, y_rel)
            pieces.append(
                jnp.concatenate(
                    [source[slot, :half, :], source[slot, part : part + half, :]], axis=0
                )
            )
            cross_part = source[slot, half:part, :].astype(F32)
            self_part = source[slot, part + half :, :].astype(F32)
            begin = model * width + block * out_rows
            cross_rows[begin : begin + out_rows, :] = cross_part[:out_rows]
            self_rows[begin : begin + out_rows, :] = self_part[:out_rows]
            norm_sum = norm_sum + self_part[out_rows:]
        begin = block * block_rows
        for kind in range(4):
            joined = jnp.concatenate(
                [piece[:, kind * width : (kind + 1) * width] for piece in pieces], axis=1
            )
            if kind < 3:
                w_qkv[begin : begin + block_rows, kind * features : (kind + 1) * features] = joined
            else:
                w_cross[begin : begin + block_rows, :] = joined
    norm[...] = norm_sum
    w_self_out[...] = self_rows[...].astype(BF16)
    w_cross_out[...] = cross_rows[...].astype(BF16)
    tokens = hidden[...]
    for kind in range(3):
        columns = slice(kind * features, (kind + 1) * features)
        qkv[:, columns] = dot_nn(tokens, w_qkv[:, columns]).astype(BF16)
    scale = HEAD ** (-0.5)
    for begin in range(0, rows, BLOCK):
        span = slice(begin, begin + BLOCK)
        mask = block_mask(lengths, begin // SEQ)
        for first in range(0, features // HEAD, HEADS_AT_ONCE):
            queries, key_rows, value_rows = [
                [
                    qkv[span, kind * features + head * HEAD : kind * features + (head + 1) * HEAD]
                    for head in range(first, first + HEADS_AT_ONCE)
                ]
                for kind in range(3)
            ]
            scores = [dot_nt(*pair) for pair in zip(queries, key_rows)]
            probs = softmax([jnp.where(mask, each * scale, MASK_VALUE) for each in scores])
            mixed = [dot_nn(*pair) for pair in zip([each.astype(BF16) for each in probs], value_rows)]
            heads[span, first * HEAD : (first + HEADS_AT_ONCE) * HEAD] = jnp.concatenate(
                [each.astype(BF16) for each in mixed], axis=1
            )
    first_in[...] = tokens.astype(F32) + dot_nn(heads[...], w_self_out[...])


def assemble_image(place, image_own, image_other, weight):
    block_rows = image_own.shape[1]
    width = image_own.shape[2] // 2
    features = width * MODEL
    for block in range(GROUPS):
        pieces = []
        for model in range(MODEL):
            side, y_rel = divmod(model, 2)
            pieces.append((image_own, image_other)[side][slot_of(place, block, y_rel)])
        begin = block * block_rows
        for kind in range(2):
            weight[begin : begin + block_rows, kind * features : (kind + 1) * features] = (
                jnp.concatenate(
                    [piece[:, kind * width : (kind + 1) * width] for piece in pieces], axis=1
                )
            )


def head_rows(values, head_mask):
    stacked = jnp.concatenate([values] * (WIDE // HEAD), axis=0)
    return jnp.where(head_mask, stacked, jnp.zeros_like(stacked))


def fold_heads(values, head_mask):
    kept = jnp.where(head_mask, values, 0.0)
    count = WIDE // HEAD
    size = values.shape[0] // count
    total = kept[:size]
    for index in range(1, count):
        total = total + kept[index * size : (index + 1) * size]
    return total


def query_head_mask():
    shape = (QUERIES * (WIDE // HEAD), WIDE)
    row = lax.broadcasted_iota(jnp.int32, shape, 0)
    column = lax.broadcasted_iota(jnp.int32, shape, 1)
    return lax.shift_right_logical(row, 5) == lax.shift_right_logical(column, 6)


def patch_softmax(queries, keys):
    scores = [dot_nt(*pair) * HEAD ** (-0.5) for pair in zip(queries, keys)]
    column = lax.broadcasted_iota(jnp.int32, scores[0].shape, 1)
    return softmax([jnp.where(column < PATCHES, each, MASK_VALUE) for each in scores])


def query_rows(values):
    items = values.shape[0] // SEQ
    return jnp.concatenate(
        [values[item * SEQ : item * SEQ + QUERIES] for item in range(items)], axis=0
    )


def look_kernel(
    place,
    feats,
    image_own,
    image_other,
    first_in,
    norm,
    w_cross,
    w_cross_out,
    key_values,
    second_in,
    queries,
    heads,
    weight,
    even,
    odd,
):
    features = first_in.shape[1]
    patches = feats.shape[1]
    step, steps = pl.program_id(0), pl.num_programs(0)

    @pl.when(step == 0)
    def _():
        assemble_image(place, image_own, image_other, weight)
        normed, _ = normalise(query_rows(first_in[...]))
        one_query = normed * norm[0:1, :] + norm[1:2, :]
        second_in[...] = one_query
        queries[...] = dot_nn(one_query.astype(BF16), w_cross[...]).astype(BF16)
        for held in (even, odd):
            held[...] = jnp.zeros_like(held)

    def project(index, held):
        held[:patches, :] = dot_nn(feats[index], weight[...]).astype(BF16)

    def keep(index, held):
        key_values[index * SLOT : (index + 1) * SLOT, :] = held[...]

    def attend(item, held):
        head_mask = query_head_mask()
        span = pl.ds(pl.multiple_of(item * QUERIES, QUERIES), QUERIES)
        columns = [slice(begin, begin + WIDE) for begin in range(0, features, WIDE)]
        value_columns = [slice(features + each.start, features + each.stop) for each in columns]
        expanded = [head_rows(queries[span, each], head_mask) for each in columns]
        probs = patch_softmax(expanded, [held[:, each] for each in columns])
        mixed = [
            dot_nn(prob.astype(BF16), held[:, each]) for prob, each in zip(probs, value_columns)
        ]
        for each, values in zip(columns, mixed):
            heads[span, each] = fold_heads(values, head_mask).astype(BF16)

    @pl.when(step < steps - 1)
    def _():
        project(0, even)
        attend(jnp.maximum(2 * step - 1, 0), odd)
        keep(0, even)
        project(1, odd)
        attend(2 * step, even)
        keep(1, odd)

    @pl.when(step == steps - 1)
    def _():
        attend(2 * step - 1, odd)
        second_in[...] += dot_nn(heads[...], w_cross_out[...])


def gelu_cumulative(inputs):
    return 0.5 * (1.0 + lax.erf(inputs * 0.7071067811865476))


def feed_kernel(
    place,
    lengths,
    norm,
    first_hbm,
    second_hbm,
    out_grad_hbm,
    up_first,
    down_first,
    up_last,
    down_last,
    up_first_other,
    down_first_other,
    up_last_other,
    down_last_other,
    block_out,
    two_grad,
    keep_hbm,
    send_hbm,
    norm_grads,
    first_in,
    second_in,
    out_grad,
    w_up,
    w_down,
    two_rows,
    pre_act,
    result,
    keep,
    send,
    in_sem,
    up_sem,
    down_sem,
    keep_sem,
    send_sem,
    out_sem,
):
    rows, features = first_in.shape
    items = rows // SEQ
    hidden_width = up_first.shape[3]
    piece_rows = up_first.shape[2]
    half = 2 * hidden_width
    up_parts = ((up_first, up_last), (up_first_other, up_last_other))
    down_parts = ((down_first, down_last), (down_first_other, down_last_other))

    def put(target, source, begin, width, semaphore):
        columns = pl.ds(begin, width)
        copy = pltpu.make_async_copy(source.at[:, columns], target.at[:, columns], semaphore)
        copy.start()
        return copy

    entries = [
        pltpu.make_async_copy(source, target, in_sem.at[index])
        for index, (source, target) in enumerate(
            ((first_hbm, first_in), (second_hbm, second_in), (out_grad_hbm, out_grad))
        )
    ]
    entries[0].start()
    entries[1].start()
    for first in range(2):

        @pl.when(place[0] == first)
        def _():
            for model in range(MODEL):
                side, y_rel = divmod(model, 2)
                for block in range(GROUPS):
                    source = up_parts[side][(block + first) % 2]
                    pltpu.make_async_copy(
                        source.at[y_rel, place[GROUPS + block]],
                        w_up.at[model, pl.ds(block * piece_rows, piece_rows), :],
                        up_sem.at[model],
                    ).start()
                for block in range(GROUPS):
                    source = down_parts[side][y_rel]
                    pltpu.make_async_copy(
                        source.at[(block + first) % 2, place[GROUPS + block]],
                        w_down.at[model, pl.ds(block * piece_rows, piece_rows), :],
                        down_sem.at[model],
                    ).start()

    entries[2].start()
    entries[0].wait()
    entries[1].wait()
    copies = []
    normed_one, _ = normalise(first_in[...])
    after_one = normed_one * norm[0:1, :] + norm[1:2, :]
    normed_two, _ = normalise(second_in[...])
    after_two = normed_two * norm[2:3, :] + norm[3:4, :]
    for item in range(items):
        begin = item * SEQ
        two_rows[begin : begin + QUERIES, :] = after_two[item * QUERIES : (item + 1) * QUERIES]
        two_rows[begin + QUERIES : begin + SEQ, :] = after_one[begin + QUERIES : begin + SEQ]
    feed_in = two_rows[...].astype(BF16)
    send[:, 2 * half : 2 * half + features] = feed_in
    copies.append(put(send_hbm, send, 2 * half, features, send_sem.at[4]))
    third_in = two_rows[...]
    for model in range(MODEL):
        side, y_rel = divmod(model, 2)
        target = (keep, send)[side]
        begin = y_rel * hidden_width
        pltpu.make_async_copy(w_up.at[model], w_up.at[model], up_sem.at[model]).wait()
        pre = dot_nn(feed_in, w_up[model])
        pre_act[:, model * hidden_width : (model + 1) * hidden_width] = pre
        act = (pre * gelu_cumulative(pre)).astype(BF16)
        target[:, begin : begin + hidden_width] = act
        semaphore = (keep_sem, send_sem)[side].at[y_rel]
        copies.append(put((keep_hbm, send_hbm)[side], target, begin, hidden_width, semaphore))
        pltpu.make_async_copy(w_down.at[model], w_down.at[model], down_sem.at[model]).wait()
        third_in = third_in + dot_nn(act, w_down[model])
    normed, inverse = normalise(third_in)
    result[...] = (normed * norm[4:5, :] + norm[5:6, :]).astype(BF16)
    copies.append(pltpu.make_async_copy(result, block_out, out_sem.at[0]))
    copies[-1].start()
    entries[2].wait()
    position = lax.broadcasted_iota(jnp.int32, (SEQ, features), 0)
    slope = jnp.concatenate(
        [
            jnp.where(
                position < lengths[item] + QUERIES,
                out_grad[item * SEQ : (item + 1) * SEQ, :].astype(F32),
                0.0,
            )
            for item in range(items)
        ],
        axis=0,
    )
    norm_grads[...] = jnp.zeros_like(norm_grads)
    norm_grads[4:5, :] = jnp.sum(slope * normed, axis=0, keepdims=True)
    norm_grads[5:6, :] = jnp.sum(slope, axis=0, keepdims=True)
    third_grad = norm_back(slope, normed, inverse, norm[4:5, :])
    grad_rows = third_grad.astype(BF16)
    send[:, 2 * half + features :] = grad_rows
    copies.append(put(send_hbm, send, 2 * half + features, features, send_sem.at[5]))
    total = third_grad
    for model in range(MODEL):
        side, y_rel = divmod(model, 2)
        target = (keep, send)[side]
        begin = half + y_rel * hidden_width
        pre = pre_act[:, model * hidden_width : (model + 1) * hidden_width]
        density = jnp.exp(-0.5 * pre * pre) * 0.3989422804014327
        slope_part = gelu_cumulative(pre) + pre * density
        grad_pre = (dot_nt(grad_rows, w_down[model]) * slope_part).astype(BF16)
        target[:, begin : begin + hidden_width] = grad_pre
        semaphore = (keep_sem, send_sem)[side].at[2 + y_rel]
        copies.append(put((keep_hbm, send_hbm)[side], target, begin, hidden_width, semaphore))
        total = total + dot_nt(grad_pre, w_up[model])
    two_rows[...] = total
    copies.append(pltpu.make_async_copy(two_rows, two_grad, out_sem.at[1]))
    copies[-1].start()
    for copy in copies:
        copy.wait()


def put_left(place, block, y_rel, keep, send, value):
    for along_x, target in ((0, keep), (1, send)):

        @pl.when(place[block] == along_x)
        def _(target=target):
            target[y_rel, place[GROUPS + block]] = value


def put_right(place, block, y_rel, keep, send, value):
    (keep, send)[y_rel][place[block], place[GROUPS + block]] = value


def feed_grad_kernel(
    place, hidden, rows, hidden_other, rows_other, left_keep, left_send, right_keep, right_send
):
    piece_rows = left_keep.shape[2]
    kind, y_step = pl.program_id(0), pl.program_id(1)

    @pl.when(kind == 0)
    def _():
        grad_up = dot_tn(rows[...], hidden[...])
        grad_up = (grad_up + dot_tn(rows_other[...], hidden_other[...])).astype(BF16)
        for block in range(GROUPS):
            span = slice(block * piece_rows, (block + 1) * piece_rows)
            put_left(place, block, y_step, left_keep, left_send, grad_up[span])

    for y_rel in range(2):

        @pl.when((kind == 1) & (y_step == y_rel))
        def _(y_rel=y_rel):
            grad_down = dot_tn(hidden[...], rows[...])
            grad_down = (grad_down + dot_tn(hidden_other[...], rows_other[...])).astype(BF16)
            for block in range(GROUPS):
                span = slice(block * piece_rows, (block + 1) * piece_rows)
                put_right(place, block, y_rel, right_keep, right_send, grad_down[span])


def cross_backward_kernel(
    two_grad,
    first_in,
    second_in,
    norm,
    w_cross,
    w_cross_out,
    queries,
    heads,
    key_values,
    norm_grads_in,
    keep,
    send,
    one_query_grad,
    norm_grads,
    head_grads,
    query_grads,
    grad_rows,
):
    features = first_in.shape[1]
    half = features // 2
    count = queries.shape[0]
    step = pl.program_id(0)
    items = pl.num_programs(0) - 3
    scale = HEAD ** (-0.5)

    @pl.when(step == 0)
    def _():
        two_query = query_rows(two_grad[...])
        normed, inverse = normalise(second_in[...])
        norm_grads[...] = norm_grads_in[...]
        norm_grads[2:3, :] = jnp.sum(two_query * normed, axis=0, keepdims=True)
        norm_grads[3:4, :] = jnp.sum(two_query, axis=0, keepdims=True)
        second_grad = norm_back(two_query, normed, inverse, norm[2:3, :])
        one_query_grad[...] = second_grad
        grad_rows[...] = second_grad.astype(BF16)
        head_grads[...] = dot_nt(grad_rows[...], w_cross_out[...]).astype(BF16)

    @pl.when(step < items)
    def _():
        head_mask = query_head_mask()
        span = pl.ds(pl.multiple_of(step * QUERIES, QUERIES), QUERIES)
        columns = [slice(begin, begin + WIDE) for begin in range(0, features, WIDE)]
        keys = [key_values[:, each] for each in columns]
        value_rows = [
            key_values[:, features + each.start : features + each.stop] for each in columns
        ]
        expanded = [head_rows(queries[span, each], head_mask) for each in columns]
        slopes = [head_rows(head_grads[span, each], head_mask) for each in columns]
        grad_probs = [dot_nt(*pair) for pair in zip(slopes, value_rows)]
        probs = patch_softmax(expanded, keys)
        inner = [
            jnp.sum(each * prob, axis=-1, keepdims=True) for each, prob in zip(grad_probs, probs)
        ]
        grad_scores = [
            (prob * (each - total)).astype(BF16)
            for prob, each, total in zip(probs, grad_probs, inner)
        ]
        grad_values = [
            dot_tn(prob.astype(BF16), slope).astype(BF16) for prob, slope in zip(probs, slopes)
        ]
        grad_keys = [
            (dot_tn(*pair) * scale).astype(BF16) for pair in zip(grad_scores, expanded)
        ]
        grad_queries = [dot_nn(*pair) for pair in zip(grad_scores, keys)]
        for index, each in enumerate(columns):
            query_grads[span, each] = (
                fold_heads(grad_queries[index], head_mask) * scale
            ).astype(BF16)
            for part in range(0, WIDE, WIDE // 2):
                side, place_at = divmod(each.start + part, half)
                target, lanes = (keep, send)[side], slice(part, part + WIDE // 2)
                target[:, place_at : place_at + WIDE // 2] = grad_keys[index][:, lanes]
                place_at += half
                target[:, place_at : place_at + WIDE // 2] = grad_values[index][:, lanes]

    @pl.when(step >= items)
    def _():
        for target in (keep, send):
            target[count:, :] = jnp.zeros((SLOT - count, features), BF16)

    @pl.when(step == items)
    def _():
        normed_one, _ = normalise(query_rows(first_in[...]))
        query_in = (normed_one * norm[0:1, :] + norm[1:2, :]).astype(BF16)
        for target in (keep, send):
            target[:count, :] = query_in

    @pl.when(step == items + 1)
    def _():
        for target in (keep, send):
            target[:count, :] = grad_rows[...]

    @pl.when(step == items + 2)
    def _():
        for side, target in enumerate((keep, send)):
            columns = slice(side * half, (side + 1) * half)
            target[:count, :half] = query_grads[:, columns]
            target[:count, half:] = heads[:, columns]
        one_query_grad[...] += dot_nt(query_grads[...], w_cross[...])


def image_grad_kernel(
    count,
    place,
    feats,
    keep_rows,
    other_rows,
    keep,
    other,
    left_keep,
    left_send,
    right_keep,
    right_send,
    total,
    spread,
):
    features = keep.shape[1]
    half = features // 2
    width = half // 2
    image_rows = feats.shape[2] // GROUPS
    image_half = image_rows // 2
    block_rows = features // GROUPS
    out_rows = width // GROUPS
    split = left_keep.shape[2]
    step, steps = pl.program_id(0), pl.num_programs(0)

    @pl.when(step == 0)
    def _():
        spread[...] = jnp.zeros_like(spread)

    for item in range(feats.shape[0]):
        spread[item * SLOT : item * SLOT + feats.shape[1], :] = feats[item]

    @pl.when(step == 0)
    def _():
        total[...] = dot_tn(spread[...], keep_rows[...])

    @pl.when((step > 0) & (step < steps // 2))
    def _():
        total[...] += dot_tn(spread[...], keep_rows[...])

    @pl.when(step >= steps // 2)
    def _():
        total[...] += dot_tn(spread[...], other_rows[...])

    @pl.when(step == steps - 1)
    def _():
        inputs, slopes = slice(0, count), slice(SLOT, SLOT + count)
        parts = slice(2 * SLOT, 2 * SLOT + count)
        grad_query = dot_tn(keep[inputs, :], keep[parts, :half]) + dot_tn(
            other[inputs, :], other[parts, :half]
        )
        grad_out = dot_tn(keep[parts, half:], keep[slopes, :]) + dot_tn(
            other[parts, half:], other[slopes, :]
        )
        for block in range(GROUPS):
            for y_rel in range(2):
                columns = slice(y_rel * width, (y_rel + 1) * width)
                image_part = [
                    total[
                        begin : begin + image_half,
                        kind + y_rel * width : kind + (y_rel + 1) * width,
                    ]
                    for begin in (block * image_rows, block * image_rows + image_half)
                    for kind in (0, half)
                ]
                begin = block * block_rows
                cross_part = [
                    grad_query[begin + part * out_rows : begin + (part + 1) * out_rows, columns]
                    for part in range(MODEL)
                ]
                begin = y_rel * width + block * out_rows
                piece = jnp.concatenate(
                    [
                        jnp.concatenate(image_part, axis=1),
                        jnp.concatenate(cross_part, axis=1),
                        grad_out[begin : begin + out_rows],
                    ],
                    axis=0,
                )
                put_left(place, block, y_rel, left_keep, left_send, piece[:split].astype(BF16))
                put_right(place, block, y_rel, right_keep, right_send, piece[split:].astype(BF16))


def self_backward_kernel(
    lengths,
    one_query_grad,
    two_grad,
    first_in,
    norm,
    hidden,
    qkv,
    heads,
    w_qkv,
    w_self_out,
    norm_grads_in,
    input_grad,
    keep,
    send,
    norm_total,
    one_grad,
    head_grads,
    grad_qkv,
):
    rows, features = hidden.shape
    items = rows // SEQ
    half = features // 2
    for item in range(items):
        begin = item * SEQ
        one_grad[begin : begin + QUERIES, :] = one_query_grad[
            item * QUERIES : (item + 1) * QUERIES, :
        ]
        one_grad[begin + QUERIES : begin + SEQ, :] = two_grad[begin + QUERIES : begin + SEQ, :]
    normed, inverse = normalise(first_in[...])
    gradient = one_grad[...]
    norm_sum = norm_grads_in[...] + jnp.concatenate(
        [
            jnp.sum(gradient * normed, axis=0, keepdims=True),
            jnp.sum(gradient, axis=0, keepdims=True),
            jnp.zeros((NORM_ROWS - 2, features), F32),
        ],
        axis=0,
    )
    norm_total[...] = norm_sum
    first_grad = norm_back(gradient, normed, inverse, norm[0:1, :])
    one_grad[...] = first_grad
    grad_rows = first_grad.astype(BF16)
    head_grads[...] = dot_nt(grad_rows, w_self_out[...]).astype(BF16)
    scale = HEAD ** (-0.5)
    for begin in range(0, rows, BLOCK):
        span = slice(begin, begin + BLOCK)
        mask = block_mask(lengths, begin // SEQ)
        for first in range(0, features // HEAD, HEADS_AT_ONCE):
            chosen = range(first, first + HEADS_AT_ONCE)
            queries, key_rows, value_rows = [
                [
                    qkv[span, kind * features + head * HEAD : kind * features + (head + 1) * HEAD]
                    for head in chosen
                ]
                for kind in range(3)
            ]
            slopes = [head_grads[span, head * HEAD : (head + 1) * HEAD] for head in chosen]
            scores = [dot_nt(*pair) for pair in zip(queries, key_rows)]
            grad_probs = [dot_nt(*pair) for pair in zip(slopes, value_rows)]
            probs = softmax([jnp.where(mask, each * scale, MASK_VALUE) for each in scores])
            inner = [
                jnp.sum(each * prob, axis=-1, keepdims=True)
                for each, prob in zip(grad_probs, probs)
            ]
            grad_scores = [
                (prob * (each - total)).astype(BF16)
                for prob, each, total in zip(probs, grad_probs, inner)
            ]
            results = (
                [dot_nn(*pair) * scale for pair in zip(grad_scores, key_rows)],
                [dot_tn(*pair) * scale for pair in zip(grad_scores, queries)],
                [dot_tn(prob.astype(BF16), slope) for prob, slope in zip(probs, slopes)],
            )
            for kind in range(3):
                begin_at = kind * features + first * HEAD
                grad_qkv[span, begin_at : begin_at + HEADS_AT_ONCE * HEAD] = jnp.concatenate(
                    [each.astype(BF16) for each in results[kind]], axis=1
                )
    total = one_grad[...]
    for kind in range(3):
        columns = slice(kind * features, (kind + 1) * features)
        total = total + dot_nt(grad_qkv[:, columns], w_qkv[:, columns])
        first = kind * features
        keep[:, kind * half : (kind + 1) * half] = grad_qkv[:, first : first + half]
        send[:rows, kind * half : (kind + 1) * half] = grad_qkv[:, first + half : first + features]
    input_grad[...] = total.astype(BF16)
    keep[:, 3 * half :] = heads[:, :half]
    send[:rows, 3 * half : 4 * half] = heads[:, half:]
    send[:rows, 4 * half : 6 * half] = hidden[...]
    send[:rows, 6 * half :] = grad_rows
    send[rows:, :] = jnp.zeros((send.shape[0] - rows, send.shape[1]), BF16)
    send[rows : rows + 16, :features] = jnp.concatenate(
        [norm_sum, jnp.zeros_like(norm_sum)], axis=0
    ).astype(BF16)


def self_grad_kernel(
    place, keep, send, other, norm_total, left_keep, left_send, right_keep, right_send
):
    features = norm_total.shape[1]
    rows = keep.shape[0]
    half = features // 2
    width = half // 2
    block_rows = features // GROUPS
    out_rows = width // GROUPS
    split = left_keep.shape[2]
    inputs, slopes = slice(4 * half, 6 * half), slice(6 * half, 8 * half)
    columns = slice(0, 3 * half)
    grad_in = dot_tn(send[:rows, inputs], keep[:, columns])
    grad_in = grad_in + dot_tn(other[:rows, inputs], other[:rows, columns])
    columns = slice(3 * half, 4 * half)
    grad_out = dot_tn(keep[:, columns], send[:rows, slopes])
    grad_out = grad_out + dot_tn(other[:rows, columns], other[:rows, slopes])
    norm_rows = norm_total[...] + other[rows : rows + 16, :features].astype(F32)[:NORM_ROWS]
    for block in range(GROUPS):
        span = slice(block * block_rows, (block + 1) * block_rows)
        for y_rel in range(2):
            pieces = [
                grad_in[span, kind * half + y_rel * width : kind * half + (y_rel + 1) * width]
                for kind in range(3)
            ]
            begin = y_rel * width + block * out_rows
            out_part = grad_out[begin : begin + out_rows]
            pieces.append(
                jnp.concatenate(
                    [out_part[:, part * width : (part + 1) * width] for part in range(MODEL)],
                    axis=0,
                )
            )
            piece = jnp.concatenate([jnp.concatenate(pieces, axis=1), norm_rows], axis=0)
            put_left(place, block, y_rel, left_keep, left_send, piece[:split].astype(BF16))
            put_right(place, block, y_rel, right_keep, right_send, piece[split:].astype(BF16))


def adam_step(weight, moment_one, moment_two, gradient, decay_rate):
    moment_one = BETA_ONE * moment_one + (1.0 - BETA_ONE) * gradient
    moment_two = BETA_TWO * moment_two + (1.0 - BETA_TWO) * gradient * gradient
    update = (
        moment_one
        / (1.0 - BETA_ONE**STEP)
        / (jnp.sqrt(moment_two / (1.0 - BETA_TWO**STEP)) + ADAM_EPSILON)
        + decay_rate * weight
    )
    return moment_one, moment_two, update


def place_sums(target, sums):
    column = lax.broadcasted_iota(jnp.int32, (1, LANES), 1)
    rows = []
    for kind in range(2):
        row = jnp.zeros((1, LANES), F32)
        for index, pair in sums.items():
            row = jnp.where(column == index, pair[kind], row)
        rows.append(row)
    target[...] = jnp.concatenate(rows, axis=0)


def sum_pair(weight, update):
    return jnp.sum(weight * weight), jnp.sum(update * update)


def feed_update_kernel(
    gradient,
    up,
    up_moments,
    down,
    down_moments,
    up_next,
    down_next,
    up_update,
    down_update,
    squares,
):
    rows = up.shape[0]
    sums = {}
    for index, weight, moments, following, result, span in (
        (8, up, up_moments, up_next, up_update, slice(0, rows)),
        (9, down, down_moments, down_next, down_update, slice(rows, None)),
    ):
        following[0], following[1], update = adam_step(
            weight[...], moments[0], moments[1], gradient[span, :], DECAY_RATE
        )
        result[...] = update
        sums[index] = sum_pair(weight[...], update)
    place_sums(squares, sums)


def image_update_kernel(gradient, weight, moments, following, result, squares):
    width = weight.shape[2]
    half = weight.shape[1] // 2
    sums = {}
    for kind in range(2):
        parts = []
        for part in range(2):
            span = slice(part * half, (part + 1) * half)
            lanes = slice((2 * part + kind) * width, (2 * part + kind + 1) * width)
            following[0, kind, span, :], following[1, kind, span, :], update = adam_step(
                weight[kind, span, :],
                moments[0, kind, span, :],
                moments[1, kind, span, :],
                gradient[:half, lanes],
                DECAY_RATE,
            )
            result[kind, span, :] = update
            parts.append(sum_pair(weight[kind, span, :], update))
        sums[6 + kind] = tuple(left + right for left, right in zip(*parts))
    place_sums(squares, sums)


def last_update_kernel(
    gradient,
    cross_gradient,
    norm_gradient,
    inward,
    inward_moments,
    outward,
    outward_moments,
    norm,
    norm_moments,
    inward_next,
    outward_next,
    norm_next,
    inward_update,
    outward_update,
    norm_update,
    squares,
):
    own_in, width = inward.shape[1:]
    own_out = outward.shape[1]
    cross_rows = cross_gradient.shape[0] - 2 * own_out
    cross_query = cross_gradient[cross_rows : cross_rows + own_out, :]
    gradients = [gradient[:own_in, kind * width : (kind + 1) * width] for kind in range(3)]
    gradients.append(
        jnp.concatenate(
            [cross_query[:, part * width : (part + 1) * width] for part in range(MODEL)], axis=0
        )
    )
    sums = {}
    for kind in range(4):
        inward_next[0, kind], inward_next[1, kind], update = adam_step(
            inward[kind],
            inward_moments[0, kind],
            inward_moments[1, kind],
            gradients[kind],
            DECAY_RATE,
        )
        inward_update[kind] = update
        sums[kind] = sum_pair(inward[kind], update)
    folded = gradient[:own_in, 3 * width :]
    self_out = jnp.concatenate(
        [folded[part * own_out : (part + 1) * own_out] for part in range(MODEL)], axis=1
    )
    for kind, part in enumerate((self_out, cross_gradient[cross_rows + own_out :, :])):
        outward_next[0, kind], outward_next[1, kind], update = adam_step(
            outward[kind], outward_moments[0, kind], outward_moments[1, kind], part, DECAY_RATE
        )
        outward_update[kind] = update
        sums[4 + kind] = sum_pair(outward[kind], update)
    norm_next[0], norm_next[1], update = adam_step(
        norm[...], norm_moments[0], norm_moments[1], norm_gradient[...], 0.0
    )
    norm_update[...] = update
    for kind in range(norm.shape[0]):
        sums[10 + kind] = sum_pair(norm[kind : kind + 1, :], update[kind : kind + 1, :])
    place_sums(squares, sums)


def apply_kernel(squares, *refs):
    groups = len(refs) // 5
    weights, averages, updates = refs[:groups], refs[groups : 2 * groups], refs[2 * groups : 3 * groups]
    new_weights, new_averages = refs[3 * groups : 4 * groups], refs[4 * groups : 5 * groups]
    trust_out, norms_out = refs[5 * groups :]
    sums = jnp.sum(squares[...], axis=0)
    trust = jnp.sqrt(sums[0:1]) * lax.rsqrt(sums[1:2] + SQUARE_EPSILON)
    trust_out[...] = trust
    norms_out[...] = jnp.sqrt(sums)
    column = lax.broadcasted_iota(jnp.int32, trust.shape, 1)

    def ratio(index):
        return jnp.sum(jnp.where(column == index, trust, 0.0), axis=1, keepdims=True)

    index = 0
    for weight, average, update, new_weight, new_average in zip(
        weights, averages, updates, new_weights, new_averages
    ):
        if len(weight.shape) == 3:
            spans = list(range(weight.shape[0]))
        elif weight.shape[0] == 6:
            spans = [slice(row, row + 1) for row in range(6)]
        else:
            spans = [slice(None)]
        for span in spans:
            value = weight[span] - LEARN_RATE * ratio(index) * update[span]
            new_weight[span] = value
            new_average[span] = AVERAGE_RATE * average[span] + (1.0 - AVERAGE_RATE) * value
            index += 1


SCALARS = pl.BlockSpec(memory_space=pltpu.SMEM)
WHOLE = pl.BlockSpec(memory_space=pltpu.VMEM)


def local_call(kernel, scalars, arrays, out_shapes, scratch, flops, name, limit):
    size = sum(a.size * a.dtype.itemsize for a in arrays)
    size += sum(a.size * a.dtype.itemsize for a in out_shapes)
    return pl.pallas_call(
        kernel,
        out_shape=tuple(out_shapes),
        in_specs=[SCALARS] * len(scalars) + [WHOLE] * len(arrays),
        out_specs=tuple([WHOLE] * len(out_shapes)),
        scratch_shapes=scratch,
        compiler_params=pltpu.CompilerParams(vmem_limit_bytes=limit * MIB),
        cost_estimate=pl.CostEstimate(flops=flops, bytes_accessed=size, transcendentals=0),
        name=name,
    )(*scalars, *arrays)


def shape_of(*dims, dtype=BF16):
    return jax.ShapeDtypeStruct(dims, dtype)


def part_shapes(left_rows, right_rows, features):
    left, right = shape_of(2, 4, left_rows, features), shape_of(2, 4, right_rows, features)
    return left, left, right, right


def like(array):
    return jax.ShapeDtypeStruct(array.shape, array.dtype)


def update_call(kernel, arrays, moments, weights, name):
    shapes = [like(each) for each in (*moments, *weights)] + [shape_of(2, LANES, dtype=F32)]
    return local_call(kernel, (), arrays, shapes, [], 0, name, 20)


def apply_call(squares, weights, averages, updates):
    shapes = [like(each) for each in (*weights, *averages)]
    shapes += [shape_of(1, LANES, dtype=F32), shape_of(2, LANES, dtype=F32)]
    return local_call(
        apply_kernel, (), (squares, *weights, *averages, *updates), shapes, [], 0, "apply", 60
    )


class Direct:
    def __init__(self, dp, mp):
        self.count = dp * mp
        self.mp = mp
        self.depth = dp // 2
        index = lax.axis_index("dp")
        block = jnp.arange(GROUPS, dtype=jnp.int32)
        along_x = (block % 2) ^ (index % 2)
        along_z = (index // 2 - block // 2) % self.depth
        self.place = jnp.concatenate([along_x, along_z]).astype(jnp.int32)

    def hop(self, values, flip):
        return lax.ppermute(values, AXES, [(i, i ^ flip) for i in range(self.count)])

    def hop_core(self, values):
        return self.hop(values, 1)

    def hop_y(self, values):
        return self.hop(values, 2)

    def hop_x(self, values):
        return self.hop(values, self.mp)

    def hop_z(self, values, distance):
        step = 2 * self.mp * distance
        return lax.ppermute(values, AXES, [(i, (i + step) % self.count) for i in range(self.count)])

    def spread_z(self, piece):
        return jnp.stack([piece] + [self.hop_z(piece, step) for step in range(1, self.depth)])


    def spread_first(self, held, split):
        return self.hop_y(held[:, :split]), self.hop_x(held[:, split:])

    def join_first(self, held, split, others):
        return jnp.stack([held[:, :split], others[0]]), jnp.stack([held[:, split:], others[1]])

    def spread_second(self, parts):
        return self.hop_x(parts[0]), self.hop_y(parts[1])

    def join_second(self, parts, others):
        left = jnp.stack([parts[0], others[0]])
        right = jnp.stack([parts[1], others[1]]).transpose(1, 0, 2, 3, 4)
        whole = jnp.concatenate([left, right], axis=3)
        return whole.reshape(SLOTS, *whole.shape[3:])


    def fold_first(self, grads):
        return self.hop_x(grads[1]), self.hop_y(grads[3])

    def fold_second(self, grads, others):
        return (
            self.hop_y(total([grads[0][1], others[0][1]])),
            self.hop_x(total([grads[2][1], others[1][1]])),
        )

    def kept(self, grads, others, last):
        return [[grads[2 * side][0], others[side][0], last[side]] for side in range(2)]

    def fold_z(self, sides):
        return [
            self.hop_z(total(*[[part[step] for part in parts] for parts in sides]), -step)
            for step in range(1, self.depth)
        ]

    def ring_z(self, sides, step, carried=None):
        addends = [[part[step] for part in parts] for parts in sides]
        own = total(*addends, dtype=F32)
        if carried is not None:
            own = own + carried.astype(F32)
        return self.hop_z(own.astype(BF16), 1)

    def finish(self, sides, others):
        own = total(*[[part[0] for part in parts] for parts in sides], dtype=F32)
        return total([own, *others], dtype=F32)


def total(*sides, dtype=BF16):
    sums = []
    for parts in sides:
        result = parts[0].astype(F32)
        for part in parts[1:]:
            result = result + part.astype(F32)
        sums.append(result.astype(dtype))
    return sums[0] if len(sums) == 1 else jnp.concatenate(sums, axis=0)


class Plain:
    def __init__(self, dp, mp):
        self.dp = dp
        self.mp = mp
        self.side = lax.axis_index("mp") // 2
        block = jnp.arange(GROUPS, dtype=jnp.int32)
        self.place = jnp.concatenate([block % 2, block // 2]).astype(jnp.int32)

    def hop_core(self, values):
        count = self.dp * self.mp
        return lax.ppermute(values, AXES, [(i, i ^ 2) for i in range(count)])

    def collect(self, piece):
        rows, width = piece.shape
        blocks = lax.all_gather(piece, AXES, axis=0).reshape(self.dp, self.mp, rows, width)
        rows = rows * self.dp // GROUPS
        blocks = blocks.transpose(1, 0, 2, 3).reshape(2, 2, 4, 2, rows, width)
        blocks = blocks.transpose(0, 3, 1, 2, 4, 5).reshape(2, SLOTS, rows, width)
        return jnp.where(self.side == 0, blocks, blocks[::-1])

    def joined(self, grads):
        left = jnp.stack(grads[:2])
        right = jnp.stack(grads[2:]).transpose(1, 0, 2, 3, 4)
        return jnp.concatenate([left, right], axis=3)

    def scatter(self, own):
        rows, width = own.shape[3:]
        own = own.transpose(1, 2, 0, 3, 4).reshape(1, 2, GROUPS, rows, width)
        both = jnp.zeros((2, *own.shape[1:]), F32)
        both = lax.dynamic_update_slice_in_dim(both, own.astype(F32), self.side, 0)
        both = both.reshape(self.mp, self.dp, rows * GROUPS // self.dp, width)
        both = both.transpose(1, 0, 2, 3).reshape(-1, width)
        return lax.psum_scatter(both, AXES, scatter_dimension=0, tiled=True)


def tie(*arrays):
    return lax.optimization_barrier(arrays)


def padded(feats):
    pad = ((0, 0), (0, SLOT - PATCHES), (0, 0))
    return jnp.pad(feats, pad).reshape(-1, feats.shape[2])


def tie(*arrays):
    return lax.optimization_barrier(arrays)


def add(left_side, right_side):
    return (left_side.astype(F32) + right_side.astype(F32)).astype(BF16)


def self_forward(place, lengths, hidden, begin):
    rows, features = hidden.shape
    return local_call(
        self_forward_kernel,
        (place, lengths),
        (hidden, *begin),
        (
            shape_of(rows, features, dtype=F32),
            shape_of(rows, 3 * features),
            shape_of(rows, features),
            shape_of(features, 3 * features),
            shape_of(features, features),
            shape_of(features, features),
            shape_of(features, features),
            shape_of(NORM_ROWS, features, dtype=F32),
        ),
        [pltpu.VMEM((features, features), F32), pltpu.VMEM((features, features), F32)],
        10 * rows * features * features,
        "self_forward",
        28,
    )


def fixed(shape):
    return pl.BlockSpec(shape, lambda *_: (0,) * len(shape))


def look(place, feats, image, first_in, norm, w_cross, w_cross_out):
    items, patches, encoded = feats.shape
    items = items // 2
    rows, features = items * SLOT, first_in.shape[1]
    count = items * QUERIES
    last = items // 2 - 1
    arrays = (*image, first_in, norm, w_cross, w_cross_out)
    return pl.pallas_call(
        look_kernel,
        out_shape=(
            shape_of(rows, 2 * features),
            shape_of(count, features, dtype=F32),
            shape_of(count, features),
            shape_of(count, features),
        ),
        grid_spec=pltpu.PrefetchScalarGridSpec(
            num_scalar_prefetch=1,
            grid=(items // 2 + 1,),
            in_specs=[
                pl.BlockSpec(
                    (2, patches, encoded),
                    lambda step, where: (
                        where[2 * GROUPS] // 2 + jnp.minimum(step, last),
                        0,
                        0,
                    ),
                )
            ]
            + [fixed(each.shape) for each in arrays],
            out_specs=(
                pl.BlockSpec(
                    (2 * SLOT, 2 * features), lambda step, where: (jnp.minimum(step, last), 0)
                ),
                fixed((count, features)),
                fixed((count, features)),
                fixed((count, features)),
            ),
            scratch_shapes=[
                pltpu.VMEM((encoded, 2 * features), BF16),
                pltpu.VMEM((SLOT, 2 * features), BF16),
                pltpu.VMEM((SLOT, 2 * features), BF16),
            ],
        ),
        compiler_params=pltpu.CompilerParams(vmem_limit_bytes=46 * MIB),
        cost_estimate=pl.CostEstimate(
            flops=5 * rows * encoded * features,
            bytes_accessed=2 * rows * (encoded + 2 * features) + 4 * encoded * features,
            transcendentals=0,
        ),
        name="look",
    )(place, feats, *arrays)


def feed(place, lengths, first_in, second_in, norm, out_grad, weights):
    rows, features = first_in.shape
    width = weights[0].shape[3]
    anywhere = pl.BlockSpec(memory_space=pl.ANY)
    return pl.pallas_call(
        feed_kernel,
        out_shape=(
            shape_of(rows, features),
            shape_of(rows, features, dtype=F32),
            shape_of(rows, 4 * width),
            shape_of(rows, 4 * width + 2 * features),
            shape_of(NORM_ROWS, features, dtype=F32),
        ),
        in_specs=[SCALARS, SCALARS, WHOLE] + [anywhere] * (3 + len(weights)),
        out_specs=(anywhere, anywhere, anywhere, anywhere, WHOLE),
        scratch_shapes=[
            pltpu.VMEM(first_in.shape, F32),
            pltpu.VMEM(second_in.shape, F32),
            pltpu.VMEM((rows, features), BF16),
            pltpu.VMEM((MODEL, features, width), BF16),
            pltpu.VMEM((MODEL, width, features), BF16),
            pltpu.VMEM((rows, features), F32),
            pltpu.VMEM((rows, MODEL * width), F32),
            pltpu.VMEM((rows, features), BF16),
            pltpu.VMEM((rows, 4 * width), BF16),
            pltpu.VMEM((rows, 4 * width + 2 * features), BF16),
            pltpu.SemaphoreType.DMA((3,)),
            pltpu.SemaphoreType.DMA((MODEL,)),
            pltpu.SemaphoreType.DMA((MODEL,)),
            pltpu.SemaphoreType.DMA((4,)),
            pltpu.SemaphoreType.DMA((6,)),
            pltpu.SemaphoreType.DMA((2,)),
        ],
        compiler_params=pltpu.CompilerParams(vmem_limit_bytes=58 * MIB),
        cost_estimate=pl.CostEstimate(
            flops=8 * rows * features * MODEL * width,
            bytes_accessed=4 * MODEL * width * features,
            transcendentals=0,
        ),
        name="feed",
    )(place, lengths, norm, first_in, second_in, out_grad, *weights)


def feed_grad(place, keep, send, other, rows):
    features = (send.shape[1] - keep.shape[1]) // 2
    width = keep.shape[1] // 4
    tokens = keep.shape[0]
    shapes = part_shapes(rows, rows, features)
    hidden_spec = pl.BlockSpec(
        (tokens, width), lambda kind, y_step, where: (0, 2 * (1 - kind) + y_step)
    )
    row_spec = pl.BlockSpec(
        (tokens, features), lambda kind, y_step, where: (0, 4 * width // features + kind)
    )
    return pl.pallas_call(
        feed_grad_kernel,
        out_shape=shapes,
        grid_spec=pltpu.PrefetchScalarGridSpec(
            num_scalar_prefetch=1,
            grid=(2, 2),
            in_specs=[hidden_spec, row_spec, hidden_spec, row_spec],
            out_specs=[fixed(shape.shape) for shape in shapes],
        ),
        compiler_params=pltpu.CompilerParams(vmem_limit_bytes=36 * MIB),
        cost_estimate=pl.CostEstimate(
            flops=4 * tokens * features * keep.shape[1],
            bytes_accessed=24 * tokens * features,
            transcendentals=0,
        ),
        name="feed_grad",
    )(place, keep, send, other, other)


def cross_backward(
    two_grad,
    first_in,
    second_in,
    norm,
    w_cross,
    w_cross_out,
    queries,
    heads,
    key_values,
    norm_grads,
):
    features = first_in.shape[1]
    count = queries.shape[0]
    items = key_values.shape[0] // SLOT
    rows = (items + 3) * SLOT
    arrays = (
        two_grad,
        first_in,
        second_in,
        norm,
        w_cross,
        w_cross_out,
        queries,
        heads,
        key_values,
        norm_grads,
    )
    specs = [fixed(each.shape) for each in arrays]
    specs[8] = pl.BlockSpec(
        (SLOT, 2 * features), lambda item: (jnp.minimum(item, items - 1), 0)
    )
    row_spec = pl.BlockSpec((SLOT, features), lambda item: (item, 0))
    return pl.pallas_call(
        cross_backward_kernel,
        grid=(items + 3,),
        out_shape=(
            shape_of(rows, features),
            shape_of(rows, features),
            shape_of(count, features, dtype=F32),
            shape_of(NORM_ROWS, features, dtype=F32),
        ),
        in_specs=specs,
        out_specs=(row_spec, row_spec, fixed((count, features)), fixed((NORM_ROWS, features))),
        scratch_shapes=[pltpu.VMEM((count, features), BF16)] * 3,
        compiler_params=pltpu.CompilerParams(vmem_limit_bytes=36 * MIB),
        cost_estimate=pl.CostEstimate(
            flops=20 * count * features * features,
            bytes_accessed=12 * rows * features,
            transcendentals=0,
        ),
        name="cross_backward",
    )(*arrays)


def image_grad(place, feats, keep, other):
    features = keep.shape[1]
    items, patches, encoded = feats.shape
    rows = items * SLOT
    piece = encoded // GROUPS // 2 + 2 * (features // MODEL // GROUPS)
    steps = 4
    block = rows // steps
    last = steps // 2 - 1
    shapes = part_shapes(IMAGE_SPLIT, piece - IMAGE_SPLIT, features)
    out_specs = [pl.BlockSpec(shape.shape, lambda step, where: (0, 0, 0, 0)) for shape in shapes]
    rest = pl.BlockSpec((4 * SLOT, features), lambda step, where: (items // 8, 0))
    return pl.pallas_call(
        functools.partial(image_grad_kernel, items // 2 * QUERIES),
        out_shape=shapes,
        grid_spec=pltpu.PrefetchScalarGridSpec(
            num_scalar_prefetch=1,
            grid=(steps,),
            in_specs=[
                pl.BlockSpec(
                    (items // steps, patches, encoded),
                    lambda step, where: (
                        (step + where[2 * GROUPS] // (items // steps)) % steps,
                        0,
                        0,
                    ),
                ),
                pl.BlockSpec((block, features), lambda step, where: (jnp.minimum(step, last), 0)),
                pl.BlockSpec(
                    (block, features), lambda step, where: (jnp.maximum(step - last - 1, 0), 0)
                ),
                rest,
                rest,
            ],
            out_specs=out_specs,
            scratch_shapes=[pltpu.VMEM((encoded, features), F32), pltpu.VMEM((block, encoded), BF16)],
        ),
        compiler_params=pltpu.CompilerParams(vmem_limit_bytes=34 * MIB),
        cost_estimate=pl.CostEstimate(
            flops=2 * rows * encoded * features,
            bytes_accessed=2 * rows * (encoded + features),
            transcendentals=0,
        ),
        name="image_grad",
    )(place, feats, keep, other, keep, other)


def self_backward(
    lengths,
    one_query_grad,
    two_grad,
    first_in,
    norm,
    hidden,
    qkv,
    heads,
    w_qkv,
    w_self_out,
    norm_grads,
):
    rows, features = hidden.shape
    return local_call(
        self_backward_kernel,
        (lengths,),
        (
            one_query_grad,
            two_grad,
            first_in,
            norm,
            hidden,
            qkv,
            heads,
            w_qkv,
            w_self_out,
            norm_grads,
        ),
        (
            shape_of(rows, features),
            shape_of(rows, 2 * features),
            shape_of(rows + 16, 4 * features),
            shape_of(NORM_ROWS, features, dtype=F32),
        ),
        [
            pltpu.VMEM((rows, features), F32),
            pltpu.VMEM((rows, features), BF16),
            pltpu.VMEM((rows, 3 * features), BF16),
        ],
        16 * rows * features * features,
        "self_backward",
        30,
    )


def self_grad(place, keep, send, other, norm_total):
    features = norm_total.shape[1]
    rows = features // GROUPS + NORM_ROWS
    return local_call(
        self_grad_kernel,
        (place,),
        (keep, send, other, norm_total),
        part_shapes(SELF_SPLIT, rows - SELF_SPLIT, features),
        [],
        8 * keep.shape[0] * features * features,
        "self_grad",
        24,
    )


def run_direct(hidden, feats, first_item, lengths, out_grad, image, begin, weights):
    moves = Direct(lax.axis_size("dp"), lax.axis_size("mp"))
    place = moves.place
    feats_place = jnp.concatenate([place, first_item[None].astype(jnp.int32)])
    begin_split = begin.shape[0] // 2
    image_split = image.shape[0] * 96 // 176
    feed_split = weights.shape[0] // 2

    begin = moves.spread_z(begin)
    begin, image, feats = tie(begin, image, feats)
    begin_others = moves.spread_first(begin, begin_split)
    image = moves.spread_z(image)
    begin_others, image, weights, feats = tie(begin_others, image, weights, feats)
    begin_parts = moves.join_first(begin, begin_split, begin_others)
    begin_others = moves.spread_second(begin_parts)
    image_others = moves.spread_first(image, image_split)
    weights = moves.spread_z(weights)
    begin_others, image_others, weights = tie(begin_others, image_others, weights)

    image_parts = moves.join_first(image, image_split, image_others)
    image_others = moves.spread_second(image_parts)
    weight_others = moves.spread_first(weights, feed_split)
    begin = moves.join_second(begin_parts, begin_others)
    begin_other = moves.hop_core(begin)
    first_in, qkv, heads, w_qkv, w_cross, w_self_out, w_cross_out, norm = self_forward(
        place, lengths, hidden, (begin, begin_other)
    )
    first_in, image_others, weight_others = tie(first_in, image_others, weight_others)
    image = moves.join_second(image_parts, image_others)
    weight_parts = moves.join_first(weights, feed_split, weight_others)
    image_other = moves.hop_core(image)
    weight_others = moves.spread_second(weight_parts)
    held_others = [moves.hop_core(part) for part in weight_parts]
    key_values, second_in, cross_queries, cross_heads = look(
        feats_place, feats, (image, image_other), first_in, norm, w_cross, w_cross_out
    )
    second_in, weight_others, held_others = tie(second_in, weight_others, held_others)
    last_others = [moves.hop_core(part) for part in weight_others]
    gathered = (*weight_parts, *weight_others, *held_others, *last_others)
    block_out, two_grad, feed_keep, feed_send, norm_grads = feed(
        place, lengths, first_in, second_in, norm, out_grad, gathered
    )

    feed_other = moves.hop_core(feed_send)
    cross_keep, cross_send, one_query_grad, norm_grads = cross_backward(
        two_grad,
        first_in,
        second_in,
        norm,
        w_cross,
        w_cross_out,
        cross_queries,
        cross_heads,
        key_values,
        norm_grads,
    )
    cross_send, feed_other = tie(cross_send, feed_other)
    cross_other = moves.hop_core(cross_send)
    feed_grads = feed_grad(place, feed_keep, feed_send, feed_other, feed_split)
    cross_other, feed_grads = tie(cross_other, feed_grads)
    feed_first = moves.fold_first(feed_grads)
    image_grads = image_grad(feats_place, feats, cross_keep, cross_other)
    one_query_grad, image_grads, feed_first = tie(one_query_grad, image_grads, feed_first)
    feed_second = moves.fold_second(feed_grads, feed_first)
    image_first = moves.fold_first(image_grads)
    input_grad, self_keep, self_send, norm_total = self_backward(
        lengths,
        one_query_grad,
        two_grad,
        first_in,
        norm,
        hidden,
        qkv,
        heads,
        w_qkv,
        w_self_out,
        norm_grads,
    )
    self_send, image_first, feed_second = tie(self_send, image_first, feed_second)
    self_other = moves.hop_core(self_send)
    feed_kept = moves.kept(feed_grads, feed_first, feed_second)
    feed_other = moves.ring_z(feed_kept, 1)
    image_second = moves.fold_second(image_grads, image_first)
    self_grads = self_grad(place, self_keep, self_send, self_other, norm_total)
    self_grads, feed_other = tie(self_grads, feed_other)
    self_first = moves.fold_first(self_grads)
    feed_other = moves.ring_z(feed_kept, 2, feed_other)
    feed_other, image_second = tie(feed_other, image_second)
    image_kept = moves.kept(image_grads, image_first, image_second)
    feed_other = moves.ring_z(feed_kept, 3, feed_other)
    image_other = moves.ring_z(image_kept, 1)
    self_first, image_other, feed_other = tie(self_first, image_other, feed_other)
    self_second = moves.fold_second(self_grads, self_first)
    image_other = moves.ring_z(image_kept, 2, image_other)
    feed_sum = moves.finish(feed_kept, [feed_other])
    image_other, self_second = tie(image_other, self_second)
    image_other = moves.ring_z(image_kept, 3, image_other)
    self_kept = moves.kept(self_grads, self_first, self_second)
    self_others = moves.fold_z(self_kept)
    image_sum = moves.finish(image_kept, [image_other])
    in_sum = moves.finish(self_kept, self_others)
    return block_out, input_grad, in_sum, image_sum, feed_sum


def run_plain(hidden, feats, first_item, lengths, out_grad, image, begin, weights):
    moves = Plain(lax.axis_size("dp"), lax.axis_size("mp"))
    place = moves.place
    feats_place = jnp.concatenate([place, first_item[None].astype(jnp.int32)])
    features = hidden.shape[1]
    width = features // MODEL
    block_rows, out_rows = features // GROUPS, width // GROUPS
    own_in, own_out = block_rows * GROUPS // moves.dp, out_rows * GROUPS // moves.dp
    half = block_rows // 2
    part = begin.shape[0] - NORM_ROWS
    inward = moves.collect(begin[:own_in])
    cross_out = moves.collect(begin[own_in : own_in + own_out])
    self_out = moves.collect(begin[own_in + own_out : part])
    norm_all = lax.psum(begin[part:].astype(F32), AXES).astype(BF16)
    norm_first = jnp.zeros((2, SLOTS, NORM_ROWS, features), BF16).at[0, 0].set(norm_all)
    begin = jnp.concatenate(
        [
            inward[:, :, :half],
            cross_out,
            jnp.zeros_like(norm_first),
            inward[:, :, half:],
            self_out,
            norm_first,
        ],
        axis=2,
    )
    image = moves.collect(image)
    own_up = weights.shape[0] // 2
    ups, downs = [
        moves.collect(part).reshape(2, 2, 2, 4, -1, features)
        for part in (weights[:own_up], weights[own_up:])
    ]
    gathered = tuple(
        part
        for side in range(2)
        for last in range(2)
        for part in (ups[side, last], downs[side, :, last])
    )
    first_in, qkv, heads, w_qkv, w_cross, w_self_out, w_cross_out, norm = self_forward(
        place, lengths, hidden, (begin[0], begin[1])
    )
    key_values, second_in, cross_queries, cross_heads = look(
        feats_place, feats, (image[0], image[1]), first_in, norm, w_cross, w_cross_out
    )
    block_out, two_grad, feed_keep, feed_send, norm_grads = feed(
        place, lengths, first_in, second_in, norm, out_grad, gathered
    )
    feed_half = gathered[0].shape[2]
    feed_grads = feed_grad(place, feed_keep, feed_send, moves.hop_core(feed_send), feed_half)
    cross_keep, cross_send, one_query_grad, norm_grads = cross_backward(
        two_grad,
        first_in,
        second_in,
        norm,
        w_cross,
        w_cross_out,
        cross_queries,
        cross_heads,
        key_values,
        norm_grads,
    )
    image_grads = image_grad(feats_place, feats, cross_keep, moves.hop_core(cross_send))
    input_grad, self_keep, self_send, norm_total = self_backward(
        lengths,
        one_query_grad,
        two_grad,
        first_in,
        norm,
        hidden,
        qkv,
        heads,
        w_qkv,
        w_self_out,
        norm_grads,
    )
    self_grads = self_grad(place, self_keep, self_send, moves.hop_core(self_send), norm_total)

    def beside(values):
        count = values.shape[-2] // MODEL
        return jnp.concatenate(
            [values[..., part * count : (part + 1) * count, :] for part in range(MODEL)], axis=-1
        )

    def below(values):
        count = values.shape[-1] // MODEL
        return jnp.concatenate(
            [values[..., part * count : (part + 1) * count] for part in range(MODEL)], axis=-2
        )

    grads = moves.joined(self_grads)
    in_part = moves.scatter(grads[..., :block_rows, : 3 * width])
    self_out = moves.scatter(beside(grads[..., :block_rows, 3 * width :]))
    norm_sum = lax.psum(norm_total, AXES)
    in_sum = jnp.concatenate([jnp.concatenate([in_part, below(self_out)], axis=1), norm_sum])
    grads = moves.joined(image_grads)
    image_rows = grads.shape[3] - 2 * out_rows
    image_part = grads[..., :image_rows, :]
    image_part = jnp.concatenate(
        [image_part[..., : features // 2], image_part[..., features // 2 :]], axis=3
    )
    image_part = moves.scatter(image_part)
    image_half = image_part.shape[0] // 2
    image_part = jnp.concatenate([image_part[:image_half], image_part[image_half:]], axis=1)
    cross_query = moves.scatter(below(grads[..., image_rows : image_rows + out_rows, :]))
    cross_out = moves.scatter(grads[..., image_rows + out_rows :, :])
    image_sum = jnp.concatenate([image_part, beside(cross_query), cross_out])
    grads = moves.joined(feed_grads)
    feed_sum = jnp.concatenate(
        [moves.scatter(jnp.stack(feed_grads[:2])), moves.scatter(grads[..., feed_half:, :])]
    )
    return block_out, input_grad, in_sum, image_sum, feed_sum


def per_device(
    hidden_in,
    image_feats,
    caption_lengths,
    out_grad,
    proj_in,
    proj_in_moments,
    proj_in_average,
    proj_out,
    proj_out_moments,
    proj_out_average,
    image_kv,
    image_kv_moments,
    image_kv_average,
    feed_up,
    feed_up_moments,
    feed_up_average,
    feed_down,
    feed_down_moments,
    feed_down_average,
    norm_params,
    norm_params_moments,
    norm_params_average,
):
    data_ways, model_ways = lax.axis_size("dp"), lax.axis_size("mp")
    data_index, model_index = lax.axis_index("dp"), lax.axis_index("mp")
    rows, features = hidden_in.shape
    items = rows // SEQ
    width = features // model_ways
    own_norm = norm_params.shape[1]
    norm_begin = (model_index * data_ways + data_index) * own_norm
    lengths = lax.dynamic_slice_in_dim(caption_lengths, model_index * items, items, 0)
    direct = data_ways == GROUPS and model_ways == MODEL
    if direct:
        feats = lax.dynamic_slice_in_dim(image_feats, model_index // 2 * 2 * items, 2 * items, 0)
        first_item = model_index % 2 * items
    else:
        feats = jnp.concatenate(
            [
                lax.dynamic_slice_in_dim(image_feats, (model_index % 2 + 2 * side) * items, items, 0)
                for side in range(2)
            ]
        )
        first_item = model_index // 2 * items
    image_piece = jnp.concatenate([image_kv[0], image_kv[1]], axis=1).astype(BF16)
    in_piece = jnp.concatenate([proj_in[kind] for kind in range(4)], axis=1).astype(BF16)
    out_pieces = [proj_out[kind].astype(BF16) for kind in range(2)]
    feed_piece = jnp.concatenate([feed_up, feed_down], axis=0).astype(BF16)
    norm_rows = lax.dynamic_update_slice(
        jnp.zeros((NORM_ROWS, features), F32), norm_params, (0, norm_begin)
    ).astype(BF16)
    own_in, own_out, own_image = proj_in.shape[1], proj_out.shape[1], image_kv.shape[1]
    if direct:
        run, half = run_direct, own_in // 2
        begin_piece = jnp.concatenate(
            [
                in_piece[:half],
                out_pieces[1],
                jnp.zeros_like(norm_rows),
                in_piece[half:],
                out_pieces[0],
                norm_rows,
            ],
            axis=0,
        )
    else:
        run = run_plain
        begin_piece = jnp.concatenate(
            [in_piece, out_pieces[1], out_pieces[0], norm_rows], axis=0
        )
    block_out, input_grad, in_sum, image_sum, feed_sum = run(
        hidden_in, feats, first_item, lengths, out_grad, image_piece, begin_piece, feed_piece
    )
    norm_shard = lax.dynamic_slice(in_sum[own_in:], (0, norm_begin), norm_params.shape)
    up_next, down_next, up_update, down_update, feed_squares = update_call(
        feed_update_kernel,
        (feed_sum, feed_up, feed_up_moments, feed_down, feed_down_moments),
        (feed_up_moments, feed_down_moments),
        (feed_up, feed_down),
        "feed_update",
    )
    image_next, image_update, image_squares = update_call(
        image_update_kernel,
        (image_sum, image_kv, image_kv_moments),
        (image_kv_moments,),
        (image_kv,),
        "image_update",
    )
    in_next, out_next, norm_next, in_update, out_update, norm_update, last_squares = update_call(
        last_update_kernel,
        (
            in_sum,
            image_sum,
            norm_shard,
            proj_in,
            proj_in_moments,
            proj_out,
            proj_out_moments,
            norm_params,
            norm_params_moments,
        ),
        (proj_in_moments, proj_out_moments, norm_params_moments),
        (proj_in, proj_out, norm_params),
        "last_update",
    )
    own_squares = feed_squares + image_squares + last_squares
    ways = data_ways * model_ways
    copies = jnp.broadcast_to(own_squares[None], (ways,) + own_squares.shape)
    squares = lax.all_to_all(copies, AXES, 0, 0, tiled=True)
    results = apply_call(
        squares,
        (proj_in, proj_out, image_kv, feed_up, feed_down, norm_params),
        (
            proj_in_average,
            proj_out_average,
            image_kv_average,
            feed_up_average,
            feed_down_average,
            norm_params_average,
        ),
        (in_update, out_update, image_update, up_update, down_update, norm_update),
    )
    new_weights, new_averages, (trust, norms) = results[:6], results[6:12], results[12:]
    moments = (in_next, out_next, image_next, up_next, down_next, norm_next)
    outputs = [
        each for group in zip(new_weights, moments, new_averages) for each in group
    ]
    tensors = sum(each.shape[0] for each in (proj_in, proj_out, image_kv, norm_params)) + 2
    return (block_out, input_grad, *outputs, trust[0, :tensors], norms[:, :tensors])


def solution(mesh):
    rows = P(AXES, None)
    by_column = P(None, "dp", "mp")
    by_row = P(None, ("mp", "dp"), None)
    weights = (
        by_column,
        P(None, None, "dp", "mp"),
        by_column,
        by_row,
        P(None, None, ("mp", "dp"), None),
        by_row,
        by_column,
        P(None, None, "dp", "mp"),
        by_column,
        P("dp", "mp"),
        P(None, "dp", "mp"),
        P("dp", "mp"),
        P(("mp", "dp"), None),
        P(None, ("mp", "dp"), None),
        P(("mp", "dp"), None),
        P(None, ("mp", "dp")),
        P(None, None, ("mp", "dp")),
        P(None, ("mp", "dp")),
    )
    return jax.shard_map(
        per_device,
        mesh=mesh,
        in_specs=(rows, P("dp", None, None), P("dp"), rows, *weights),
        out_specs=(rows, rows, *weights, P(), P()),
        check_vma=False,
    )
```

```python
import functools

import jax
import jax.numpy as jnp
from jax import lax
from jax.experimental import pallas as pl
from jax.experimental.pallas import tpu as pltpu
from jax.sharding import PartitionSpec as P

HEAD = 64
PATCHES = 257
QUERIES = 32
TEXT = 32
SEQ = QUERIES + TEXT
STEP = 10


NORM_EPSILON = 1e-06
ADAM_EPSILON = 1e-06
SQUARE_EPSILON = 1e-06
BETA_ONE = 0.9
BETA_TWO = 0.999
LEARN_RATE = 0.5
DECAY_RATE = 0.01
AVERAGE_RATE = 0.6
MASK_VALUE = -1e30

AXES = ("dp", "mp")
GROUPS = 8
MODEL = 4
SLOTS = 16
NORM_ROWS = 8
LANES = 128
IMAGE_SPLIT = 64
SELF_SPLIT = 48
BLOCK = 128
WIDE = 256
HEADS_AT_ONCE = 12
SLOT = 272
MIB = 1024 * 1024

BF16 = jnp.bfloat16
F32 = jnp.float32


def dot_nn(left_side, right_side):
    return lax.dot_general(
        left_side, right_side, (((1,), (0,)), ((), ())), preferred_element_type=F32
    )


def dot_nt(left_side, right_side):
    return lax.dot_general(
        left_side, right_side, (((1,), (1,)), ((), ())), preferred_element_type=F32
    )


def dot_tn(left_side, right_side):
    return lax.dot_general(
        left_side, right_side, (((0,), (0,)), ((), ())), preferred_element_type=F32
    )


def normalise(inputs):
    centred = inputs - jnp.mean(inputs, axis=-1, keepdims=True)
    inverse = lax.rsqrt(jnp.mean(centred * centred, axis=-1, keepdims=True) + NORM_EPSILON)
    return centred * inverse, inverse


def norm_back(gradient, normed, inverse, gain):
    scaled = gradient * gain
    centre_term = jnp.mean(scaled, axis=-1, keepdims=True)
    normed_term = jnp.mean(scaled * normed, axis=-1, keepdims=True)
    return inverse * (scaled - centre_term - normed * normed_term)


def slot_of(place, block, y_rel):
    return place[block] * 8 + y_rel * 4 + place[GROUPS + block]


def softmax(scores):
    tops = [jnp.max(each, axis=-1, keepdims=True) for each in scores]
    exponents = [jnp.exp(each - top) for each, top in zip(scores, tops)]
    totals = [jnp.sum(each, axis=-1, keepdims=True) for each in exponents]
    return [each / total for each, total in zip(exponents, totals)]


def block_mask(lengths, first_item):
    per_block = BLOCK // SEQ
    row = lax.broadcasted_iota(jnp.int32, (BLOCK, BLOCK), 0)
    column = lax.broadcasted_iota(jnp.int32, (BLOCK, BLOCK), 1)
    row_item, column_item = lax.shift_right_logical(row, 6), lax.shift_right_logical(column, 6)
    slot = column - column_item * SEQ
    limit = jnp.zeros((BLOCK, BLOCK), jnp.int32)
    for item in range(per_block):
        limit = jnp.where(column_item == item, lengths[first_item + item] + QUERIES, limit)
    return (row_item == column_item) & (slot < limit)


def self_forward_kernel(
    place,
    lengths,
    hidden,
    begin_own,
    begin_other,
    first_in,
    qkv,
    heads,
    w_qkv,
    w_cross,
    w_self_out,
    w_cross_out,
    norm,
    self_rows,
    cross_rows,
):
    rows, features = hidden.shape
    width = features // MODEL
    block_rows = features // GROUPS
    out_rows = width // GROUPS
    half, part = block_rows // 2, begin_own.shape[1] // 2
    norm_sum = jnp.zeros((NORM_ROWS, features), F32)
    for block in range(GROUPS):
        pieces = []
        for model in range(MODEL):
            side, y_rel = divmod(model, 2)
            source, slot = (begin_own, begin_other)[side], slot_of(place, block, y_rel)
            pieces.append(
                jnp.concatenate(
                    [source[slot, :half, :], source[slot, part : part + half, :]], axis=0
                )
            )
            cross_part = source[slot, half:part, :].astype(F32)
            self_part = source[slot, part + half :, :].astype(F32)
            begin = model * width + block * out_rows
            cross_rows[begin : begin + out_rows, :] = cross_part[:out_rows]
            self_rows[begin : begin + out_rows, :] = self_part[:out_rows]
            norm_sum = norm_sum + self_part[out_rows:]
        begin = block * block_rows
        for kind in range(4):
            joined = jnp.concatenate(
                [piece[:, kind * width : (kind + 1) * width] for piece in pieces], axis=1
            )
            if kind < 3:
                w_qkv[begin : begin + block_rows, kind * features : (kind + 1) * features] = joined
            else:
                w_cross[begin : begin + block_rows, :] = joined
    norm[...] = norm_sum
    w_self_out[...] = self_rows[...].astype(BF16)
    w_cross_out[...] = cross_rows[...].astype(BF16)
    tokens = hidden[...]
    for kind in range(3):
        columns = slice(kind * features, (kind + 1) * features)
        qkv[:, columns] = dot_nn(tokens, w_qkv[:, columns]).astype(BF16)
    scale = HEAD ** (-0.5)
    for begin in range(0, rows, BLOCK):
        span = slice(begin, begin + BLOCK)
        mask = block_mask(lengths, begin // SEQ)
        for first in range(0, features // HEAD, HEADS_AT_ONCE):
            queries, key_rows, value_rows = [
                [
                    qkv[span, kind * features + head * HEAD : kind * features + (head + 1) * HEAD]
                    for head in range(first, first + HEADS_AT_ONCE)
                ]
                for kind in range(3)
            ]
            scores = [dot_nt(*pair) for pair in zip(queries, key_rows)]
            probs = softmax([jnp.where(mask, each * scale, MASK_VALUE) for each in scores])
            mixed = [dot_nn(*pair) for pair in zip([each.astype(BF16) for each in probs], value_rows)]
            heads[span, first * HEAD : (first + HEADS_AT_ONCE) * HEAD] = jnp.concatenate(
                [each.astype(BF16) for each in mixed], axis=1
            )
    first_in[...] = tokens.astype(F32) + dot_nn(heads[...], w_self_out[...])


def assemble_image(place, image_own, image_other, weight):
    block_rows = image_own.shape[1]
    width = image_own.shape[2] // 2
    features = width * MODEL
    for block in range(GROUPS):
        pieces = []
        for model in range(MODEL):
            side, y_rel = divmod(model, 2)
            pieces.append((image_own, image_other)[side][slot_of(place, block, y_rel)])
        begin = block * block_rows
        for kind in range(2):
            weight[begin : begin + block_rows, kind * features : (kind + 1) * features] = (
                jnp.concatenate(
                    [piece[:, kind * width : (kind + 1) * width] for piece in pieces], axis=1
                )
            )


def head_rows(values, head_mask):
    stacked = jnp.concatenate([values] * (WIDE // HEAD), axis=0)
    return jnp.where(head_mask, stacked, jnp.zeros_like(stacked))


def fold_heads(values, head_mask):
    kept = jnp.where(head_mask, values, 0.0)
    count = WIDE // HEAD
    size = values.shape[0] // count
    total = kept[:size]
    for index in range(1, count):
        total = total + kept[index * size : (index + 1) * size]
    return total


def query_head_mask():
    shape = (QUERIES * (WIDE // HEAD), WIDE)
    row = lax.broadcasted_iota(jnp.int32, shape, 0)
    column = lax.broadcasted_iota(jnp.int32, shape, 1)
    return lax.shift_right_logical(row, 5) == lax.shift_right_logical(column, 6)


def patch_softmax(queries, keys):
    scores = [dot_nt(*pair) * HEAD ** (-0.5) for pair in zip(queries, keys)]
    column = lax.broadcasted_iota(jnp.int32, scores[0].shape, 1)
    return softmax([jnp.where(column < PATCHES, each, MASK_VALUE) for each in scores])


def query_rows(values):
    items = values.shape[0] // SEQ
    return jnp.concatenate(
        [values[item * SEQ : item * SEQ + QUERIES] for item in range(items)], axis=0
    )


def look_kernel(
    place,
    feats,
    image_own,
    image_other,
    first_in,
    norm,
    w_cross,
    w_cross_out,
    key_values,
    second_in,
    queries,
    heads,
    weight,
):
    features = first_in.shape[1]
    patches = feats.shape[1]
    step, steps = pl.program_id(0), pl.num_programs(0)

    @pl.when(step == 0)
    def _():
        assemble_image(place, image_own, image_other, weight)
        normed, _ = normalise(query_rows(first_in[...]))
        one_query = normed * norm[0:1, :] + norm[1:2, :]
        second_in[...] = one_query
        queries[...] = dot_nn(one_query.astype(BF16), w_cross[...]).astype(BF16)

    key_values[:patches, :] = dot_nn(feats[0], weight[...]).astype(BF16)
    key_values[patches:, :] = jnp.zeros((SLOT - patches, weight.shape[1]), BF16)
    head_mask = query_head_mask()
    span = pl.ds(pl.multiple_of(step * QUERIES, QUERIES), QUERIES)
    columns = [slice(begin, begin + WIDE) for begin in range(0, features, WIDE)]
    value_columns = [slice(features + each.start, features + each.stop) for each in columns]
    expanded = [head_rows(queries[span, each], head_mask) for each in columns]
    probs = patch_softmax(expanded, [key_values[:, each] for each in columns])
    mixed = [
        dot_nn(prob.astype(BF16), key_values[:, each]) for prob, each in zip(probs, value_columns)
    ]
    for each, values in zip(columns, mixed):
        heads[span, each] = fold_heads(values, head_mask).astype(BF16)

    @pl.when(step == steps - 1)
    def _():
        second_in[...] += dot_nn(heads[...], w_cross_out[...])


def gelu_cumulative(inputs):
    return 0.5 * (1.0 + lax.erf(inputs * 0.7071067811865476))


def feed_kernel(
    place,
    lengths,
    norm,
    first_hbm,
    second_hbm,
    out_grad_hbm,
    up_first,
    down_first,
    up_last,
    down_last,
    up_first_other,
    down_first_other,
    up_last_other,
    down_last_other,
    block_out,
    two_grad,
    keep_hbm,
    send_hbm,
    norm_grads,
    first_in,
    second_in,
    out_grad,
    w_up,
    w_down,
    two_rows,
    pre_act,
    result,
    keep,
    send,
    in_sem,
    up_sem,
    down_sem,
    keep_sem,
    send_sem,
    out_sem,
):
    rows, features = first_in.shape
    items = rows // SEQ
    hidden_width = up_first.shape[3]
    piece_rows = up_first.shape[2]
    half = 2 * hidden_width
    up_parts = ((up_first, up_last), (up_first_other, up_last_other))
    down_parts = ((down_first, down_last), (down_first_other, down_last_other))

    def put(target, source, begin, width, semaphore):
        columns = pl.ds(begin, width)
        copy = pltpu.make_async_copy(source.at[:, columns], target.at[:, columns], semaphore)
        copy.start()
        return copy

    entries = [
        pltpu.make_async_copy(source, target, in_sem.at[index])
        for index, (source, target) in enumerate(
            ((first_hbm, first_in), (second_hbm, second_in), (out_grad_hbm, out_grad))
        )
    ]
    entries[0].start()
    entries[1].start()
    for first in range(2):

        @pl.when(place[0] == first)
        def _():
            for model in range(MODEL):
                side, y_rel = divmod(model, 2)
                for block in range(GROUPS):
                    source = up_parts[side][(block + first) % 2]
                    pltpu.make_async_copy(
                        source.at[y_rel, place[GROUPS + block]],
                        w_up.at[model, pl.ds(block * piece_rows, piece_rows), :],
                        up_sem.at[model],
                    ).start()
                for block in range(GROUPS):
                    source = down_parts[side][y_rel]
                    pltpu.make_async_copy(
                        source.at[(block + first) % 2, place[GROUPS + block]],
                        w_down.at[model, pl.ds(block * piece_rows, piece_rows), :],
                        down_sem.at[model],
                    ).start()

    entries[2].start()
    entries[0].wait()
    entries[1].wait()
    copies = []
    normed_one, _ = normalise(first_in[...])
    after_one = normed_one * norm[0:1, :] + norm[1:2, :]
    normed_two, _ = normalise(second_in[...])
    after_two = normed_two * norm[2:3, :] + norm[3:4, :]
    for item in range(items):
        begin = item * SEQ
        two_rows[begin : begin + QUERIES, :] = after_two[item * QUERIES : (item + 1) * QUERIES]
        two_rows[begin + QUERIES : begin + SEQ, :] = after_one[begin + QUERIES : begin + SEQ]
    feed_in = two_rows[...].astype(BF16)
    send[:, 2 * half : 2 * half + features] = feed_in
    copies.append(put(send_hbm, send, 2 * half, features, send_sem.at[4]))
    third_in = two_rows[...]
    for model in range(MODEL):
        side, y_rel = divmod(model, 2)
        target = (keep, send)[side]
        begin = y_rel * hidden_width
        pltpu.make_async_copy(w_up.at[model], w_up.at[model], up_sem.at[model]).wait()
        pre = dot_nn(feed_in, w_up[model])
        pre_act[:, model * hidden_width : (model + 1) * hidden_width] = pre
        act = (pre * gelu_cumulative(pre)).astype(BF16)
        target[:, begin : begin + hidden_width] = act
        semaphore = (keep_sem, send_sem)[side].at[y_rel]
        copies.append(put((keep_hbm, send_hbm)[side], target, begin, hidden_width, semaphore))
        pltpu.make_async_copy(w_down.at[model], w_down.at[model], down_sem.at[model]).wait()
        third_in = third_in + dot_nn(act, w_down[model])
    normed, inverse = normalise(third_in)
    result[...] = (normed * norm[4:5, :] + norm[5:6, :]).astype(BF16)
    copies.append(pltpu.make_async_copy(result, block_out, out_sem.at[0]))
    copies[-1].start()
    entries[2].wait()
    position = lax.broadcasted_iota(jnp.int32, (SEQ, features), 0)
    slope = jnp.concatenate(
        [
            jnp.where(
                position < lengths[item] + QUERIES,
                out_grad[item * SEQ : (item + 1) * SEQ, :].astype(F32),
                0.0,
            )
            for item in range(items)
        ],
        axis=0,
    )
    norm_grads[...] = jnp.zeros_like(norm_grads)
    norm_grads[4:5, :] = jnp.sum(slope * normed, axis=0, keepdims=True)
    norm_grads[5:6, :] = jnp.sum(slope, axis=0, keepdims=True)
    third_grad = norm_back(slope, normed, inverse, norm[4:5, :])
    grad_rows = third_grad.astype(BF16)
    send[:, 2 * half + features :] = grad_rows
    copies.append(put(send_hbm, send, 2 * half + features, features, send_sem.at[5]))
    total = third_grad
    for model in range(MODEL):
        side, y_rel = divmod(model, 2)
        target = (keep, send)[side]
        begin = half + y_rel * hidden_width
        pre = pre_act[:, model * hidden_width : (model + 1) * hidden_width]
        density = jnp.exp(-0.5 * pre * pre) * 0.3989422804014327
        slope_part = gelu_cumulative(pre) + pre * density
        grad_pre = (dot_nt(grad_rows, w_down[model]) * slope_part).astype(BF16)
        target[:, begin : begin + hidden_width] = grad_pre
        semaphore = (keep_sem, send_sem)[side].at[2 + y_rel]
        copies.append(put((keep_hbm, send_hbm)[side], target, begin, hidden_width, semaphore))
        total = total + dot_nt(grad_pre, w_up[model])
    two_rows[...] = total
    copies.append(pltpu.make_async_copy(two_rows, two_grad, out_sem.at[1]))
    copies[-1].start()
    for copy in copies:
        copy.wait()


def put_left(place, block, y_rel, keep, send, value):
    for along_x, target in ((0, keep), (1, send)):

        @pl.when(place[block] == along_x)
        def _(target=target):
            target[y_rel, place[GROUPS + block]] = value


def put_right(place, block, y_rel, keep, send, value):
    (keep, send)[y_rel][place[block], place[GROUPS + block]] = value


def feed_grad_kernel(
    place, hidden, rows, hidden_other, rows_other, left_keep, left_send, right_keep, right_send
):
    piece_rows = left_keep.shape[2]
    kind, y_step = pl.program_id(0), pl.program_id(1)

    @pl.when(kind == 0)
    def _():
        grad_up = dot_tn(rows[...], hidden[...])
        grad_up = (grad_up + dot_tn(rows_other[...], hidden_other[...])).astype(BF16)
        for block in range(GROUPS):
            span = slice(block * piece_rows, (block + 1) * piece_rows)
            put_left(place, block, y_step, left_keep, left_send, grad_up[span])

    for y_rel in range(2):

        @pl.when((kind == 1) & (y_step == y_rel))
        def _(y_rel=y_rel):
            grad_down = dot_tn(hidden[...], rows[...])
            grad_down = (grad_down + dot_tn(hidden_other[...], rows_other[...])).astype(BF16)
            for block in range(GROUPS):
                span = slice(block * piece_rows, (block + 1) * piece_rows)
                put_right(place, block, y_rel, right_keep, right_send, grad_down[span])


def cross_backward_kernel(
    two_grad,
    first_in,
    second_in,
    norm,
    w_cross,
    w_cross_out,
    queries,
    heads,
    key_values,
    norm_grads_in,
    keep,
    send,
    one_query_grad,
    norm_grads,
    head_grads,
    query_grads,
    grad_rows,
):
    features = first_in.shape[1]
    half = features // 2
    count = queries.shape[0]
    step = pl.program_id(0)
    items = pl.num_programs(0) - 3
    scale = HEAD ** (-0.5)

    @pl.when(step == 0)
    def _():
        two_query = query_rows(two_grad[...])
        normed, inverse = normalise(second_in[...])
        norm_grads[...] = norm_grads_in[...]
        norm_grads[2:3, :] = jnp.sum(two_query * normed, axis=0, keepdims=True)
        norm_grads[3:4, :] = jnp.sum(two_query, axis=0, keepdims=True)
        second_grad = norm_back(two_query, normed, inverse, norm[2:3, :])
        one_query_grad[...] = second_grad
        grad_rows[...] = second_grad.astype(BF16)
        head_grads[...] = dot_nt(grad_rows[...], w_cross_out[...]).astype(BF16)

    @pl.when(step < items)
    def _():
        head_mask = query_head_mask()
        span = pl.ds(pl.multiple_of(step * QUERIES, QUERIES), QUERIES)
        columns = [slice(begin, begin + WIDE) for begin in range(0, features, WIDE)]
        keys = [key_values[:, each] for each in columns]
        value_rows = [
            key_values[:, features + each.start : features + each.stop] for each in columns
        ]
        expanded = [head_rows(queries[span, each], head_mask) for each in columns]
        slopes = [head_rows(head_grads[span, each], head_mask) for each in columns]
        grad_probs = [dot_nt(*pair) for pair in zip(slopes, value_rows)]
        probs = patch_softmax(expanded, keys)
        inner = [
            jnp.sum(each * prob, axis=-1, keepdims=True) for each, prob in zip(grad_probs, probs)
        ]
        grad_scores = [
            (prob * (each - total)).astype(BF16)
            for prob, each, total in zip(probs, grad_probs, inner)
        ]
        grad_values = [
            dot_tn(prob.astype(BF16), slope).astype(BF16) for prob, slope in zip(probs, slopes)
        ]
        grad_keys = [
            (dot_tn(*pair) * scale).astype(BF16) for pair in zip(grad_scores, expanded)
        ]
        grad_queries = [dot_nn(*pair) for pair in zip(grad_scores, keys)]
        for index, each in enumerate(columns):
            query_grads[span, each] = (
                fold_heads(grad_queries[index], head_mask) * scale
            ).astype(BF16)
            for part in range(0, WIDE, WIDE // 2):
                side, place_at = divmod(each.start + part, half)
                target, lanes = (keep, send)[side], slice(part, part + WIDE // 2)
                target[:, place_at : place_at + WIDE // 2] = grad_keys[index][:, lanes]
                place_at += half
                target[:, place_at : place_at + WIDE // 2] = grad_values[index][:, lanes]

    @pl.when(step >= items)
    def _():
        for target in (keep, send):
            target[count:, :] = jnp.zeros((SLOT - count, features), BF16)

    @pl.when(step == items)
    def _():
        normed_one, _ = normalise(query_rows(first_in[...]))
        query_in = (normed_one * norm[0:1, :] + norm[1:2, :]).astype(BF16)
        for target in (keep, send):
            target[:count, :] = query_in

    @pl.when(step == items + 1)
    def _():
        for target in (keep, send):
            target[:count, :] = grad_rows[...]

    @pl.when(step == items + 2)
    def _():
        for side, target in enumerate((keep, send)):
            columns = slice(side * half, (side + 1) * half)
            target[:count, :half] = query_grads[:, columns]
            target[:count, half:] = heads[:, columns]
        one_query_grad[...] += dot_nt(query_grads[...], w_cross[...])


def image_grad_kernel(
    count,
    place,
    feats,
    keep_rows,
    other_rows,
    keep,
    other,
    left_keep,
    left_send,
    right_keep,
    right_send,
    total,
    spread,
):
    features = keep.shape[1]
    half = features // 2
    width = half // 2
    image_rows = feats.shape[2] // GROUPS
    image_half = image_rows // 2
    block_rows = features // GROUPS
    out_rows = width // GROUPS
    split = left_keep.shape[2]
    step, steps = pl.program_id(0), pl.num_programs(0)

    @pl.when(step == 0)
    def _():
        spread[...] = jnp.zeros_like(spread)

    for item in range(feats.shape[0]):
        spread[item * SLOT : item * SLOT + feats.shape[1], :] = feats[item]

    @pl.when(step == 0)
    def _():
        total[...] = dot_tn(spread[...], keep_rows[...])

    @pl.when((step > 0) & (step < steps // 2))
    def _():
        total[...] += dot_tn(spread[...], keep_rows[...])

    @pl.when(step >= steps // 2)
    def _():
        total[...] += dot_tn(spread[...], other_rows[...])

    @pl.when(step == steps - 1)
    def _():
        inputs, slopes = slice(0, count), slice(SLOT, SLOT + count)
        parts = slice(2 * SLOT, 2 * SLOT + count)
        grad_query = dot_tn(keep[inputs, :], keep[parts, :half]) + dot_tn(
            other[inputs, :], other[parts, :half]
        )
        grad_out = dot_tn(keep[parts, half:], keep[slopes, :]) + dot_tn(
            other[parts, half:], other[slopes, :]
        )
        for block in range(GROUPS):
            for y_rel in range(2):
                columns = slice(y_rel * width, (y_rel + 1) * width)
                image_part = [
                    total[
                        begin : begin + image_half,
                        kind + y_rel * width : kind + (y_rel + 1) * width,
                    ]
                    for begin in (block * image_rows, block * image_rows + image_half)
                    for kind in (0, half)
                ]
                begin = block * block_rows
                cross_part = [
                    grad_query[begin + part * out_rows : begin + (part + 1) * out_rows, columns]
                    for part in range(MODEL)
                ]
                begin = y_rel * width + block * out_rows
                piece = jnp.concatenate(
                    [
                        jnp.concatenate(image_part, axis=1),
                        jnp.concatenate(cross_part, axis=1),
                        grad_out[begin : begin + out_rows],
                    ],
                    axis=0,
                )
                put_left(place, block, y_rel, left_keep, left_send, piece[:split].astype(BF16))
                put_right(place, block, y_rel, right_keep, right_send, piece[split:].astype(BF16))


def self_backward_kernel(
    lengths,
    one_query_grad,
    two_grad,
    first_in,
    norm,
    hidden,
    qkv,
    heads,
    w_qkv,
    w_self_out,
    norm_grads_in,
    input_grad,
    keep,
    send,
    norm_total,
    one_grad,
    head_grads,
    grad_qkv,
):
    rows, features = hidden.shape
    items = rows // SEQ
    half = features // 2
    for item in range(items):
        begin = item * SEQ
        one_grad[begin : begin + QUERIES, :] = one_query_grad[
            item * QUERIES : (item + 1) * QUERIES, :
        ]
        one_grad[begin + QUERIES : begin + SEQ, :] = two_grad[begin + QUERIES : begin + SEQ, :]
    normed, inverse = normalise(first_in[...])
    gradient = one_grad[...]
    norm_sum = norm_grads_in[...] + jnp.concatenate(
        [
            jnp.sum(gradient * normed, axis=0, keepdims=True),
            jnp.sum(gradient, axis=0, keepdims=True),
            jnp.zeros((NORM_ROWS - 2, features), F32),
        ],
        axis=0,
    )
    norm_total[...] = norm_sum
    first_grad = norm_back(gradient, normed, inverse, norm[0:1, :])
    one_grad[...] = first_grad
    grad_rows = first_grad.astype(BF16)
    head_grads[...] = dot_nt(grad_rows, w_self_out[...]).astype(BF16)
    scale = HEAD ** (-0.5)
    for begin in range(0, rows, BLOCK):
        span = slice(begin, begin + BLOCK)
        mask = block_mask(lengths, begin // SEQ)
        for first in range(0, features // HEAD, HEADS_AT_ONCE):
            chosen = range(first, first + HEADS_AT_ONCE)
            queries, key_rows, value_rows = [
                [
                    qkv[span, kind * features + head * HEAD : kind * features + (head + 1) * HEAD]
                    for head in chosen
                ]
                for kind in range(3)
            ]
            slopes = [head_grads[span, head * HEAD : (head + 1) * HEAD] for head in chosen]
            scores = [dot_nt(*pair) for pair in zip(queries, key_rows)]
            grad_probs = [dot_nt(*pair) for pair in zip(slopes, value_rows)]
            probs = softmax([jnp.where(mask, each * scale, MASK_VALUE) for each in scores])
            inner = [
                jnp.sum(each * prob, axis=-1, keepdims=True)
                for each, prob in zip(grad_probs, probs)
            ]
            grad_scores = [
                (prob * (each - total)).astype(BF16)
                for prob, each, total in zip(probs, grad_probs, inner)
            ]
            results = (
                [dot_nn(*pair) * scale for pair in zip(grad_scores, key_rows)],
                [dot_tn(*pair) * scale for pair in zip(grad_scores, queries)],
                [dot_tn(prob.astype(BF16), slope) for prob, slope in zip(probs, slopes)],
            )
            for kind in range(3):
                begin_at = kind * features + first * HEAD
                grad_qkv[span, begin_at : begin_at + HEADS_AT_ONCE * HEAD] = jnp.concatenate(
                    [each.astype(BF16) for each in results[kind]], axis=1
                )
    total = one_grad[...]
    for kind in range(3):
        columns = slice(kind * features, (kind + 1) * features)
        total = total + dot_nt(grad_qkv[:, columns], w_qkv[:, columns])
        first = kind * features
        keep[:, kind * half : (kind + 1) * half] = grad_qkv[:, first : first + half]
        send[:rows, kind * half : (kind + 1) * half] = grad_qkv[:, first + half : first + features]
    input_grad[...] = total.astype(BF16)
    keep[:, 3 * half :] = heads[:, :half]
    send[:rows, 3 * half : 4 * half] = heads[:, half:]
    send[:rows, 4 * half : 6 * half] = hidden[...]
    send[:rows, 6 * half :] = grad_rows
    send[rows:, :] = jnp.zeros((send.shape[0] - rows, send.shape[1]), BF16)
    send[rows : rows + 16, :features] = jnp.concatenate(
        [norm_sum, jnp.zeros_like(norm_sum)], axis=0
    ).astype(BF16)


def self_grad_kernel(
    place, keep, send, other, norm_total, left_keep, left_send, right_keep, right_send
):
    features = norm_total.shape[1]
    rows = keep.shape[0]
    half = features // 2
    width = half // 2
    block_rows = features // GROUPS
    out_rows = width // GROUPS
    split = left_keep.shape[2]
    inputs, slopes = slice(4 * half, 6 * half), slice(6 * half, 8 * half)
    columns = slice(0, 3 * half)
    grad_in = dot_tn(send[:rows, inputs], keep[:, columns])
    grad_in = grad_in + dot_tn(other[:rows, inputs], other[:rows, columns])
    columns = slice(3 * half, 4 * half)
    grad_out = dot_tn(keep[:, columns], send[:rows, slopes])
    grad_out = grad_out + dot_tn(other[:rows, columns], other[:rows, slopes])
    norm_rows = norm_total[...] + other[rows : rows + 16, :features].astype(F32)[:NORM_ROWS]
    for block in range(GROUPS):
        span = slice(block * block_rows, (block + 1) * block_rows)
        for y_rel in range(2):
            pieces = [
                grad_in[span, kind * half + y_rel * width : kind * half + (y_rel + 1) * width]
                for kind in range(3)
            ]
            begin = y_rel * width + block * out_rows
            out_part = grad_out[begin : begin + out_rows]
            pieces.append(
                jnp.concatenate(
                    [out_part[:, part * width : (part + 1) * width] for part in range(MODEL)],
                    axis=0,
                )
            )
            piece = jnp.concatenate([jnp.concatenate(pieces, axis=1), norm_rows], axis=0)
            put_left(place, block, y_rel, left_keep, left_send, piece[:split].astype(BF16))
            put_right(place, block, y_rel, right_keep, right_send, piece[split:].astype(BF16))


def adam_step(weight, moment_one, moment_two, gradient, decay_rate):
    moment_one = BETA_ONE * moment_one + (1.0 - BETA_ONE) * gradient
    moment_two = BETA_TWO * moment_two + (1.0 - BETA_TWO) * gradient * gradient
    update = (
        moment_one
        / (1.0 - BETA_ONE**STEP)
        / (jnp.sqrt(moment_two / (1.0 - BETA_TWO**STEP)) + ADAM_EPSILON)
        + decay_rate * weight
    )
    return moment_one, moment_two, update


def place_sums(target, sums):
    column = lax.broadcasted_iota(jnp.int32, (1, LANES), 1)
    rows = []
    for kind in range(2):
        row = jnp.zeros((1, LANES), F32)
        for index, pair in sums.items():
            row = jnp.where(column == index, pair[kind], row)
        rows.append(row)
    target[...] = jnp.concatenate(rows, axis=0)


def sum_pair(weight, update):
    return jnp.sum(weight * weight), jnp.sum(update * update)


def feed_update_kernel(
    gradient,
    up,
    up_moments,
    down,
    down_moments,
    up_next,
    down_next,
    up_update,
    down_update,
    squares,
):
    rows = up.shape[0]
    sums = {}
    for index, weight, moments, following, result, span in (
        (8, up, up_moments, up_next, up_update, slice(0, rows)),
        (9, down, down_moments, down_next, down_update, slice(rows, None)),
    ):
        following[0], following[1], update = adam_step(
            weight[...], moments[0], moments[1], gradient[span, :], DECAY_RATE
        )
        result[...] = update
        sums[index] = sum_pair(weight[...], update)
    place_sums(squares, sums)


def image_update_kernel(gradient, weight, moments, following, result, squares):
    width = weight.shape[2]
    half = weight.shape[1] // 2
    sums = {}
    for kind in range(2):
        parts = []
        for part in range(2):
            span = slice(part * half, (part + 1) * half)
            lanes = slice((2 * part + kind) * width, (2 * part + kind + 1) * width)
            following[0, kind, span, :], following[1, kind, span, :], update = adam_step(
                weight[kind, span, :],
                moments[0, kind, span, :],
                moments[1, kind, span, :],
                gradient[:half, lanes],
                DECAY_RATE,
            )
            result[kind, span, :] = update
            parts.append(sum_pair(weight[kind, span, :], update))
        sums[6 + kind] = tuple(left + right for left, right in zip(*parts))
    place_sums(squares, sums)


def last_update_kernel(
    gradient,
    cross_gradient,
    norm_gradient,
    inward,
    inward_moments,
    outward,
    outward_moments,
    norm,
    norm_moments,
    inward_next,
    outward_next,
    norm_next,
    inward_update,
    outward_update,
    norm_update,
    squares,
):
    own_in, width = inward.shape[1:]
    own_out = outward.shape[1]
    cross_rows = cross_gradient.shape[0] - 2 * own_out
    cross_query = cross_gradient[cross_rows : cross_rows + own_out, :]
    gradients = [gradient[:own_in, kind * width : (kind + 1) * width] for kind in range(3)]
    gradients.append(
        jnp.concatenate(
            [cross_query[:, part * width : (part + 1) * width] for part in range(MODEL)], axis=0
        )
    )
    sums = {}
    for kind in range(4):
        inward_next[0, kind], inward_next[1, kind], update = adam_step(
            inward[kind],
            inward_moments[0, kind],
            inward_moments[1, kind],
            gradients[kind],
            DECAY_RATE,
        )
        inward_update[kind] = update
        sums[kind] = sum_pair(inward[kind], update)
    folded = gradient[:own_in, 3 * width :]
    self_out = jnp.concatenate(
        [folded[part * own_out : (part + 1) * own_out] for part in range(MODEL)], axis=1
    )
    for kind, part in enumerate((self_out, cross_gradient[cross_rows + own_out :, :])):
        outward_next[0, kind], outward_next[1, kind], update = adam_step(
            outward[kind], outward_moments[0, kind], outward_moments[1, kind], part, DECAY_RATE
        )
        outward_update[kind] = update
        sums[4 + kind] = sum_pair(outward[kind], update)
    norm_next[0], norm_next[1], update = adam_step(
        norm[...], norm_moments[0], norm_moments[1], norm_gradient[...], 0.0
    )
    norm_update[...] = update
    for kind in range(norm.shape[0]):
        sums[10 + kind] = sum_pair(norm[kind : kind + 1, :], update[kind : kind + 1, :])
    place_sums(squares, sums)


def apply_kernel(squares, *refs):
    groups = len(refs) // 5
    weights, averages, updates = refs[:groups], refs[groups : 2 * groups], refs[2 * groups : 3 * groups]
    new_weights, new_averages = refs[3 * groups : 4 * groups], refs[4 * groups : 5 * groups]
    trust_out, norms_out = refs[5 * groups :]
    sums = jnp.sum(squares[...], axis=0)
    trust = jnp.sqrt(sums[0:1]) * lax.rsqrt(sums[1:2] + SQUARE_EPSILON)
    trust_out[...] = trust
    norms_out[...] = jnp.sqrt(sums)
    column = lax.broadcasted_iota(jnp.int32, trust.shape, 1)

    def ratio(index):
        return jnp.sum(jnp.where(column == index, trust, 0.0), axis=1, keepdims=True)

    index = 0
    for weight, average, update, new_weight, new_average in zip(
        weights, averages, updates, new_weights, new_averages
    ):
        if len(weight.shape) == 3:
            spans = list(range(weight.shape[0]))
        elif weight.shape[0] == 6:
            spans = [slice(row, row + 1) for row in range(6)]
        else:
            spans = [slice(None)]
        for span in spans:
            value = weight[span] - LEARN_RATE * ratio(index) * update[span]
            new_weight[span] = value
            new_average[span] = AVERAGE_RATE * average[span] + (1.0 - AVERAGE_RATE) * value
            index += 1


SCALARS = pl.BlockSpec(memory_space=pltpu.SMEM)
WHOLE = pl.BlockSpec(memory_space=pltpu.VMEM)


def local_call(kernel, scalars, arrays, out_shapes, scratch, flops, name, limit):
    size = sum(a.size * a.dtype.itemsize for a in arrays)
    size += sum(a.size * a.dtype.itemsize for a in out_shapes)
    return pl.pallas_call(
        kernel,
        out_shape=tuple(out_shapes),
        in_specs=[SCALARS] * len(scalars) + [WHOLE] * len(arrays),
        out_specs=tuple([WHOLE] * len(out_shapes)),
        scratch_shapes=scratch,
        compiler_params=pltpu.CompilerParams(vmem_limit_bytes=limit * MIB),
        cost_estimate=pl.CostEstimate(flops=flops, bytes_accessed=size, transcendentals=0),
        name=name,
    )(*scalars, *arrays)


def shape_of(*dims, dtype=BF16):
    return jax.ShapeDtypeStruct(dims, dtype)


def part_shapes(left_rows, right_rows, features):
    left, right = shape_of(2, 4, left_rows, features), shape_of(2, 4, right_rows, features)
    return left, left, right, right


def like(array):
    return jax.ShapeDtypeStruct(array.shape, array.dtype)


def update_call(kernel, arrays, moments, weights, name):
    shapes = [like(each) for each in (*moments, *weights)] + [shape_of(2, LANES, dtype=F32)]
    return local_call(kernel, (), arrays, shapes, [], 0, name, 20)


def apply_call(squares, weights, averages, updates):
    shapes = [like(each) for each in (*weights, *averages)]
    shapes += [shape_of(1, LANES, dtype=F32), shape_of(2, LANES, dtype=F32)]
    return local_call(
        apply_kernel, (), (squares, *weights, *averages, *updates), shapes, [], 0, "apply", 60
    )


class Direct:
    def __init__(self, dp, mp):
        self.count = dp * mp
        self.mp = mp
        self.depth = dp // 2
        index = lax.axis_index("dp")
        block = jnp.arange(GROUPS, dtype=jnp.int32)
        along_x = (block % 2) ^ (index % 2)
        along_z = (index // 2 - block // 2) % self.depth
        self.place = jnp.concatenate([along_x, along_z]).astype(jnp.int32)

    def hop(self, values, flip):
        return lax.ppermute(values, AXES, [(i, i ^ flip) for i in range(self.count)])

    def hop_core(self, values):
        return self.hop(values, 1)

    def hop_y(self, values):
        return self.hop(values, 2)

    def hop_x(self, values):
        return self.hop(values, self.mp)

    def hop_z(self, values, distance):
        step = 2 * self.mp * distance
        return lax.ppermute(values, AXES, [(i, (i + step) % self.count) for i in range(self.count)])

    def spread_z(self, piece):
        return jnp.stack([piece] + [self.hop_z(piece, step) for step in range(1, self.depth)])


    def spread_first(self, held, split):
        return self.hop_y(held[:, :split]), self.hop_x(held[:, split:])

    def join_first(self, held, split, others):
        return jnp.stack([held[:, :split], others[0]]), jnp.stack([held[:, split:], others[1]])

    def spread_second(self, parts):
        return self.hop_x(parts[0]), self.hop_y(parts[1])

    def join_second(self, parts, others):
        left = jnp.stack([parts[0], others[0]])
        right = jnp.stack([parts[1], others[1]]).transpose(1, 0, 2, 3, 4)
        whole = jnp.concatenate([left, right], axis=3)
        return whole.reshape(SLOTS, *whole.shape[3:])


    def fold_first(self, grads):
        return self.hop_x(grads[1]), self.hop_y(grads[3])

    def fold_second(self, grads, others):
        return (
            self.hop_y(total([grads[0][1], others[0][1]])),
            self.hop_x(total([grads[2][1], others[1][1]])),
        )

    def kept(self, grads, others, last):
        return [[grads[2 * side][0], others[side][0], last[side]] for side in range(2)]

    def fold_z(self, sides):
        return [
            self.hop_z(total(*[[part[step] for part in parts] for parts in sides]), -step)
            for step in range(1, self.depth)
        ]

    def ring_z(self, sides, step, carried=None):
        addends = [[part[step] for part in parts] for parts in sides]
        own = total(*addends, dtype=F32)
        if carried is not None:
            own = own + carried.astype(F32)
        return self.hop_z(own.astype(BF16), 1)

    def finish(self, sides, others):
        own = total(*[[part[0] for part in parts] for parts in sides], dtype=F32)
        return total([own, *others], dtype=F32)


def total(*sides, dtype=BF16):
    sums = []
    for parts in sides:
        result = parts[0].astype(F32)
        for part in parts[1:]:
            result = result + part.astype(F32)
        sums.append(result.astype(dtype))
    return sums[0] if len(sums) == 1 else jnp.concatenate(sums, axis=0)


class Plain:
    def __init__(self, dp, mp):
        self.dp = dp
        self.mp = mp
        self.side = lax.axis_index("mp") // 2
        block = jnp.arange(GROUPS, dtype=jnp.int32)
        self.place = jnp.concatenate([block % 2, block // 2]).astype(jnp.int32)

    def hop_core(self, values):
        count = self.dp * self.mp
        return lax.ppermute(values, AXES, [(i, i ^ 2) for i in range(count)])

    def collect(self, piece):
        rows, width = piece.shape
        blocks = lax.all_gather(piece, AXES, axis=0).reshape(self.dp, self.mp, rows, width)
        rows = rows * self.dp // GROUPS
        blocks = blocks.transpose(1, 0, 2, 3).reshape(2, 2, 4, 2, rows, width)
        blocks = blocks.transpose(0, 3, 1, 2, 4, 5).reshape(2, SLOTS, rows, width)
        return jnp.where(self.side == 0, blocks, blocks[::-1])

    def joined(self, grads):
        left = jnp.stack(grads[:2])
        right = jnp.stack(grads[2:]).transpose(1, 0, 2, 3, 4)
        return jnp.concatenate([left, right], axis=3)

    def scatter(self, own):
        rows, width = own.shape[3:]
        own = own.transpose(1, 2, 0, 3, 4).reshape(1, 2, GROUPS, rows, width)
        both = jnp.zeros((2, *own.shape[1:]), F32)
        both = lax.dynamic_update_slice_in_dim(both, own.astype(F32), self.side, 0)
        both = both.reshape(self.mp, self.dp, rows * GROUPS // self.dp, width)
        both = both.transpose(1, 0, 2, 3).reshape(-1, width)
        return lax.psum_scatter(both, AXES, scatter_dimension=0, tiled=True)


def tie(*arrays):
    return lax.optimization_barrier(arrays)


def padded(feats):
    pad = ((0, 0), (0, SLOT - PATCHES), (0, 0))
    return jnp.pad(feats, pad).reshape(-1, feats.shape[2])


def tie(*arrays):
    return lax.optimization_barrier(arrays)


def add(left_side, right_side):
    return (left_side.astype(F32) + right_side.astype(F32)).astype(BF16)


def self_forward(place, lengths, hidden, begin):
    rows, features = hidden.shape
    return local_call(
        self_forward_kernel,
        (place, lengths),
        (hidden, *begin),
        (
            shape_of(rows, features, dtype=F32),
            shape_of(rows, 3 * features),
            shape_of(rows, features),
            shape_of(features, 3 * features),
            shape_of(features, features),
            shape_of(features, features),
            shape_of(features, features),
            shape_of(NORM_ROWS, features, dtype=F32),
        ),
        [pltpu.VMEM((features, features), F32), pltpu.VMEM((features, features), F32)],
        10 * rows * features * features,
        "self_forward",
        28,
    )


def fixed(shape):
    return pl.BlockSpec(shape, lambda *_: (0,) * len(shape))


def look(place, feats, image, first_in, norm, w_cross, w_cross_out):
    items, patches, encoded = feats.shape
    items = items // 2
    rows, features = items * SLOT, first_in.shape[1]
    count = items * QUERIES
    arrays = (*image, first_in, norm, w_cross, w_cross_out)
    return pl.pallas_call(
        look_kernel,
        out_shape=(
            shape_of(rows, 2 * features),
            shape_of(count, features, dtype=F32),
            shape_of(count, features),
            shape_of(count, features),
        ),
        grid_spec=pltpu.PrefetchScalarGridSpec(
            num_scalar_prefetch=1,
            grid=(items,),
            in_specs=[
                pl.BlockSpec(
                    (1, patches, encoded), lambda item, where: (where[2 * GROUPS] + item, 0, 0)
                )
            ]
            + [fixed(each.shape) for each in arrays],
            out_specs=(
                pl.BlockSpec((SLOT, 2 * features), lambda item, where: (item, 0)),
                fixed((count, features)),
                fixed((count, features)),
                fixed((count, features)),
            ),
            scratch_shapes=[
                pltpu.VMEM((encoded, 2 * features), BF16),
            ],
        ),
        compiler_params=pltpu.CompilerParams(vmem_limit_bytes=46 * MIB),
        cost_estimate=pl.CostEstimate(
            flops=5 * rows * encoded * features,
            bytes_accessed=2 * rows * (encoded + 2 * features) + 4 * encoded * features,
            transcendentals=0,
        ),
        name="look",
    )(place, feats, *arrays)


def feed(place, lengths, first_in, second_in, norm, out_grad, weights):
    rows, features = first_in.shape
    width = weights[0].shape[3]
    anywhere = pl.BlockSpec(memory_space=pl.ANY)
    return pl.pallas_call(
        feed_kernel,
        out_shape=(
            shape_of(rows, features),
            shape_of(rows, features, dtype=F32),
            shape_of(rows, 4 * width),
            shape_of(rows, 4 * width + 2 * features),
            shape_of(NORM_ROWS, features, dtype=F32),
        ),
        in_specs=[SCALARS, SCALARS, WHOLE] + [anywhere] * (3 + len(weights)),
        out_specs=(anywhere, anywhere, anywhere, anywhere, WHOLE),
        scratch_shapes=[
            pltpu.VMEM(first_in.shape, F32),
            pltpu.VMEM(second_in.shape, F32),
            pltpu.VMEM((rows, features), BF16),
            pltpu.VMEM((MODEL, features, width), BF16),
            pltpu.VMEM((MODEL, width, features), BF16),
            pltpu.VMEM((rows, features), F32),
            pltpu.VMEM((rows, MODEL * width), F32),
            pltpu.VMEM((rows, features), BF16),
            pltpu.VMEM((rows, 4 * width), BF16),
            pltpu.VMEM((rows, 4 * width + 2 * features), BF16),
            pltpu.SemaphoreType.DMA((3,)),
            pltpu.SemaphoreType.DMA((MODEL,)),
            pltpu.SemaphoreType.DMA((MODEL,)),
            pltpu.SemaphoreType.DMA((4,)),
            pltpu.SemaphoreType.DMA((6,)),
            pltpu.SemaphoreType.DMA((2,)),
        ],
        compiler_params=pltpu.CompilerParams(vmem_limit_bytes=58 * MIB),
        cost_estimate=pl.CostEstimate(
            flops=8 * rows * features * MODEL * width,
            bytes_accessed=4 * MODEL * width * features,
            transcendentals=0,
        ),
        name="feed",
    )(place, lengths, norm, first_in, second_in, out_grad, *weights)


def feed_grad(place, keep, send, other, rows):
    features = (send.shape[1] - keep.shape[1]) // 2
    width = keep.shape[1] // 4
    tokens = keep.shape[0]
    shapes = part_shapes(rows, rows, features)
    hidden_spec = pl.BlockSpec(
        (tokens, width), lambda kind, y_step, where: (0, 2 * (1 - kind) + y_step)
    )
    row_spec = pl.BlockSpec(
        (tokens, features), lambda kind, y_step, where: (0, 4 * width // features + kind)
    )
    return pl.pallas_call(
        feed_grad_kernel,
        out_shape=shapes,
        grid_spec=pltpu.PrefetchScalarGridSpec(
            num_scalar_prefetch=1,
            grid=(2, 2),
            in_specs=[hidden_spec, row_spec, hidden_spec, row_spec],
            out_specs=[fixed(shape.shape) for shape in shapes],
        ),
        compiler_params=pltpu.CompilerParams(vmem_limit_bytes=36 * MIB),
        cost_estimate=pl.CostEstimate(
            flops=4 * tokens * features * keep.shape[1],
            bytes_accessed=24 * tokens * features,
            transcendentals=0,
        ),
        name="feed_grad",
    )(place, keep, send, other, other)


def cross_backward(
    two_grad,
    first_in,
    second_in,
    norm,
    w_cross,
    w_cross_out,
    queries,
    heads,
    key_values,
    norm_grads,
):
    features = first_in.shape[1]
    count = queries.shape[0]
    items = key_values.shape[0] // SLOT
    rows = (items + 3) * SLOT
    arrays = (
        two_grad,
        first_in,
        second_in,
        norm,
        w_cross,
        w_cross_out,
        queries,
        heads,
        key_values,
        norm_grads,
    )
    specs = [fixed(each.shape) for each in arrays]
    specs[8] = pl.BlockSpec(
        (SLOT, 2 * features), lambda item: (jnp.minimum(item, items - 1), 0)
    )
    row_spec = pl.BlockSpec((SLOT, features), lambda item: (item, 0))
    return pl.pallas_call(
        cross_backward_kernel,
        grid=(items + 3,),
        out_shape=(
            shape_of(rows, features),
            shape_of(rows, features),
            shape_of(count, features, dtype=F32),
            shape_of(NORM_ROWS, features, dtype=F32),
        ),
        in_specs=specs,
        out_specs=(row_spec, row_spec, fixed((count, features)), fixed((NORM_ROWS, features))),
        scratch_shapes=[pltpu.VMEM((count, features), BF16)] * 3,
        compiler_params=pltpu.CompilerParams(vmem_limit_bytes=36 * MIB),
        cost_estimate=pl.CostEstimate(
            flops=20 * count * features * features,
            bytes_accessed=12 * rows * features,
            transcendentals=0,
        ),
        name="cross_backward",
    )(*arrays)


def image_grad(place, feats, keep, other):
    features = keep.shape[1]
    items, patches, encoded = feats.shape
    rows = items * SLOT
    piece = encoded // GROUPS // 2 + 2 * (features // MODEL // GROUPS)
    steps = 4
    block = rows // steps
    last = steps // 2 - 1
    shapes = part_shapes(IMAGE_SPLIT, piece - IMAGE_SPLIT, features)
    out_specs = [pl.BlockSpec(shape.shape, lambda step, where: (0, 0, 0, 0)) for shape in shapes]
    rest = pl.BlockSpec((4 * SLOT, features), lambda step, where: (items // 8, 0))
    return pl.pallas_call(
        functools.partial(image_grad_kernel, items // 2 * QUERIES),
        out_shape=shapes,
        grid_spec=pltpu.PrefetchScalarGridSpec(
            num_scalar_prefetch=1,
            grid=(steps,),
            in_specs=[
                pl.BlockSpec(
                    (items // steps, patches, encoded),
                    lambda step, where: (
                        (step + where[2 * GROUPS] // (items // steps)) % steps,
                        0,
                        0,
                    ),
                ),
                pl.BlockSpec((block, features), lambda step, where: (jnp.minimum(step, last), 0)),
                pl.BlockSpec(
                    (block, features), lambda step, where: (jnp.maximum(step - last - 1, 0), 0)
                ),
                rest,
                rest,
            ],
            out_specs=out_specs,
            scratch_shapes=[pltpu.VMEM((encoded, features), F32), pltpu.VMEM((block, encoded), BF16)],
        ),
        compiler_params=pltpu.CompilerParams(vmem_limit_bytes=34 * MIB),
        cost_estimate=pl.CostEstimate(
            flops=2 * rows * encoded * features,
            bytes_accessed=2 * rows * (encoded + features),
            transcendentals=0,
        ),
        name="image_grad",
    )(place, feats, keep, other, keep, other)


def self_backward(
    lengths,
    one_query_grad,
    two_grad,
    first_in,
    norm,
    hidden,
    qkv,
    heads,
    w_qkv,
    w_self_out,
    norm_grads,
):
    rows, features = hidden.shape
    return local_call(
        self_backward_kernel,
        (lengths,),
        (
            one_query_grad,
            two_grad,
            first_in,
            norm,
            hidden,
            qkv,
            heads,
            w_qkv,
            w_self_out,
            norm_grads,
        ),
        (
            shape_of(rows, features),
            shape_of(rows, 2 * features),
            shape_of(rows + 16, 4 * features),
            shape_of(NORM_ROWS, features, dtype=F32),
        ),
        [
            pltpu.VMEM((rows, features), F32),
            pltpu.VMEM((rows, features), BF16),
            pltpu.VMEM((rows, 3 * features), BF16),
        ],
        16 * rows * features * features,
        "self_backward",
        30,
    )


def self_grad(place, keep, send, other, norm_total):
    features = norm_total.shape[1]
    rows = features // GROUPS + NORM_ROWS
    return local_call(
        self_grad_kernel,
        (place,),
        (keep, send, other, norm_total),
        part_shapes(SELF_SPLIT, rows - SELF_SPLIT, features),
        [],
        8 * keep.shape[0] * features * features,
        "self_grad",
        24,
    )


def run_direct(hidden, feats, first_item, lengths, out_grad, image, begin, weights):
    moves = Direct(lax.axis_size("dp"), lax.axis_size("mp"))
    place = moves.place
    feats_place = jnp.concatenate([place, first_item[None].astype(jnp.int32)])
    begin_split = begin.shape[0] // 2
    image_split = image.shape[0] * 96 // 176
    feed_split = weights.shape[0] // 2

    begin = moves.spread_z(begin)
    begin, image, feats = tie(begin, image, feats)
    begin_others = moves.spread_first(begin, begin_split)
    image = moves.spread_z(image)
    begin_others, image, weights, feats = tie(begin_others, image, weights, feats)
    begin_parts = moves.join_first(begin, begin_split, begin_others)
    begin_others = moves.spread_second(begin_parts)
    image_others = moves.spread_first(image, image_split)
    weights = moves.spread_z(weights)
    begin_others, image_others, weights = tie(begin_others, image_others, weights)

    image_parts = moves.join_first(image, image_split, image_others)
    image_others = moves.spread_second(image_parts)
    weight_others = moves.spread_first(weights, feed_split)
    begin = moves.join_second(begin_parts, begin_others)
    begin_other = moves.hop_core(begin)
    first_in, qkv, heads, w_qkv, w_cross, w_self_out, w_cross_out, norm = self_forward(
        place, lengths, hidden, (begin, begin_other)
    )
    first_in, image_others, weight_others = tie(first_in, image_others, weight_others)
    image = moves.join_second(image_parts, image_others)
    weight_parts = moves.join_first(weights, feed_split, weight_others)
    image_other = moves.hop_core(image)
    weight_others = moves.spread_second(weight_parts)
    held_others = [moves.hop_core(part) for part in weight_parts]
    key_values, second_in, cross_queries, cross_heads = look(
        feats_place, feats, (image, image_other), first_in, norm, w_cross, w_cross_out
    )
    second_in, weight_others, held_others = tie(second_in, weight_others, held_others)
    last_others = [moves.hop_core(part) for part in weight_others]
    gathered = (*weight_parts, *weight_others, *held_others, *last_others)
    block_out, two_grad, feed_keep, feed_send, norm_grads = feed(
        place, lengths, first_in, second_in, norm, out_grad, gathered
    )

    feed_other = moves.hop_core(feed_send)
    cross_keep, cross_send, one_query_grad, norm_grads = cross_backward(
        two_grad,
        first_in,
        second_in,
        norm,
        w_cross,
        w_cross_out,
        cross_queries,
        cross_heads,
        key_values,
        norm_grads,
    )
    cross_send, feed_other = tie(cross_send, feed_other)
    cross_other = moves.hop_core(cross_send)
    feed_grads = feed_grad(place, feed_keep, feed_send, feed_other, feed_split)
    cross_other, feed_grads = tie(cross_other, feed_grads)
    feed_first = moves.fold_first(feed_grads)
    image_grads = image_grad(feats_place, feats, cross_keep, cross_other)
    one_query_grad, image_grads, feed_first = tie(one_query_grad, image_grads, feed_first)
    feed_second = moves.fold_second(feed_grads, feed_first)
    image_first = moves.fold_first(image_grads)
    input_grad, self_keep, self_send, norm_total = self_backward(
        lengths,
        one_query_grad,
        two_grad,
        first_in,
        norm,
        hidden,
        qkv,
        heads,
        w_qkv,
        w_self_out,
        norm_grads,
    )
    self_send, image_first, feed_second = tie(self_send, image_first, feed_second)
    self_other = moves.hop_core(self_send)
    feed_kept = moves.kept(feed_grads, feed_first, feed_second)
    feed_other = moves.ring_z(feed_kept, 1)
    image_second = moves.fold_second(image_grads, image_first)
    self_grads = self_grad(place, self_keep, self_send, self_other, norm_total)
    self_grads, feed_other = tie(self_grads, feed_other)
    self_first = moves.fold_first(self_grads)
    feed_other = moves.ring_z(feed_kept, 2, feed_other)
    feed_other, image_second = tie(feed_other, image_second)
    image_kept = moves.kept(image_grads, image_first, image_second)
    feed_other = moves.ring_z(feed_kept, 3, feed_other)
    image_other = moves.ring_z(image_kept, 1)
    self_first, image_other, feed_other = tie(self_first, image_other, feed_other)
    self_second = moves.fold_second(self_grads, self_first)
    image_other = moves.ring_z(image_kept, 2, image_other)
    feed_sum = moves.finish(feed_kept, [feed_other])
    image_other, self_second = tie(image_other, self_second)
    image_other = moves.ring_z(image_kept, 3, image_other)
    self_kept = moves.kept(self_grads, self_first, self_second)
    self_others = moves.fold_z(self_kept)
    image_sum = moves.finish(image_kept, [image_other])
    in_sum = moves.finish(self_kept, self_others)
    return block_out, input_grad, in_sum, image_sum, feed_sum


def run_plain(hidden, feats, first_item, lengths, out_grad, image, begin, weights):
    moves = Plain(lax.axis_size("dp"), lax.axis_size("mp"))
    place = moves.place
    feats_place = jnp.concatenate([place, first_item[None].astype(jnp.int32)])
    features = hidden.shape[1]
    width = features // MODEL
    block_rows, out_rows = features // GROUPS, width // GROUPS
    own_in, own_out = block_rows * GROUPS // moves.dp, out_rows * GROUPS // moves.dp
    half = block_rows // 2
    part = begin.shape[0] - NORM_ROWS
    inward = moves.collect(begin[:own_in])
    cross_out = moves.collect(begin[own_in : own_in + own_out])
    self_out = moves.collect(begin[own_in + own_out : part])
    norm_all = lax.psum(begin[part:].astype(F32), AXES).astype(BF16)
    norm_first = jnp.zeros((2, SLOTS, NORM_ROWS, features), BF16).at[0, 0].set(norm_all)
    begin = jnp.concatenate(
        [
            inward[:, :, :half],
            cross_out,
            jnp.zeros_like(norm_first),
            inward[:, :, half:],
            self_out,
            norm_first,
        ],
        axis=2,
    )
    image = moves.collect(image)
    own_up = weights.shape[0] // 2
    ups, downs = [
        moves.collect(part).reshape(2, 2, 2, 4, -1, features)
        for part in (weights[:own_up], weights[own_up:])
    ]
    gathered = tuple(
        part
        for side in range(2)
        for last in range(2)
        for part in (ups[side, last], downs[side, :, last])
    )
    first_in, qkv, heads, w_qkv, w_cross, w_self_out, w_cross_out, norm = self_forward(
        place, lengths, hidden, (begin[0], begin[1])
    )
    key_values, second_in, cross_queries, cross_heads = look(
        feats_place, feats, (image[0], image[1]), first_in, norm, w_cross, w_cross_out
    )
    block_out, two_grad, feed_keep, feed_send, norm_grads = feed(
        place, lengths, first_in, second_in, norm, out_grad, gathered
    )
    feed_half = gathered[0].shape[2]
    feed_grads = feed_grad(place, feed_keep, feed_send, moves.hop_core(feed_send), feed_half)
    cross_keep, cross_send, one_query_grad, norm_grads = cross_backward(
        two_grad,
        first_in,
        second_in,
        norm,
        w_cross,
        w_cross_out,
        cross_queries,
        cross_heads,
        key_values,
        norm_grads,
    )
    image_grads = image_grad(feats_place, feats, cross_keep, moves.hop_core(cross_send))
    input_grad, self_keep, self_send, norm_total = self_backward(
        lengths,
        one_query_grad,
        two_grad,
        first_in,
        norm,
        hidden,
        qkv,
        heads,
        w_qkv,
        w_self_out,
        norm_grads,
    )
    self_grads = self_grad(place, self_keep, self_send, moves.hop_core(self_send), norm_total)

    def beside(values):
        count = values.shape[-2] // MODEL
        return jnp.concatenate(
            [values[..., part * count : (part + 1) * count, :] for part in range(MODEL)], axis=-1
        )

    def below(values):
        count = values.shape[-1] // MODEL
        return jnp.concatenate(
            [values[..., part * count : (part + 1) * count] for part in range(MODEL)], axis=-2
        )

    grads = moves.joined(self_grads)
    in_part = moves.scatter(grads[..., :block_rows, : 3 * width])
    self_out = moves.scatter(beside(grads[..., :block_rows, 3 * width :]))
    norm_sum = lax.psum(norm_total, AXES)
    in_sum = jnp.concatenate([jnp.concatenate([in_part, below(self_out)], axis=1), norm_sum])
    grads = moves.joined(image_grads)
    image_rows = grads.shape[3] - 2 * out_rows
    image_part = grads[..., :image_rows, :]
    image_part = jnp.concatenate(
        [image_part[..., : features // 2], image_part[..., features // 2 :]], axis=3
    )
    image_part = moves.scatter(image_part)
    image_half = image_part.shape[0] // 2
    image_part = jnp.concatenate([image_part[:image_half], image_part[image_half:]], axis=1)
    cross_query = moves.scatter(below(grads[..., image_rows : image_rows + out_rows, :]))
    cross_out = moves.scatter(grads[..., image_rows + out_rows :, :])
    image_sum = jnp.concatenate([image_part, beside(cross_query), cross_out])
    grads = moves.joined(feed_grads)
    feed_sum = jnp.concatenate(
        [moves.scatter(jnp.stack(feed_grads[:2])), moves.scatter(grads[..., feed_half:, :])]
    )
    return block_out, input_grad, in_sum, image_sum, feed_sum


def per_device(
    hidden_in,
    image_feats,
    caption_lengths,
    out_grad,
    proj_in,
    proj_in_moments,
    proj_in_average,
    proj_out,
    proj_out_moments,
    proj_out_average,
    image_kv,
    image_kv_moments,
    image_kv_average,
    feed_up,
    feed_up_moments,
    feed_up_average,
    feed_down,
    feed_down_moments,
    feed_down_average,
    norm_params,
    norm_params_moments,
    norm_params_average,
):
    data_ways, model_ways = lax.axis_size("dp"), lax.axis_size("mp")
    data_index, model_index = lax.axis_index("dp"), lax.axis_index("mp")
    rows, features = hidden_in.shape
    items = rows // SEQ
    width = features // model_ways
    own_norm = norm_params.shape[1]
    norm_begin = (model_index * data_ways + data_index) * own_norm
    lengths = lax.dynamic_slice_in_dim(caption_lengths, model_index * items, items, 0)
    direct = data_ways == GROUPS and model_ways == MODEL
    if direct:
        feats = lax.dynamic_slice_in_dim(image_feats, model_index // 2 * 2 * items, 2 * items, 0)
        first_item = model_index % 2 * items
    else:
        feats = jnp.concatenate(
            [
                lax.dynamic_slice_in_dim(image_feats, (model_index % 2 + 2 * side) * items, items, 0)
                for side in range(2)
            ]
        )
        first_item = model_index // 2 * items
    image_piece = jnp.concatenate([image_kv[0], image_kv[1]], axis=1).astype(BF16)
    in_piece = jnp.concatenate([proj_in[kind] for kind in range(4)], axis=1).astype(BF16)
    out_pieces = [proj_out[kind].astype(BF16) for kind in range(2)]
    feed_piece = jnp.concatenate([feed_up, feed_down], axis=0).astype(BF16)
    norm_rows = lax.dynamic_update_slice(
        jnp.zeros((NORM_ROWS, features), F32), norm_params, (0, norm_begin)
    ).astype(BF16)
    own_in, own_out, own_image = proj_in.shape[1], proj_out.shape[1], image_kv.shape[1]
    if direct:
        run, half = run_direct, own_in // 2
        begin_piece = jnp.concatenate(
            [
                in_piece[:half],
                out_pieces[1],
                jnp.zeros_like(norm_rows),
                in_piece[half:],
                out_pieces[0],
                norm_rows,
            ],
            axis=0,
        )
    else:
        run = run_plain
        begin_piece = jnp.concatenate(
            [in_piece, out_pieces[1], out_pieces[0], norm_rows], axis=0
        )
    block_out, input_grad, in_sum, image_sum, feed_sum = run(
        hidden_in, feats, first_item, lengths, out_grad, image_piece, begin_piece, feed_piece
    )
    norm_shard = lax.dynamic_slice(in_sum[own_in:], (0, norm_begin), norm_params.shape)
    up_next, down_next, up_update, down_update, feed_squares = update_call(
        feed_update_kernel,
        (feed_sum, feed_up, feed_up_moments, feed_down, feed_down_moments),
        (feed_up_moments, feed_down_moments),
        (feed_up, feed_down),
        "feed_update",
    )
    image_next, image_update, image_squares = update_call(
        image_update_kernel,
        (image_sum, image_kv, image_kv_moments),
        (image_kv_moments,),
        (image_kv,),
        "image_update",
    )
    in_next, out_next, norm_next, in_update, out_update, norm_update, last_squares = update_call(
        last_update_kernel,
        (
            in_sum,
            image_sum,
            norm_shard,
            proj_in,
            proj_in_moments,
            proj_out,
            proj_out_moments,
            norm_params,
            norm_params_moments,
        ),
        (proj_in_moments, proj_out_moments, norm_params_moments),
        (proj_in, proj_out, norm_params),
        "last_update",
    )
    own_squares = feed_squares + image_squares + last_squares
    ways = data_ways * model_ways
    copies = jnp.broadcast_to(own_squares[None], (ways,) + own_squares.shape)
    squares = lax.all_to_all(copies, AXES, 0, 0, tiled=True)
    results = apply_call(
        squares,
        (proj_in, proj_out, image_kv, feed_up, feed_down, norm_params),
        (
            proj_in_average,
            proj_out_average,
            image_kv_average,
            feed_up_average,
            feed_down_average,
            norm_params_average,
        ),
        (in_update, out_update, image_update, up_update, down_update, norm_update),
    )
    new_weights, new_averages, (trust, norms) = results[:6], results[6:12], results[12:]
    moments = (in_next, out_next, image_next, up_next, down_next, norm_next)
    outputs = [
        each for group in zip(new_weights, moments, new_averages) for each in group
    ]
    tensors = sum(each.shape[0] for each in (proj_in, proj_out, image_kv, norm_params)) + 2
    return (block_out, input_grad, *outputs, trust[0, :tensors], norms[:, :tensors])


def solution(mesh):
    rows = P(AXES, None)
    by_column = P(None, "dp", "mp")
    by_row = P(None, ("mp", "dp"), None)
    weights = (
        by_column,
        P(None, None, "dp", "mp"),
        by_column,
        by_row,
        P(None, None, ("mp", "dp"), None),
        by_row,
        by_column,
        P(None, None, "dp", "mp"),
        by_column,
        P("dp", "mp"),
        P(None, "dp", "mp"),
        P("dp", "mp"),
        P(("mp", "dp"), None),
        P(None, ("mp", "dp"), None),
        P(("mp", "dp"), None),
        P(None, ("mp", "dp")),
        P(None, None, ("mp", "dp")),
        P(None, ("mp", "dp")),
    )
    return jax.shard_map(
        per_device,
        mesh=mesh,
        in_specs=(rows, P("dp", None, None), P("dp"), rows, *weights),
        out_specs=(rows, rows, *weights, P(), P()),
        check_vma=False,
    )
```

```python
import functools

import jax
import jax.numpy as jnp
from jax import lax
from jax.experimental import pallas as pl
from jax.experimental.pallas import tpu as pltpu
from jax.sharding import PartitionSpec as P

HEAD = 64
PATCHES = 257
QUERIES = 32
TEXT = 32
SEQ = QUERIES + TEXT
STEP = 10


NORM_EPSILON = 1e-06
ADAM_EPSILON = 1e-06
SQUARE_EPSILON = 1e-06
BETA_ONE = 0.9
BETA_TWO = 0.999
LEARN_RATE = 0.5
DECAY_RATE = 0.01
AVERAGE_RATE = 0.6
MASK_VALUE = -1e30

AXES = ("dp", "mp")
GROUPS = 8
MODEL = 4
SLOTS = 16
NORM_ROWS = 8
LANES = 128
IMAGE_SPLIT = 64
SELF_SPLIT = 48
BLOCK = 128
WIDE = 256
HEADS_AT_ONCE = 12
SLOT = 272
MIB = 1024 * 1024

BF16 = jnp.bfloat16
F32 = jnp.float32


def dot_nn(left_side, right_side):
    return lax.dot_general(
        left_side, right_side, (((1,), (0,)), ((), ())), preferred_element_type=F32
    )


def dot_nt(left_side, right_side):
    return lax.dot_general(
        left_side, right_side, (((1,), (1,)), ((), ())), preferred_element_type=F32
    )


def dot_tn(left_side, right_side):
    return lax.dot_general(
        left_side, right_side, (((0,), (0,)), ((), ())), preferred_element_type=F32
    )


def normalise(inputs):
    centred = inputs - jnp.mean(inputs, axis=-1, keepdims=True)
    inverse = lax.rsqrt(jnp.mean(centred * centred, axis=-1, keepdims=True) + NORM_EPSILON)
    return centred * inverse, inverse


def norm_back(gradient, normed, inverse, gain):
    scaled = gradient * gain
    centre_term = jnp.mean(scaled, axis=-1, keepdims=True)
    normed_term = jnp.mean(scaled * normed, axis=-1, keepdims=True)
    return inverse * (scaled - centre_term - normed * normed_term)


def slot_of(place, block, y_rel):
    return place[block] * 8 + y_rel * 4 + place[GROUPS + block]


def softmax(scores):
    tops = [jnp.max(each, axis=-1, keepdims=True) for each in scores]
    exponents = [jnp.exp(each - top) for each, top in zip(scores, tops)]
    totals = [jnp.sum(each, axis=-1, keepdims=True) for each in exponents]
    return [each / total for each, total in zip(exponents, totals)]


def block_mask(lengths, first_item):
    per_block = BLOCK // SEQ
    row = lax.broadcasted_iota(jnp.int32, (BLOCK, BLOCK), 0)
    column = lax.broadcasted_iota(jnp.int32, (BLOCK, BLOCK), 1)
    row_item, column_item = lax.shift_right_logical(row, 6), lax.shift_right_logical(column, 6)
    slot = column - column_item * SEQ
    limit = jnp.zeros((BLOCK, BLOCK), jnp.int32)
    for item in range(per_block):
        limit = jnp.where(column_item == item, lengths[first_item + item] + QUERIES, limit)
    return (row_item == column_item) & (slot < limit)


def self_forward_kernel(
    place,
    lengths,
    hidden,
    begin_own,
    begin_other,
    first_in,
    qkv,
    heads,
    w_qkv,
    w_cross,
    w_self_out,
    w_cross_out,
    norm,
    self_rows,
    cross_rows,
):
    rows, features = hidden.shape
    width = features // MODEL
    block_rows = features // GROUPS
    out_rows = width // GROUPS
    half, part = block_rows // 2, begin_own.shape[1] // 2
    norm_sum = jnp.zeros((NORM_ROWS, features), F32)
    for block in range(GROUPS):
        pieces = []
        for model in range(MODEL):
            side, y_rel = divmod(model, 2)
            source, slot = (begin_own, begin_other)[side], slot_of(place, block, y_rel)
            pieces.append(
                jnp.concatenate(
                    [source[slot, :half, :], source[slot, part : part + half, :]], axis=0
                )
            )
            cross_part = source[slot, half:part, :].astype(F32)
            self_part = source[slot, part + half :, :].astype(F32)
            begin = model * width + block * out_rows
            cross_rows[begin : begin + out_rows, :] = cross_part[:out_rows]
            self_rows[begin : begin + out_rows, :] = self_part[:out_rows]
            norm_sum = norm_sum + self_part[out_rows:]
        begin = block * block_rows
        for kind in range(4):
            joined = jnp.concatenate(
                [piece[:, kind * width : (kind + 1) * width] for piece in pieces], axis=1
            )
            if kind < 3:
                w_qkv[begin : begin + block_rows, kind * features : (kind + 1) * features] = joined
            else:
                w_cross[begin : begin + block_rows, :] = joined
    norm[...] = norm_sum
    w_self_out[...] = self_rows[...].astype(BF16)
    w_cross_out[...] = cross_rows[...].astype(BF16)
    tokens = hidden[...]
    for kind in range(3):
        columns = slice(kind * features, (kind + 1) * features)
        qkv[:, columns] = dot_nn(tokens, w_qkv[:, columns]).astype(BF16)
    scale = HEAD ** (-0.5)
    for begin in range(0, rows, BLOCK):
        span = slice(begin, begin + BLOCK)
        mask = block_mask(lengths, begin // SEQ)
        for first in range(0, features // HEAD, HEADS_AT_ONCE):
            queries, key_rows, value_rows = [
                [
                    qkv[span, kind * features + head * HEAD : kind * features + (head + 1) * HEAD]
                    for head in range(first, first + HEADS_AT_ONCE)
                ]
                for kind in range(3)
            ]
            scores = [dot_nt(*pair) for pair in zip(queries, key_rows)]
            probs = softmax([jnp.where(mask, each * scale, MASK_VALUE) for each in scores])
            mixed = [dot_nn(*pair) for pair in zip([each.astype(BF16) for each in probs], value_rows)]
            heads[span, first * HEAD : (first + HEADS_AT_ONCE) * HEAD] = jnp.concatenate(
                [each.astype(BF16) for each in mixed], axis=1
            )
    first_in[...] = tokens.astype(F32) + dot_nn(heads[...], w_self_out[...])


def assemble_image(place, image_own, image_other, weight):
    block_rows = image_own.shape[1]
    width = image_own.shape[2] // 2
    features = width * MODEL
    for block in range(GROUPS):
        pieces = []
        for model in range(MODEL):
            side, y_rel = divmod(model, 2)
            pieces.append((image_own, image_other)[side][slot_of(place, block, y_rel)])
        begin = block * block_rows
        for kind in range(2):
            weight[begin : begin + block_rows, kind * features : (kind + 1) * features] = (
                jnp.concatenate(
                    [piece[:, kind * width : (kind + 1) * width] for piece in pieces], axis=1
                )
            )


def head_rows(values, head_mask):
    stacked = jnp.concatenate([values] * (WIDE // HEAD), axis=0)
    return jnp.where(head_mask, stacked, jnp.zeros_like(stacked))


def fold_heads(values, head_mask):
    kept = jnp.where(head_mask, values, 0.0)
    count = WIDE // HEAD
    size = values.shape[0] // count
    total = kept[:size]
    for index in range(1, count):
        total = total + kept[index * size : (index + 1) * size]
    return total


def query_head_mask():
    shape = (QUERIES * (WIDE // HEAD), WIDE)
    row = lax.broadcasted_iota(jnp.int32, shape, 0)
    column = lax.broadcasted_iota(jnp.int32, shape, 1)
    return lax.shift_right_logical(row, 5) == lax.shift_right_logical(column, 6)


def patch_softmax(queries, keys):
    scores = [dot_nt(*pair) * HEAD ** (-0.5) for pair in zip(queries, keys)]
    column = lax.broadcasted_iota(jnp.int32, scores[0].shape, 1)
    return softmax([jnp.where(column < PATCHES, each, MASK_VALUE) for each in scores])


def query_rows(values):
    items = values.shape[0] // SEQ
    return jnp.concatenate(
        [values[item * SEQ : item * SEQ + QUERIES] for item in range(items)], axis=0
    )


def look_kernel(
    place,
    feats,
    image_own,
    image_other,
    first_in,
    norm,
    w_cross,
    w_cross_out,
    key_values,
    second_in,
    queries,
    heads,
    weight,
):
    features = first_in.shape[1]
    patches = feats.shape[1]
    step, steps = pl.program_id(0), pl.num_programs(0)

    @pl.when(step == 0)
    def _():
        assemble_image(place, image_own, image_other, weight)
        normed, _ = normalise(query_rows(first_in[...]))
        one_query = normed * norm[0:1, :] + norm[1:2, :]
        second_in[...] = one_query
        queries[...] = dot_nn(one_query.astype(BF16), w_cross[...]).astype(BF16)

    key_values[:patches, :] = dot_nn(feats[0], weight[...]).astype(BF16)
    key_values[patches:, :] = jnp.zeros((SLOT - patches, weight.shape[1]), BF16)
    head_mask = query_head_mask()
    span = pl.ds(pl.multiple_of(step * QUERIES, QUERIES), QUERIES)
    columns = [slice(begin, begin + WIDE) for begin in range(0, features, WIDE)]
    value_columns = [slice(features + each.start, features + each.stop) for each in columns]
    expanded = [head_rows(queries[span, each], head_mask) for each in columns]
    probs = patch_softmax(expanded, [key_values[:, each] for each in columns])
    mixed = [
        dot_nn(prob.astype(BF16), key_values[:, each]) for prob, each in zip(probs, value_columns)
    ]
    for each, values in zip(columns, mixed):
        heads[span, each] = fold_heads(values, head_mask).astype(BF16)

    @pl.when(step == steps - 1)
    def _():
        second_in[...] += dot_nn(heads[...], w_cross_out[...])


def gelu_cumulative(inputs):
    return 0.5 * (1.0 + lax.erf(inputs * 0.7071067811865476))


def feed_kernel(
    place,
    lengths,
    norm,
    first_hbm,
    second_hbm,
    out_grad_hbm,
    up_first,
    down_first,
    up_last,
    down_last,
    up_first_other,
    down_first_other,
    up_last_other,
    down_last_other,
    block_out,
    two_grad,
    keep_hbm,
    send_hbm,
    norm_grads,
    first_in,
    second_in,
    out_grad,
    w_up,
    w_down,
    two_rows,
    pre_act,
    result,
    keep,
    send,
    in_sem,
    up_sem,
    down_sem,
    keep_sem,
    send_sem,
    out_sem,
):
    rows, features = first_in.shape
    items = rows // SEQ
    hidden_width = up_first.shape[3]
    piece_rows = up_first.shape[2]
    half = 2 * hidden_width
    up_parts = ((up_first, up_last), (up_first_other, up_last_other))
    down_parts = ((down_first, down_last), (down_first_other, down_last_other))

    def put(target, source, begin, width, semaphore):
        columns = pl.ds(begin, width)
        copy = pltpu.make_async_copy(source.at[:, columns], target.at[:, columns], semaphore)
        copy.start()
        return copy

    entries = [
        pltpu.make_async_copy(source, target, in_sem.at[index])
        for index, (source, target) in enumerate(
            ((first_hbm, first_in), (second_hbm, second_in), (out_grad_hbm, out_grad))
        )
    ]
    entries[0].start()
    entries[1].start()
    for first in range(2):

        @pl.when(place[0] == first)
        def _():
            for model in range(MODEL):
                side, y_rel = divmod(model, 2)
                for block in range(GROUPS):
                    source = up_parts[side][(block + first) % 2]
                    pltpu.make_async_copy(
                        source.at[y_rel, place[GROUPS + block]],
                        w_up.at[model, pl.ds(block * piece_rows, piece_rows), :],
                        up_sem.at[model],
                    ).start()
                for block in range(GROUPS):
                    source = down_parts[side][y_rel]
                    pltpu.make_async_copy(
                        source.at[(block + first) % 2, place[GROUPS + block]],
                        w_down.at[model, pl.ds(block * piece_rows, piece_rows), :],
                        down_sem.at[model],
                    ).start()

    entries[2].start()
    entries[0].wait()
    entries[1].wait()
    copies = []
    normed_one, _ = normalise(first_in[...])
    after_one = normed_one * norm[0:1, :] + norm[1:2, :]
    normed_two, _ = normalise(second_in[...])
    after_two = normed_two * norm[2:3, :] + norm[3:4, :]
    for item in range(items):
        begin = item * SEQ
        two_rows[begin : begin + QUERIES, :] = after_two[item * QUERIES : (item + 1) * QUERIES]
        two_rows[begin + QUERIES : begin + SEQ, :] = after_one[begin + QUERIES : begin + SEQ]
    feed_in = two_rows[...].astype(BF16)
    send[:, 2 * half : 2 * half + features] = feed_in
    copies.append(put(send_hbm, send, 2 * half, features, send_sem.at[4]))
    third_in = two_rows[...]
    for model in range(MODEL):
        side, y_rel = divmod(model, 2)
        target = (keep, send)[side]
        begin = y_rel * hidden_width
        pltpu.make_async_copy(w_up.at[model], w_up.at[model], up_sem.at[model]).wait()
        pre = dot_nn(feed_in, w_up[model])
        pre_act[:, model * hidden_width : (model + 1) * hidden_width] = pre
        act = (pre * gelu_cumulative(pre)).astype(BF16)
        target[:, begin : begin + hidden_width] = act
        semaphore = (keep_sem, send_sem)[side].at[y_rel]
        copies.append(put((keep_hbm, send_hbm)[side], target, begin, hidden_width, semaphore))
        pltpu.make_async_copy(w_down.at[model], w_down.at[model], down_sem.at[model]).wait()
        third_in = third_in + dot_nn(act, w_down[model])
    normed, inverse = normalise(third_in)
    result[...] = (normed * norm[4:5, :] + norm[5:6, :]).astype(BF16)
    copies.append(pltpu.make_async_copy(result, block_out, out_sem.at[0]))
    copies[-1].start()
    entries[2].wait()
    position = lax.broadcasted_iota(jnp.int32, (SEQ, features), 0)
    slope = jnp.concatenate(
        [
            jnp.where(
                position < lengths[item] + QUERIES,
                out_grad[item * SEQ : (item + 1) * SEQ, :].astype(F32),
                0.0,
            )
            for item in range(items)
        ],
        axis=0,
    )
    norm_grads[...] = jnp.zeros_like(norm_grads)
    norm_grads[4:5, :] = jnp.sum(slope * normed, axis=0, keepdims=True)
    norm_grads[5:6, :] = jnp.sum(slope, axis=0, keepdims=True)
    third_grad = norm_back(slope, normed, inverse, norm[4:5, :])
    grad_rows = third_grad.astype(BF16)
    send[:, 2 * half + features :] = grad_rows
    copies.append(put(send_hbm, send, 2 * half + features, features, send_sem.at[5]))
    total = third_grad
    for model in range(MODEL):
        side, y_rel = divmod(model, 2)
        target = (keep, send)[side]
        begin = half + y_rel * hidden_width
        pre = pre_act[:, model * hidden_width : (model + 1) * hidden_width]
        density = jnp.exp(-0.5 * pre * pre) * 0.3989422804014327
        slope_part = gelu_cumulative(pre) + pre * density
        grad_pre = (dot_nt(grad_rows, w_down[model]) * slope_part).astype(BF16)
        target[:, begin : begin + hidden_width] = grad_pre
        semaphore = (keep_sem, send_sem)[side].at[2 + y_rel]
        copies.append(put((keep_hbm, send_hbm)[side], target, begin, hidden_width, semaphore))
        total = total + dot_nt(grad_pre, w_up[model])
    two_rows[...] = total
    copies.append(pltpu.make_async_copy(two_rows, two_grad, out_sem.at[1]))
    copies[-1].start()
    for copy in copies:
        copy.wait()


def put_left(place, block, y_rel, keep, send, value):
    for along_x, target in ((0, keep), (1, send)):

        @pl.when(place[block] == along_x)
        def _(target=target):
            target[y_rel, place[GROUPS + block]] = value


def put_right(place, block, y_rel, keep, send, value):
    (keep, send)[y_rel][place[block], place[GROUPS + block]] = value


def feed_grad_kernel(
    place, hidden, rows, hidden_other, rows_other, left_keep, left_send, right_keep, right_send
):
    piece_rows = left_keep.shape[2]
    kind, y_step = pl.program_id(0), pl.program_id(1)

    @pl.when(kind == 0)
    def _():
        grad_up = dot_tn(rows[...], hidden[...])
        grad_up = (grad_up + dot_tn(rows_other[...], hidden_other[...])).astype(BF16)
        for block in range(GROUPS):
            span = slice(block * piece_rows, (block + 1) * piece_rows)
            put_left(place, block, y_step, left_keep, left_send, grad_up[span])

    for y_rel in range(2):

        @pl.when((kind == 1) & (y_step == y_rel))
        def _(y_rel=y_rel):
            grad_down = dot_tn(hidden[...], rows[...])
            grad_down = (grad_down + dot_tn(hidden_other[...], rows_other[...])).astype(BF16)
            for block in range(GROUPS):
                span = slice(block * piece_rows, (block + 1) * piece_rows)
                put_right(place, block, y_rel, right_keep, right_send, grad_down[span])


def cross_backward_kernel(
    two_grad,
    first_in,
    second_in,
    norm,
    w_cross,
    w_cross_out,
    queries,
    heads,
    key_values,
    norm_grads_in,
    keep,
    send,
    one_query_grad,
    norm_grads,
    head_grads,
    query_grads,
    grad_rows,
):
    features = first_in.shape[1]
    half = features // 2
    count = queries.shape[0]
    step = pl.program_id(0)
    items = pl.num_programs(0) - 3
    scale = HEAD ** (-0.5)

    @pl.when(step == 0)
    def _():
        two_query = query_rows(two_grad[...])
        normed, inverse = normalise(second_in[...])
        norm_grads[...] = norm_grads_in[...]
        norm_grads[2:3, :] = jnp.sum(two_query * normed, axis=0, keepdims=True)
        norm_grads[3:4, :] = jnp.sum(two_query, axis=0, keepdims=True)
        second_grad = norm_back(two_query, normed, inverse, norm[2:3, :])
        one_query_grad[...] = second_grad
        grad_rows[...] = second_grad.astype(BF16)
        head_grads[...] = dot_nt(grad_rows[...], w_cross_out[...]).astype(BF16)

    @pl.when(step < items)
    def _():
        head_mask = query_head_mask()
        span = pl.ds(pl.multiple_of(step * QUERIES, QUERIES), QUERIES)
        columns = [slice(begin, begin + WIDE) for begin in range(0, features, WIDE)]
        keys = [key_values[:, each] for each in columns]
        value_rows = [
            key_values[:, features + each.start : features + each.stop] for each in columns
        ]
        expanded = [head_rows(queries[span, each], head_mask) for each in columns]
        slopes = [head_rows(head_grads[span, each], head_mask) for each in columns]
        grad_probs = [dot_nt(*pair) for pair in zip(slopes, value_rows)]
        probs = patch_softmax(expanded, keys)
        inner = [
            jnp.sum(each * prob, axis=-1, keepdims=True) for each, prob in zip(grad_probs, probs)
        ]
        grad_scores = [
            (prob * (each - total)).astype(BF16)
            for prob, each, total in zip(probs, grad_probs, inner)
        ]
        grad_values = [
            dot_tn(prob.astype(BF16), slope).astype(BF16) for prob, slope in zip(probs, slopes)
        ]
        grad_keys = [
            (dot_tn(*pair) * scale).astype(BF16) for pair in zip(grad_scores, expanded)
        ]
        grad_queries = [dot_nn(*pair) for pair in zip(grad_scores, keys)]
        for index, each in enumerate(columns):
            query_grads[span, each] = (
                fold_heads(grad_queries[index], head_mask) * scale
            ).astype(BF16)
            for part in range(0, WIDE, WIDE // 2):
                side, place_at = divmod(each.start + part, half)
                target, lanes = (keep, send)[side], slice(part, part + WIDE // 2)
                target[:, place_at : place_at + WIDE // 2] = grad_keys[index][:, lanes]
                place_at += half
                target[:, place_at : place_at + WIDE // 2] = grad_values[index][:, lanes]

    @pl.when(step >= items)
    def _():
        for target in (keep, send):
            target[count:, :] = jnp.zeros((SLOT - count, features), BF16)

    @pl.when(step == items)
    def _():
        normed_one, _ = normalise(query_rows(first_in[...]))
        query_in = (normed_one * norm[0:1, :] + norm[1:2, :]).astype(BF16)
        for target in (keep, send):
            target[:count, :] = query_in

    @pl.when(step == items + 1)
    def _():
        for target in (keep, send):
            target[:count, :] = grad_rows[...]

    @pl.when(step == items + 2)
    def _():
        for side, target in enumerate((keep, send)):
            columns = slice(side * half, (side + 1) * half)
            target[:count, :half] = query_grads[:, columns]
            target[:count, half:] = heads[:, columns]
        one_query_grad[...] += dot_nt(query_grads[...], w_cross[...])


def image_grad_kernel(
    count,
    place,
    feats,
    keep_rows,
    other_rows,
    keep,
    other,
    left_keep,
    left_send,
    right_keep,
    right_send,
    total,
    spread,
):
    features = keep.shape[1]
    half = features // 2
    width = half // 2
    image_rows = feats.shape[2] // GROUPS
    image_half = image_rows // 2
    block_rows = features // GROUPS
    out_rows = width // GROUPS
    split = left_keep.shape[2]
    step, steps = pl.program_id(0), pl.num_programs(0)

    @pl.when(step == 0)
    def _():
        spread[...] = jnp.zeros_like(spread)

    for item in range(feats.shape[0]):
        spread[item * SLOT : item * SLOT + feats.shape[1], :] = feats[item]

    @pl.when(step == 0)
    def _():
        total[...] = dot_tn(spread[...], keep_rows[...])

    @pl.when((step > 0) & (step < steps // 2))
    def _():
        total[...] += dot_tn(spread[...], keep_rows[...])

    @pl.when(step >= steps // 2)
    def _():
        total[...] += dot_tn(spread[...], other_rows[...])

    @pl.when(step == steps - 1)
    def _():
        inputs, slopes = slice(0, count), slice(SLOT, SLOT + count)
        parts = slice(2 * SLOT, 2 * SLOT + count)
        grad_query = dot_tn(keep[inputs, :], keep[parts, :half]) + dot_tn(
            other[inputs, :], other[parts, :half]
        )
        grad_out = dot_tn(keep[parts, half:], keep[slopes, :]) + dot_tn(
            other[parts, half:], other[slopes, :]
        )
        for block in range(GROUPS):
            for y_rel in range(2):
                columns = slice(y_rel * width, (y_rel + 1) * width)
                image_part = [
                    total[
                        begin : begin + image_half,
                        kind + y_rel * width : kind + (y_rel + 1) * width,
                    ]
                    for begin in (block * image_rows, block * image_rows + image_half)
                    for kind in (0, half)
                ]
                begin = block * block_rows
                cross_part = [
                    grad_query[begin + part * out_rows : begin + (part + 1) * out_rows, columns]
                    for part in range(MODEL)
                ]
                begin = y_rel * width + block * out_rows
                piece = jnp.concatenate(
                    [
                        jnp.concatenate(image_part, axis=1),
                        jnp.concatenate(cross_part, axis=1),
                        grad_out[begin : begin + out_rows],
                    ],
                    axis=0,
                )
                put_left(place, block, y_rel, left_keep, left_send, piece[:split].astype(BF16))
                put_right(place, block, y_rel, right_keep, right_send, piece[split:].astype(BF16))


def self_backward_kernel(
    lengths,
    one_query_grad,
    two_grad,
    first_in,
    norm,
    hidden,
    qkv,
    heads,
    w_qkv,
    w_self_out,
    norm_grads_in,
    input_grad,
    keep,
    send,
    norm_total,
    one_grad,
    head_grads,
    grad_qkv,
):
    rows, features = hidden.shape
    items = rows // SEQ
    half = features // 2
    for item in range(items):
        begin = item * SEQ
        one_grad[begin : begin + QUERIES, :] = one_query_grad[
            item * QUERIES : (item + 1) * QUERIES, :
        ]
        one_grad[begin + QUERIES : begin + SEQ, :] = two_grad[begin + QUERIES : begin + SEQ, :]
    normed, inverse = normalise(first_in[...])
    gradient = one_grad[...]
    norm_sum = norm_grads_in[...] + jnp.concatenate(
        [
            jnp.sum(gradient * normed, axis=0, keepdims=True),
            jnp.sum(gradient, axis=0, keepdims=True),
            jnp.zeros((NORM_ROWS - 2, features), F32),
        ],
        axis=0,
    )
    norm_total[...] = norm_sum
    first_grad = norm_back(gradient, normed, inverse, norm[0:1, :])
    one_grad[...] = first_grad
    grad_rows = first_grad.astype(BF16)
    head_grads[...] = dot_nt(grad_rows, w_self_out[...]).astype(BF16)
    scale = HEAD ** (-0.5)
    for begin in range(0, rows, BLOCK):
        span = slice(begin, begin + BLOCK)
        mask = block_mask(lengths, begin // SEQ)
        for first in range(0, features // HEAD, HEADS_AT_ONCE):
            chosen = range(first, first + HEADS_AT_ONCE)
            queries, key_rows, value_rows = [
                [
                    qkv[span, kind * features + head * HEAD : kind * features + (head + 1) * HEAD]
                    for head in chosen
                ]
                for kind in range(3)
            ]
            slopes = [head_grads[span, head * HEAD : (head + 1) * HEAD] for head in chosen]
            scores = [dot_nt(*pair) for pair in zip(queries, key_rows)]
            grad_probs = [dot_nt(*pair) for pair in zip(slopes, value_rows)]
            probs = softmax([jnp.where(mask, each * scale, MASK_VALUE) for each in scores])
            inner = [
                jnp.sum(each * prob, axis=-1, keepdims=True)
                for each, prob in zip(grad_probs, probs)
            ]
            grad_scores = [
                (prob * (each - total)).astype(BF16)
                for prob, each, total in zip(probs, grad_probs, inner)
            ]
            results = (
                [dot_nn(*pair) * scale for pair in zip(grad_scores, key_rows)],
                [dot_tn(*pair) * scale for pair in zip(grad_scores, queries)],
                [dot_tn(prob.astype(BF16), slope) for prob, slope in zip(probs, slopes)],
            )
            for kind in range(3):
                begin_at = kind * features + first * HEAD
                grad_qkv[span, begin_at : begin_at + HEADS_AT_ONCE * HEAD] = jnp.concatenate(
                    [each.astype(BF16) for each in results[kind]], axis=1
                )
    total = one_grad[...]
    for kind in range(3):
        columns = slice(kind * features, (kind + 1) * features)
        total = total + dot_nt(grad_qkv[:, columns], w_qkv[:, columns])
        first = kind * features
        keep[:, kind * half : (kind + 1) * half] = grad_qkv[:, first : first + half]
        send[:rows, kind * half : (kind + 1) * half] = grad_qkv[:, first + half : first + features]
    input_grad[...] = total.astype(BF16)
    keep[:, 3 * half :] = heads[:, :half]
    send[:rows, 3 * half : 4 * half] = heads[:, half:]
    send[:rows, 4 * half : 6 * half] = hidden[...]
    send[:rows, 6 * half :] = grad_rows
    send[rows:, :] = jnp.zeros((send.shape[0] - rows, send.shape[1]), BF16)
    send[rows : rows + 16, :features] = jnp.concatenate(
        [norm_sum, jnp.zeros_like(norm_sum)], axis=0
    ).astype(BF16)


def self_grad_kernel(
    place, keep, send, other, norm_total, left_keep, left_send, right_keep, right_send
):
    features = norm_total.shape[1]
    rows = keep.shape[0]
    half = features // 2
    width = half // 2
    block_rows = features // GROUPS
    out_rows = width // GROUPS
    split = left_keep.shape[2]
    inputs, slopes = slice(4 * half, 6 * half), slice(6 * half, 8 * half)
    columns = slice(0, 3 * half)
    grad_in = dot_tn(send[:rows, inputs], keep[:, columns])
    grad_in = grad_in + dot_tn(other[:rows, inputs], other[:rows, columns])
    columns = slice(3 * half, 4 * half)
    grad_out = dot_tn(keep[:, columns], send[:rows, slopes])
    grad_out = grad_out + dot_tn(other[:rows, columns], other[:rows, slopes])
    norm_rows = norm_total[...] + other[rows : rows + 16, :features].astype(F32)[:NORM_ROWS]
    for block in range(GROUPS):
        span = slice(block * block_rows, (block + 1) * block_rows)
        for y_rel in range(2):
            pieces = [
                grad_in[span, kind * half + y_rel * width : kind * half + (y_rel + 1) * width]
                for kind in range(3)
            ]
            begin = y_rel * width + block * out_rows
            out_part = grad_out[begin : begin + out_rows]
            pieces.append(
                jnp.concatenate(
                    [out_part[:, part * width : (part + 1) * width] for part in range(MODEL)],
                    axis=0,
                )
            )
            piece = jnp.concatenate([jnp.concatenate(pieces, axis=1), norm_rows], axis=0)
            put_left(place, block, y_rel, left_keep, left_send, piece[:split].astype(BF16))
            put_right(place, block, y_rel, right_keep, right_send, piece[split:].astype(BF16))


def adam_step(weight, moment_one, moment_two, gradient, decay_rate):
    moment_one = BETA_ONE * moment_one + (1.0 - BETA_ONE) * gradient
    moment_two = BETA_TWO * moment_two + (1.0 - BETA_TWO) * gradient * gradient
    update = (
        moment_one
        / (1.0 - BETA_ONE**STEP)
        / (jnp.sqrt(moment_two / (1.0 - BETA_TWO**STEP)) + ADAM_EPSILON)
        + decay_rate * weight
    )
    return moment_one, moment_two, update


def place_sums(target, sums):
    column = lax.broadcasted_iota(jnp.int32, (1, LANES), 1)
    rows = []
    for kind in range(2):
        row = jnp.zeros((1, LANES), F32)
        for index, pair in sums.items():
            row = jnp.where(column == index, pair[kind], row)
        rows.append(row)
    target[...] = jnp.concatenate(rows, axis=0)


def sum_pair(weight, update):
    return jnp.sum(weight * weight), jnp.sum(update * update)


def feed_update_kernel(
    gradient,
    up,
    up_moments,
    down,
    down_moments,
    up_next,
    down_next,
    up_update,
    down_update,
    squares,
):
    rows = up.shape[0]
    sums = {}
    for index, weight, moments, following, result, span in (
        (8, up, up_moments, up_next, up_update, slice(0, rows)),
        (9, down, down_moments, down_next, down_update, slice(rows, None)),
    ):
        following[0], following[1], update = adam_step(
            weight[...], moments[0], moments[1], gradient[span, :], DECAY_RATE
        )
        result[...] = update
        sums[index] = sum_pair(weight[...], update)
    place_sums(squares, sums)


def image_update_kernel(gradient, weight, moments, following, result, squares):
    width = weight.shape[2]
    half = weight.shape[1] // 2
    sums = {}
    for kind in range(2):
        parts = []
        for part in range(2):
            span = slice(part * half, (part + 1) * half)
            lanes = slice((2 * part + kind) * width, (2 * part + kind + 1) * width)
            following[0, kind, span, :], following[1, kind, span, :], update = adam_step(
                weight[kind, span, :],
                moments[0, kind, span, :],
                moments[1, kind, span, :],
                gradient[:half, lanes],
                DECAY_RATE,
            )
            result[kind, span, :] = update
            parts.append(sum_pair(weight[kind, span, :], update))
        sums[6 + kind] = tuple(left + right for left, right in zip(*parts))
    place_sums(squares, sums)


def last_update_kernel(
    gradient,
    cross_gradient,
    norm_gradient,
    inward,
    inward_moments,
    outward,
    outward_moments,
    norm,
    norm_moments,
    inward_next,
    outward_next,
    norm_next,
    inward_update,
    outward_update,
    norm_update,
    squares,
):
    own_in, width = inward.shape[1:]
    own_out = outward.shape[1]
    cross_rows = cross_gradient.shape[0] - 2 * own_out
    cross_query = cross_gradient[cross_rows : cross_rows + own_out, :]
    gradients = [gradient[:own_in, kind * width : (kind + 1) * width] for kind in range(3)]
    gradients.append(
        jnp.concatenate(
            [cross_query[:, part * width : (part + 1) * width] for part in range(MODEL)], axis=0
        )
    )
    sums = {}
    for kind in range(4):
        inward_next[0, kind], inward_next[1, kind], update = adam_step(
            inward[kind],
            inward_moments[0, kind],
            inward_moments[1, kind],
            gradients[kind],
            DECAY_RATE,
        )
        inward_update[kind] = update
        sums[kind] = sum_pair(inward[kind], update)
    folded = gradient[:own_in, 3 * width :]
    self_out = jnp.concatenate(
        [folded[part * own_out : (part + 1) * own_out] for part in range(MODEL)], axis=1
    )
    for kind, part in enumerate((self_out, cross_gradient[cross_rows + own_out :, :])):
        outward_next[0, kind], outward_next[1, kind], update = adam_step(
            outward[kind], outward_moments[0, kind], outward_moments[1, kind], part, DECAY_RATE
        )
        outward_update[kind] = update
        sums[4 + kind] = sum_pair(outward[kind], update)
    norm_next[0], norm_next[1], update = adam_step(
        norm[...], norm_moments[0], norm_moments[1], norm_gradient[...], 0.0
    )
    norm_update[...] = update
    for kind in range(norm.shape[0]):
        sums[10 + kind] = sum_pair(norm[kind : kind + 1, :], update[kind : kind + 1, :])
    place_sums(squares, sums)


def apply_kernel(squares, *refs):
    groups = len(refs) // 5
    weights, averages, updates = refs[:groups], refs[groups : 2 * groups], refs[2 * groups : 3 * groups]
    new_weights, new_averages = refs[3 * groups : 4 * groups], refs[4 * groups : 5 * groups]
    trust_out, norms_out = refs[5 * groups :]
    sums = jnp.sum(squares[...], axis=0)
    trust = jnp.sqrt(sums[0:1]) * lax.rsqrt(sums[1:2] + SQUARE_EPSILON)
    trust_out[...] = trust
    norms_out[...] = jnp.sqrt(sums)
    column = lax.broadcasted_iota(jnp.int32, trust.shape, 1)

    def ratio(index):
        return jnp.sum(jnp.where(column == index, trust, 0.0), axis=1, keepdims=True)

    index = 0
    for weight, average, update, new_weight, new_average in zip(
        weights, averages, updates, new_weights, new_averages
    ):
        if len(weight.shape) == 3:
            spans = list(range(weight.shape[0]))
        elif weight.shape[0] == 6:
            spans = [slice(row, row + 1) for row in range(6)]
        else:
            spans = [slice(None)]
        for span in spans:
            value = weight[span] - LEARN_RATE * ratio(index) * update[span]
            new_weight[span] = value
            new_average[span] = AVERAGE_RATE * average[span] + (1.0 - AVERAGE_RATE) * value
            index += 1


SCALARS = pl.BlockSpec(memory_space=pltpu.SMEM)
WHOLE = pl.BlockSpec(memory_space=pltpu.VMEM)


def local_call(kernel, scalars, arrays, out_shapes, scratch, flops, name, limit):
    size = sum(a.size * a.dtype.itemsize for a in arrays)
    size += sum(a.size * a.dtype.itemsize for a in out_shapes)
    return pl.pallas_call(
        kernel,
        out_shape=tuple(out_shapes),
        in_specs=[SCALARS] * len(scalars) + [WHOLE] * len(arrays),
        out_specs=tuple([WHOLE] * len(out_shapes)),
        scratch_shapes=scratch,
        compiler_params=pltpu.CompilerParams(vmem_limit_bytes=limit * MIB),
        cost_estimate=pl.CostEstimate(flops=flops, bytes_accessed=size, transcendentals=0),
        name=name,
    )(*scalars, *arrays)


def shape_of(*dims, dtype=BF16):
    return jax.ShapeDtypeStruct(dims, dtype)


def part_shapes(left_rows, right_rows, features):
    left, right = shape_of(2, 4, left_rows, features), shape_of(2, 4, right_rows, features)
    return left, left, right, right


def like(array):
    return jax.ShapeDtypeStruct(array.shape, array.dtype)


def update_call(kernel, arrays, moments, weights, name):
    shapes = [like(each) for each in (*moments, *weights)] + [shape_of(2, LANES, dtype=F32)]
    return local_call(kernel, (), arrays, shapes, [], 0, name, 20)


def apply_call(squares, weights, averages, updates):
    shapes = [like(each) for each in (*weights, *averages)]
    shapes += [shape_of(1, LANES, dtype=F32), shape_of(2, LANES, dtype=F32)]
    return local_call(
        apply_kernel, (), (squares, *weights, *averages, *updates), shapes, [], 0, "apply", 60
    )


class Direct:
    def __init__(self, dp, mp):
        self.count = dp * mp
        self.mp = mp
        self.depth = dp // 2
        index = lax.axis_index("dp")
        block = jnp.arange(GROUPS, dtype=jnp.int32)
        along_x = (block % 2) ^ (index % 2)
        along_z = (index // 2 - block // 2) % self.depth
        self.place = jnp.concatenate([along_x, along_z]).astype(jnp.int32)

    def hop(self, values, flip):
        return lax.ppermute(values, AXES, [(i, i ^ flip) for i in range(self.count)])

    def hop_core(self, values):
        return self.hop(values, 1)

    def hop_y(self, values):
        return self.hop(values, 2)

    def hop_x(self, values):
        return self.hop(values, self.mp)

    def hop_z(self, values, distance):
        step = 2 * self.mp * distance
        return lax.ppermute(values, AXES, [(i, (i + step) % self.count) for i in range(self.count)])

    def spread_z(self, piece):
        return jnp.stack([piece] + [self.hop_z(piece, step) for step in range(1, self.depth)])


    def spread_first(self, held, split):
        return self.hop_y(held[:, :split]), self.hop_x(held[:, split:])

    def join_first(self, held, split, others):
        return jnp.stack([held[:, :split], others[0]]), jnp.stack([held[:, split:], others[1]])

    def spread_second(self, parts):
        return self.hop_x(parts[0]), self.hop_y(parts[1])

    def join_second(self, parts, others):
        left = jnp.stack([parts[0], others[0]])
        right = jnp.stack([parts[1], others[1]]).transpose(1, 0, 2, 3, 4)
        whole = jnp.concatenate([left, right], axis=3)
        return whole.reshape(SLOTS, *whole.shape[3:])


    def fold_first(self, grads):
        return self.hop_x(grads[1]), self.hop_y(grads[3])

    def fold_second(self, grads, others):
        return (
            self.hop_y(total([grads[0][1], others[0][1]])),
            self.hop_x(total([grads[2][1], others[1][1]])),
        )

    def kept(self, grads, others, last):
        return [[grads[2 * side][0], others[side][0], last[side]] for side in range(2)]

    def fold_z(self, sides):
        return [
            self.hop_z(total(*[[part[step] for part in parts] for parts in sides]), -step)
            for step in range(1, self.depth)
        ]

    def ring_z(self, sides, step, carried=None):
        addends = [[part[step] for part in parts] for parts in sides]
        own = total(*addends, dtype=F32)
        if carried is not None:
            own = own + carried.astype(F32)
        return self.hop_z(own.astype(BF16), 1)

    def finish(self, sides, others):
        own = total(*[[part[0] for part in parts] for parts in sides], dtype=F32)
        return total([own, *others], dtype=F32)


def total(*sides, dtype=BF16):
    sums = []
    for parts in sides:
        result = parts[0].astype(F32)
        for part in parts[1:]:
            result = result + part.astype(F32)
        sums.append(result.astype(dtype))
    return sums[0] if len(sums) == 1 else jnp.concatenate(sums, axis=0)


class Plain:
    def __init__(self, dp, mp):
        self.dp = dp
        self.mp = mp
        self.side = lax.axis_index("mp") // 2
        block = jnp.arange(GROUPS, dtype=jnp.int32)
        self.place = jnp.concatenate([block % 2, block // 2]).astype(jnp.int32)

    def hop_core(self, values):
        count = self.dp * self.mp
        return lax.ppermute(values, AXES, [(i, i ^ 2) for i in range(count)])

    def collect(self, piece):
        rows, width = piece.shape
        blocks = lax.all_gather(piece, AXES, axis=0).reshape(self.dp, self.mp, rows, width)
        rows = rows * self.dp // GROUPS
        blocks = blocks.transpose(1, 0, 2, 3).reshape(2, 2, 4, 2, rows, width)
        blocks = blocks.transpose(0, 3, 1, 2, 4, 5).reshape(2, SLOTS, rows, width)
        return jnp.where(self.side == 0, blocks, blocks[::-1])

    def joined(self, grads):
        left = jnp.stack(grads[:2])
        right = jnp.stack(grads[2:]).transpose(1, 0, 2, 3, 4)
        return jnp.concatenate([left, right], axis=3)

    def scatter(self, own):
        rows, width = own.shape[3:]
        own = own.transpose(1, 2, 0, 3, 4).reshape(1, 2, GROUPS, rows, width)
        both = jnp.zeros((2, *own.shape[1:]), F32)
        both = lax.dynamic_update_slice_in_dim(both, own.astype(F32), self.side, 0)
        both = both.reshape(self.mp, self.dp, rows * GROUPS // self.dp, width)
        both = both.transpose(1, 0, 2, 3).reshape(-1, width)
        return lax.psum_scatter(both, AXES, scatter_dimension=0, tiled=True)


def tie(*arrays):
    return lax.optimization_barrier(arrays)


def padded(feats):
    pad = ((0, 0), (0, SLOT - PATCHES), (0, 0))
    return jnp.pad(feats, pad).reshape(-1, feats.shape[2])


def tie(*arrays):
    return lax.optimization_barrier(arrays)


def add(left_side, right_side):
    return (left_side.astype(F32) + right_side.astype(F32)).astype(BF16)


def self_forward(place, lengths, hidden, begin):
    rows, features = hidden.shape
    return local_call(
        self_forward_kernel,
        (place, lengths),
        (hidden, *begin),
        (
            shape_of(rows, features, dtype=F32),
            shape_of(rows, 3 * features),
            shape_of(rows, features),
            shape_of(features, 3 * features),
            shape_of(features, features),
            shape_of(features, features),
            shape_of(features, features),
            shape_of(NORM_ROWS, features, dtype=F32),
        ),
        [pltpu.VMEM((features, features), F32), pltpu.VMEM((features, features), F32)],
        10 * rows * features * features,
        "self_forward",
        28,
    )


def fixed(shape):
    return pl.BlockSpec(shape, lambda *_: (0,) * len(shape))


def look(place, feats, image, first_in, norm, w_cross, w_cross_out):
    items, patches, encoded = feats.shape
    items = items // 2
    rows, features = items * SLOT, first_in.shape[1]
    count = items * QUERIES
    arrays = (*image, first_in, norm, w_cross, w_cross_out)
    return pl.pallas_call(
        look_kernel,
        out_shape=(
            shape_of(rows, 2 * features),
            shape_of(count, features, dtype=F32),
            shape_of(count, features),
            shape_of(count, features),
        ),
        grid_spec=pltpu.PrefetchScalarGridSpec(
            num_scalar_prefetch=1,
            grid=(items,),
            in_specs=[
                pl.BlockSpec(
                    (1, patches, encoded), lambda item, where: (where[2 * GROUPS] + item, 0, 0)
                )
            ]
            + [fixed(each.shape) for each in arrays],
            out_specs=(
                pl.BlockSpec((SLOT, 2 * features), lambda item, where: (item, 0)),
                fixed((count, features)),
                fixed((count, features)),
                fixed((count, features)),
            ),
            scratch_shapes=[
                pltpu.VMEM((encoded, 2 * features), BF16),
            ],
        ),
        compiler_params=pltpu.CompilerParams(vmem_limit_bytes=46 * MIB),
        cost_estimate=pl.CostEstimate(
            flops=5 * rows * encoded * features,
            bytes_accessed=2 * rows * (encoded + 2 * features) + 4 * encoded * features,
            transcendentals=0,
        ),
        name="look",
    )(place, feats, *arrays)


def feed(place, lengths, first_in, second_in, norm, out_grad, weights):
    rows, features = first_in.shape
    width = weights[0].shape[3]
    anywhere = pl.BlockSpec(memory_space=pl.ANY)
    return pl.pallas_call(
        feed_kernel,
        out_shape=(
            shape_of(rows, features),
            shape_of(rows, features, dtype=F32),
            shape_of(rows, 4 * width),
            shape_of(rows, 4 * width + 2 * features),
            shape_of(NORM_ROWS, features, dtype=F32),
        ),
        in_specs=[SCALARS, SCALARS, WHOLE] + [anywhere] * (3 + len(weights)),
        out_specs=(anywhere, anywhere, anywhere, anywhere, WHOLE),
        scratch_shapes=[
            pltpu.VMEM(first_in.shape, F32),
            pltpu.VMEM(second_in.shape, F32),
            pltpu.VMEM((rows, features), BF16),
            pltpu.VMEM((MODEL, features, width), BF16),
            pltpu.VMEM((MODEL, width, features), BF16),
            pltpu.VMEM((rows, features), F32),
            pltpu.VMEM((rows, MODEL * width), F32),
            pltpu.VMEM((rows, features), BF16),
            pltpu.VMEM((rows, 4 * width), BF16),
            pltpu.VMEM((rows, 4 * width + 2 * features), BF16),
            pltpu.SemaphoreType.DMA((3,)),
            pltpu.SemaphoreType.DMA((MODEL,)),
            pltpu.SemaphoreType.DMA((MODEL,)),
            pltpu.SemaphoreType.DMA((4,)),
            pltpu.SemaphoreType.DMA((6,)),
            pltpu.SemaphoreType.DMA((2,)),
        ],
        compiler_params=pltpu.CompilerParams(vmem_limit_bytes=58 * MIB),
        cost_estimate=pl.CostEstimate(
            flops=8 * rows * features * MODEL * width,
            bytes_accessed=4 * MODEL * width * features,
            transcendentals=0,
        ),
        name="feed",
    )(place, lengths, norm, first_in, second_in, out_grad, *weights)


def feed_grad(place, keep, send, other, rows):
    features = (send.shape[1] - keep.shape[1]) // 2
    width = keep.shape[1] // 4
    tokens = keep.shape[0]
    shapes = part_shapes(rows, rows, features)
    hidden_spec = pl.BlockSpec(
        (tokens, width), lambda kind, y_step, where: (0, 2 * (1 - kind) + y_step)
    )
    row_spec = pl.BlockSpec(
        (tokens, features), lambda kind, y_step, where: (0, 4 * width // features + kind)
    )
    return pl.pallas_call(
        feed_grad_kernel,
        out_shape=shapes,
        grid_spec=pltpu.PrefetchScalarGridSpec(
            num_scalar_prefetch=1,
            grid=(2, 2),
            in_specs=[hidden_spec, row_spec, hidden_spec, row_spec],
            out_specs=[fixed(shape.shape) for shape in shapes],
        ),
        compiler_params=pltpu.CompilerParams(vmem_limit_bytes=36 * MIB),
        cost_estimate=pl.CostEstimate(
            flops=4 * tokens * features * keep.shape[1],
            bytes_accessed=24 * tokens * features,
            transcendentals=0,
        ),
        name="feed_grad",
    )(place, keep, send, other, other)


def cross_backward(
    two_grad,
    first_in,
    second_in,
    norm,
    w_cross,
    w_cross_out,
    queries,
    heads,
    key_values,
    norm_grads,
):
    features = first_in.shape[1]
    count = queries.shape[0]
    items = key_values.shape[0] // SLOT
    rows = (items + 3) * SLOT
    arrays = (
        two_grad,
        first_in,
        second_in,
        norm,
        w_cross,
        w_cross_out,
        queries,
        heads,
        key_values,
        norm_grads,
    )
    specs = [fixed(each.shape) for each in arrays]
    specs[8] = pl.BlockSpec(
        (SLOT, 2 * features), lambda item: (jnp.minimum(item, items - 1), 0)
    )
    row_spec = pl.BlockSpec((SLOT, features), lambda item: (item, 0))
    return pl.pallas_call(
        cross_backward_kernel,
        grid=(items + 3,),
        out_shape=(
            shape_of(rows, features),
            shape_of(rows, features),
            shape_of(count, features, dtype=F32),
            shape_of(NORM_ROWS, features, dtype=F32),
        ),
        in_specs=specs,
        out_specs=(row_spec, row_spec, fixed((count, features)), fixed((NORM_ROWS, features))),
        scratch_shapes=[pltpu.VMEM((count, features), BF16)] * 3,
        compiler_params=pltpu.CompilerParams(vmem_limit_bytes=36 * MIB),
        cost_estimate=pl.CostEstimate(
            flops=20 * count * features * features,
            bytes_accessed=12 * rows * features,
            transcendentals=0,
        ),
        name="cross_backward",
    )(*arrays)


def image_grad(place, feats, keep, other):
    features = keep.shape[1]
    items, patches, encoded = feats.shape
    rows = items * SLOT
    piece = encoded // GROUPS // 2 + 2 * (features // MODEL // GROUPS)
    steps = 4
    block = rows // steps
    last = steps // 2 - 1
    shapes = part_shapes(IMAGE_SPLIT, piece - IMAGE_SPLIT, features)
    out_specs = [pl.BlockSpec(shape.shape, lambda step, where: (0, 0, 0, 0)) for shape in shapes]
    rest = pl.BlockSpec((4 * SLOT, features), lambda step, where: (items // 8, 0))
    return pl.pallas_call(
        functools.partial(image_grad_kernel, items // 2 * QUERIES),
        out_shape=shapes,
        grid_spec=pltpu.PrefetchScalarGridSpec(
            num_scalar_prefetch=1,
            grid=(steps,),
            in_specs=[
                pl.BlockSpec(
                    (items // steps, patches, encoded),
                    lambda step, where: (
                        (step + where[2 * GROUPS] // (items // steps)) % steps,
                        0,
                        0,
                    ),
                ),
                pl.BlockSpec((block, features), lambda step, where: (jnp.minimum(step, last), 0)),
                pl.BlockSpec(
                    (block, features), lambda step, where: (jnp.maximum(step - last - 1, 0), 0)
                ),
                rest,
                rest,
            ],
            out_specs=out_specs,
            scratch_shapes=[pltpu.VMEM((encoded, features), F32), pltpu.VMEM((block, encoded), BF16)],
        ),
        compiler_params=pltpu.CompilerParams(vmem_limit_bytes=34 * MIB),
        cost_estimate=pl.CostEstimate(
            flops=2 * rows * encoded * features,
            bytes_accessed=2 * rows * (encoded + features),
            transcendentals=0,
        ),
        name="image_grad",
    )(place, feats, keep, other, keep, other)


def self_backward(
    lengths,
    one_query_grad,
    two_grad,
    first_in,
    norm,
    hidden,
    qkv,
    heads,
    w_qkv,
    w_self_out,
    norm_grads,
):
    rows, features = hidden.shape
    return local_call(
        self_backward_kernel,
        (lengths,),
        (
            one_query_grad,
            two_grad,
            first_in,
            norm,
            hidden,
            qkv,
            heads,
            w_qkv,
            w_self_out,
            norm_grads,
        ),
        (
            shape_of(rows, features),
            shape_of(rows, 2 * features),
            shape_of(rows + 16, 4 * features),
            shape_of(NORM_ROWS, features, dtype=F32),
        ),
        [
            pltpu.VMEM((rows, features), F32),
            pltpu.VMEM((rows, features), BF16),
            pltpu.VMEM((rows, 3 * features), BF16),
        ],
        16 * rows * features * features,
        "self_backward",
        30,
    )


def self_grad(place, keep, send, other, norm_total):
    features = norm_total.shape[1]
    rows = features // GROUPS + NORM_ROWS
    return local_call(
        self_grad_kernel,
        (place,),
        (keep, send, other, norm_total),
        part_shapes(SELF_SPLIT, rows - SELF_SPLIT, features),
        [],
        8 * keep.shape[0] * features * features,
        "self_grad",
        24,
    )


def run_direct(hidden, feats, first_item, lengths, out_grad, image, begin, weights):
    moves = Direct(lax.axis_size("dp"), lax.axis_size("mp"))
    place = moves.place
    feats_place = jnp.concatenate([place, first_item[None].astype(jnp.int32)])
    begin_split = begin.shape[0] // 2
    image_split = image.shape[0] * 96 // 176
    feed_split = weights.shape[0] // 2

    begin = moves.spread_z(begin)
    begin, image, feats = tie(begin, image, feats)
    begin_others = moves.spread_first(begin, begin_split)
    image = moves.spread_z(image)
    begin_others, image, weights, feats = tie(begin_others, image, weights, feats)
    begin_parts = moves.join_first(begin, begin_split, begin_others)
    begin_others = moves.spread_second(begin_parts)
    image_others = moves.spread_first(image, image_split)
    weights = moves.spread_z(weights)
    begin_others, image_others, weights = tie(begin_others, image_others, weights)

    image_parts = moves.join_first(image, image_split, image_others)
    image_others = moves.spread_second(image_parts)
    weight_others = moves.spread_first(weights, feed_split)
    begin = moves.join_second(begin_parts, begin_others)
    begin_other = moves.hop_core(begin)
    first_in, qkv, heads, w_qkv, w_cross, w_self_out, w_cross_out, norm = self_forward(
        place, lengths, hidden, (begin, begin_other)
    )
    first_in, image_others, weight_others = tie(first_in, image_others, weight_others)
    image = moves.join_second(image_parts, image_others)
    weight_parts = moves.join_first(weights, feed_split, weight_others)
    image_other = moves.hop_core(image)
    weight_others = moves.spread_second(weight_parts)
    held_others = [moves.hop_core(part) for part in weight_parts]
    key_values, second_in, cross_queries, cross_heads = look(
        feats_place, feats, (image, image_other), first_in, norm, w_cross, w_cross_out
    )
    second_in, weight_others, held_others = tie(second_in, weight_others, held_others)
    last_others = [moves.hop_core(part) for part in weight_others]
    gathered = (*weight_parts, *weight_others, *held_others, *last_others)
    block_out, two_grad, feed_keep, feed_send, norm_grads = feed(
        place, lengths, first_in, second_in, norm, out_grad, gathered
    )

    feed_other = moves.hop_core(feed_send)
    cross_keep, cross_send, one_query_grad, norm_grads = cross_backward(
        two_grad,
        first_in,
        second_in,
        norm,
        w_cross,
        w_cross_out,
        cross_queries,
        cross_heads,
        key_values,
        norm_grads,
    )
    cross_send, feed_other = tie(cross_send, feed_other)
    cross_other = moves.hop_core(cross_send)
    feed_grads = feed_grad(place, feed_keep, feed_send, feed_other, feed_split)
    cross_other, feed_grads = tie(cross_other, feed_grads)
    feed_first = moves.fold_first(feed_grads)
    image_grads = image_grad(feats_place, feats, cross_keep, cross_other)
    one_query_grad, image_grads, feed_first = tie(one_query_grad, image_grads, feed_first)
    image_first = moves.fold_first(image_grads)
    input_grad, self_keep, self_send, norm_total = self_backward(
        lengths,
        one_query_grad,
        two_grad,
        first_in,
        norm,
        hidden,
        qkv,
        heads,
        w_qkv,
        w_self_out,
        norm_grads,
    )
    self_send, image_first, feed_first = tie(self_send, image_first, feed_first)
    self_other = moves.hop_core(self_send)
    feed_second = moves.fold_second(feed_grads, feed_first)
    self_other, feed_first, image_first = tie(self_other, feed_first, image_first)
    image_second = moves.fold_second(image_grads, image_first)
    self_grads = self_grad(place, self_keep, self_send, self_other, norm_total)
    self_first = moves.fold_first(self_grads)
    feed_kept = moves.kept(feed_grads, feed_first, feed_second)
    feed_other = moves.ring_z(feed_kept, 1)
    image_second, feed_other = tie(image_second, feed_other)
    image_kept = moves.kept(image_grads, image_first, image_second)
    feed_other = moves.ring_z(feed_kept, 2, feed_other)
    image_other = moves.ring_z(image_kept, 1)
    self_first, image_other, feed_other = tie(self_first, image_other, feed_other)
    self_second = moves.fold_second(self_grads, self_first)
    feed_other = moves.ring_z(feed_kept, 3, feed_other)
    image_other = moves.ring_z(image_kept, 2, image_other)
    self_second, image_other, feed_other = tie(self_second, image_other, feed_other)
    feed_sum = moves.finish(feed_kept, [feed_other])
    image_other = moves.ring_z(image_kept, 3, image_other)
    self_kept = moves.kept(self_grads, self_first, self_second)
    self_others = moves.fold_z(self_kept)
    image_sum = moves.finish(image_kept, [image_other])
    in_sum = moves.finish(self_kept, self_others)
    return block_out, input_grad, in_sum, image_sum, feed_sum


def run_plain(hidden, feats, first_item, lengths, out_grad, image, begin, weights):
    moves = Plain(lax.axis_size("dp"), lax.axis_size("mp"))
    place = moves.place
    feats_place = jnp.concatenate([place, first_item[None].astype(jnp.int32)])
    features = hidden.shape[1]
    width = features // MODEL
    block_rows, out_rows = features // GROUPS, width // GROUPS
    own_in, own_out = block_rows * GROUPS // moves.dp, out_rows * GROUPS // moves.dp
    half = block_rows // 2
    part = begin.shape[0] - NORM_ROWS
    inward = moves.collect(begin[:own_in])
    cross_out = moves.collect(begin[own_in : own_in + own_out])
    self_out = moves.collect(begin[own_in + own_out : part])
    norm_all = lax.psum(begin[part:].astype(F32), AXES).astype(BF16)
    norm_first = jnp.zeros((2, SLOTS, NORM_ROWS, features), BF16).at[0, 0].set(norm_all)
    begin = jnp.concatenate(
        [
            inward[:, :, :half],
            cross_out,
            jnp.zeros_like(norm_first),
            inward[:, :, half:],
            self_out,
            norm_first,
        ],
        axis=2,
    )
    image = moves.collect(image)
    own_up = weights.shape[0] // 2
    ups, downs = [
        moves.collect(part).reshape(2, 2, 2, 4, -1, features)
        for part in (weights[:own_up], weights[own_up:])
    ]
    gathered = tuple(
        part
        for side in range(2)
        for last in range(2)
        for part in (ups[side, last], downs[side, :, last])
    )
    first_in, qkv, heads, w_qkv, w_cross, w_self_out, w_cross_out, norm = self_forward(
        place, lengths, hidden, (begin[0], begin[1])
    )
    key_values, second_in, cross_queries, cross_heads = look(
        feats_place, feats, (image[0], image[1]), first_in, norm, w_cross, w_cross_out
    )
    block_out, two_grad, feed_keep, feed_send, norm_grads = feed(
        place, lengths, first_in, second_in, norm, out_grad, gathered
    )
    feed_half = gathered[0].shape[2]
    feed_grads = feed_grad(place, feed_keep, feed_send, moves.hop_core(feed_send), feed_half)
    cross_keep, cross_send, one_query_grad, norm_grads = cross_backward(
        two_grad,
        first_in,
        second_in,
        norm,
        w_cross,
        w_cross_out,
        cross_queries,
        cross_heads,
        key_values,
        norm_grads,
    )
    image_grads = image_grad(feats_place, feats, cross_keep, moves.hop_core(cross_send))
    input_grad, self_keep, self_send, norm_total = self_backward(
        lengths,
        one_query_grad,
        two_grad,
        first_in,
        norm,
        hidden,
        qkv,
        heads,
        w_qkv,
        w_self_out,
        norm_grads,
    )
    self_grads = self_grad(place, self_keep, self_send, moves.hop_core(self_send), norm_total)

    def beside(values):
        count = values.shape[-2] // MODEL
        return jnp.concatenate(
            [values[..., part * count : (part + 1) * count, :] for part in range(MODEL)], axis=-1
        )

    def below(values):
        count = values.shape[-1] // MODEL
        return jnp.concatenate(
            [values[..., part * count : (part + 1) * count] for part in range(MODEL)], axis=-2
        )

    grads = moves.joined(self_grads)
    in_part = moves.scatter(grads[..., :block_rows, : 3 * width])
    self_out = moves.scatter(beside(grads[..., :block_rows, 3 * width :]))
    norm_sum = lax.psum(norm_total, AXES)
    in_sum = jnp.concatenate([jnp.concatenate([in_part, below(self_out)], axis=1), norm_sum])
    grads = moves.joined(image_grads)
    image_rows = grads.shape[3] - 2 * out_rows
    image_part = grads[..., :image_rows, :]
    image_part = jnp.concatenate(
        [image_part[..., : features // 2], image_part[..., features // 2 :]], axis=3
    )
    image_part = moves.scatter(image_part)
    image_half = image_part.shape[0] // 2
    image_part = jnp.concatenate([image_part[:image_half], image_part[image_half:]], axis=1)
    cross_query = moves.scatter(below(grads[..., image_rows : image_rows + out_rows, :]))
    cross_out = moves.scatter(grads[..., image_rows + out_rows :, :])
    image_sum = jnp.concatenate([image_part, beside(cross_query), cross_out])
    grads = moves.joined(feed_grads)
    feed_sum = jnp.concatenate(
        [moves.scatter(jnp.stack(feed_grads[:2])), moves.scatter(grads[..., feed_half:, :])]
    )
    return block_out, input_grad, in_sum, image_sum, feed_sum


def per_device(
    hidden_in,
    image_feats,
    caption_lengths,
    out_grad,
    proj_in,
    proj_in_moments,
    proj_in_average,
    proj_out,
    proj_out_moments,
    proj_out_average,
    image_kv,
    image_kv_moments,
    image_kv_average,
    feed_up,
    feed_up_moments,
    feed_up_average,
    feed_down,
    feed_down_moments,
    feed_down_average,
    norm_params,
    norm_params_moments,
    norm_params_average,
):
    data_ways, model_ways = lax.axis_size("dp"), lax.axis_size("mp")
    data_index, model_index = lax.axis_index("dp"), lax.axis_index("mp")
    rows, features = hidden_in.shape
    items = rows // SEQ
    width = features // model_ways
    own_norm = norm_params.shape[1]
    norm_begin = (model_index * data_ways + data_index) * own_norm
    lengths = lax.dynamic_slice_in_dim(caption_lengths, model_index * items, items, 0)
    direct = data_ways == GROUPS and model_ways == MODEL
    if direct:
        feats = lax.dynamic_slice_in_dim(image_feats, model_index // 2 * 2 * items, 2 * items, 0)
        first_item = model_index % 2 * items
    else:
        feats = jnp.concatenate(
            [
                lax.dynamic_slice_in_dim(image_feats, (model_index % 2 + 2 * side) * items, items, 0)
                for side in range(2)
            ]
        )
        first_item = model_index // 2 * items
    image_piece = jnp.concatenate([image_kv[0], image_kv[1]], axis=1).astype(BF16)
    in_piece = jnp.concatenate([proj_in[kind] for kind in range(4)], axis=1).astype(BF16)
    out_pieces = [proj_out[kind].astype(BF16) for kind in range(2)]
    feed_piece = jnp.concatenate([feed_up, feed_down], axis=0).astype(BF16)
    norm_rows = lax.dynamic_update_slice(
        jnp.zeros((NORM_ROWS, features), F32), norm_params, (0, norm_begin)
    ).astype(BF16)
    own_in, own_out, own_image = proj_in.shape[1], proj_out.shape[1], image_kv.shape[1]
    if direct:
        run, half = run_direct, own_in // 2
        begin_piece = jnp.concatenate(
            [
                in_piece[:half],
                out_pieces[1],
                jnp.zeros_like(norm_rows),
                in_piece[half:],
                out_pieces[0],
                norm_rows,
            ],
            axis=0,
        )
    else:
        run = run_plain
        begin_piece = jnp.concatenate(
            [in_piece, out_pieces[1], out_pieces[0], norm_rows], axis=0
        )
    block_out, input_grad, in_sum, image_sum, feed_sum = run(
        hidden_in, feats, first_item, lengths, out_grad, image_piece, begin_piece, feed_piece
    )
    norm_shard = lax.dynamic_slice(in_sum[own_in:], (0, norm_begin), norm_params.shape)
    up_next, down_next, up_update, down_update, feed_squares = update_call(
        feed_update_kernel,
        (feed_sum, feed_up, feed_up_moments, feed_down, feed_down_moments),
        (feed_up_moments, feed_down_moments),
        (feed_up, feed_down),
        "feed_update",
    )
    image_next, image_update, image_squares = update_call(
        image_update_kernel,
        (image_sum, image_kv, image_kv_moments),
        (image_kv_moments,),
        (image_kv,),
        "image_update",
    )
    in_next, out_next, norm_next, in_update, out_update, norm_update, last_squares = update_call(
        last_update_kernel,
        (
            in_sum,
            image_sum,
            norm_shard,
            proj_in,
            proj_in_moments,
            proj_out,
            proj_out_moments,
            norm_params,
            norm_params_moments,
        ),
        (proj_in_moments, proj_out_moments, norm_params_moments),
        (proj_in, proj_out, norm_params),
        "last_update",
    )
    own_squares = feed_squares + image_squares + last_squares
    ways = data_ways * model_ways
    copies = jnp.broadcast_to(own_squares[None], (ways,) + own_squares.shape)
    squares = lax.all_to_all(copies, AXES, 0, 0, tiled=True)
    results = apply_call(
        squares,
        (proj_in, proj_out, image_kv, feed_up, feed_down, norm_params),
        (
            proj_in_average,
            proj_out_average,
            image_kv_average,
            feed_up_average,
            feed_down_average,
            norm_params_average,
        ),
        (in_update, out_update, image_update, up_update, down_update, norm_update),
    )
    new_weights, new_averages, (trust, norms) = results[:6], results[6:12], results[12:]
    moments = (in_next, out_next, image_next, up_next, down_next, norm_next)
    outputs = [
        each for group in zip(new_weights, moments, new_averages) for each in group
    ]
    tensors = sum(each.shape[0] for each in (proj_in, proj_out, image_kv, norm_params)) + 2
    return (block_out, input_grad, *outputs, trust[0, :tensors], norms[:, :tensors])


def solution(mesh):
    rows = P(AXES, None)
    by_column = P(None, "dp", "mp")
    by_row = P(None, ("mp", "dp"), None)
    weights = (
        by_column,
        P(None, None, "dp", "mp"),
        by_column,
        by_row,
        P(None, None, ("mp", "dp"), None),
        by_row,
        by_column,
        P(None, None, "dp", "mp"),
        by_column,
        P("dp", "mp"),
        P(None, "dp", "mp"),
        P("dp", "mp"),
        P(("mp", "dp"), None),
        P(None, ("mp", "dp"), None),
        P(("mp", "dp"), None),
        P(None, ("mp", "dp")),
        P(None, None, ("mp", "dp")),
        P(None, ("mp", "dp")),
    )
    return jax.shard_map(
        per_device,
        mesh=mesh,
        in_specs=(rows, P("dp", None, None), P("dp"), rows, *weights),
        out_specs=(rows, rows, *weights, P(), P()),
        check_vma=False,
    )
```
